128 devices in a mesh: ctx: 64 (over x, z, y_hi, core), ep: 2 (over y_lo).
Axes of the slice: x: 4, y: 4 (y_hi: 2, y_lo: 2; y = y_hi * 2 + y_lo), z: 4, core: 2. Of those that a mesh axis runs over, the one named last changes fastest.
Arguments:
- inputs: bfloat16 [8192, 2048], P('ctx'), may hold values from -6 to 6
- blocks: int32 [8192], P('ctx'), may hold values from 0 to 63, never falling along the last dimension, each value on 1 to 256 neighbouring positions
- expert_ids: int32 [8192, 8], P('ctx'), may hold values from 0 to 63, all different within a row; in each aligned block of 128 rows (0 to 127, 128 to 255, ...) at most 20 rows name the same one
- attention_gain: bfloat16 [2048], P('ctx'), may hold values from 0.5 to 1.5
- query_weight: bfloat16 [2048, 2048], P('ctx', 'ep'), may hold values from -0.125 to 0.125
- key_weight: bfloat16 [2048, 2048], P('ctx', 'ep'), may hold values from -0.125 to 0.125
- value_weight: bfloat16 [2048, 2048], P('ctx', 'ep'), may hold values from -0.125 to 0.125
- query_gain: bfloat16 [2048], P(('ep', 'ctx')), may hold values from 0.5 to 1.5
- key_gain: bfloat16 [2048], P(('ep', 'ctx')), may hold values from 0.5 to 1.5
- output_weight: bfloat16 [2048, 2048], P('ep', 'ctx'), may hold values from -0.5 to 0.5
- mixture_gain: bfloat16 [2048], P('ctx'), may hold values from 0.5 to 1.5
- router_weight: bfloat16 [2048, 64], P('ctx'), may hold values from -0.0625 to 0.0625
- gate_weight: bfloat16 [64, 2048, 1024], P('ctx', None, 'ep'), may hold values from -0.125 to 0.125
- up_weight: bfloat16 [64, 2048, 1024], P('ctx', None, 'ep'), may hold values from -0.125 to 0.125
- down_weight: bfloat16 [64, 1024, 2048], P('ctx', 'ep'), may hold values from -6 to 6
- cotangent: bfloat16 [8192, 2048], P('ctx'), may hold values from -6 to 6
Outputs:
- output: float32 [8192, 2048], P('ctx')
- input_grad: float32 [8192, 2048], P('ctx')
- attention_gain_grad: float32 [2048], P('ctx')
- query_weight_grad: float32 [2048, 2048], P('ctx', 'ep')
- key_weight_grad: float32 [2048, 2048], P('ctx', 'ep')
- value_weight_grad: float32 [2048, 2048], P('ctx', 'ep')
- query_gain_grad: float32 [2048], P(('ep', 'ctx'))
- key_gain_grad: float32 [2048], P(('ep', 'ctx'))
- output_weight_grad: float32 [2048, 2048], P('ep', 'ctx')
- mixture_gain_grad: float32 [2048], P('ctx')
- router_weight_grad: float32 [2048, 64], P('ctx')
- gate_weight_grad: float32 [64, 2048, 1024], P('ctx', None, 'ep')
- up_weight_grad: float32 [64, 2048, 1024], P('ctx', None, 'ep')
- down_weight_grad: float32 [64, 1024, 2048], P('ctx', 'ep')
The draws below stay inside these ranges and needn't reach their ends.
Inputs may be any that keep to these rules, and one draw needn't show every extreme that they name: `expert_ids`: each row names 8 different experts, and every expert is named somewhere; among the 128 tokens of one index of ctx no expert is named by more than 20 rows, a bound that some expert reaches in some index. `blocks`: block numbers never fall along the sequence; each block holds 1 to 256 tokens and some block holds exactly 256.
All inputs are finite; a program needn't handle non-finite values.
Results may differ from the reference program's by a relative error of at most 0.04.
Values may be sent and summed in bfloat16 or wider, within the bound.
No kernel may reach another device: no remote copies, remote signals or barrier semaphores. Data moves between devices by JAX's collectives and lax.ppermute only.
A program may use at most 256 MiB of HBM per device.

```python
import math
import jax
import jax.numpy as jnp
import numpy as np
from jax import lax

D = 2048
H = 16
HD = 128
FF = 1024
TOPK = 8
BLOCK = 256
TOK_CTX = 128
TOKENS = 8192
E = 64
CAP = 20
N_CTX = 64
N_EP = 2


def shard_levels(own_key, extent, shards, low, high):
    loudness = 1.0
    for position, shards_of in shards:
        steps = jax.random.uniform(jax.random.fold_in(jax.random.fold_in(own_key, 6), position), (shards_of,), jnp.float32, low / len(shards), high / len(shards))
        loudness = loudness * jnp.repeat(jnp.exp(steps), extent[position] // shards_of).reshape((-1,) + (1,) * (len(extent) - 1 - position))
    return loudness


def split_up(amount, total, limit, slope):
    weights = [(1 << 20) // math.isqrt(standing ** slope) + 1 for standing in range(2, amount + 1)]
    surplus, holding = total - limit - (amount - 1), [1] * (amount - 1)
    while surplus > 0:
        free = [i for i in range(amount - 1) if holding[i] < limit]
        whole, budget = sum([weights[i] for i in free]), surplus
        for i in free:
            extra = min(limit - holding[i], max(1, budget * weights[i] // whole), surplus)
            holding[i] = holding[i] + extra
            surplus = surplus - extra
    return np.array([limit] + holding)


def uneven(own_key, count, total, limit, slope):
    if count == 2:
        one = jax.random.randint(own_key, (), max(1, total - limit), min(limit, total - 1) + 1)
        return jnp.stack([one, total - one])
    tallies = jnp.asarray(split_up(count, total, limit, slope), jnp.int32)
    pairs = (count - 1) // 2
    source_of, sink = tallies[1:1 + 2 * pairs:2], tallies[2:2 + 2 * pairs:2]
    room = jnp.minimum(source_of - 1, limit - sink)
    passed = jax.random.randint(jax.random.fold_in(own_key, 1), (pairs,), 0, 1 << 20) % (room + 1)
    tallies = tallies.at[1:1 + 2 * pairs:2].set(source_of - passed).at[2:2 + 2 * pairs:2].set(sink + passed)
    return tallies[jax.random.permutation(jax.random.fold_in(own_key, 2), count)]


def assign_block(key, own, number, rows, count, top, limit, skew):
    ranking = jax.random.permutation(key, count)
    crowded, usual = portions_of(count, rows * top, limit, skew, True), portions_of(count, rows * top, limit, skew, False)
    places = jnp.arange(count)

    def named(sizes, rotation):
        used = int((sizes > 0).sum())
        fixed = max(1, used // 4)
        moved = fixed + (places - fixed + rotation * (used - fixed)) % max(1, count - fixed)
        return jnp.zeros((count,), jnp.int32).at[ranking[jnp.where(places < fixed, places, moved)]].set(jnp.asarray(sizes, jnp.int32))

    sizes = jnp.where(number % 4 == 0, named(crowded, number // 4), named(usual, number - number // 4 - 1))
    mixed = jax.random.permutation(jax.random.fold_in(own, 3), count)
    source_of, receiver = mixed[0:count // 2 * 2:2], mixed[1:count // 2 * 2:2]
    room = jnp.minimum(sizes[source_of] - 1, limit - sizes[receiver]) // 2
    room = jnp.where((source_of == ranking[0]) | (receiver == ranking[0]) | (sizes[receiver] == 0), 0, jnp.maximum(room, 0))
    moved = jax.random.randint(jax.random.fold_in(own, 4), (count // 2,), 0, 1 << 20) % (room + 1)
    sizes = sizes.at[source_of].add(-moved).at[receiver].add(moved)
    members = jnp.searchsorted(jnp.cumsum(sizes), jnp.arange(rows * top), side="right").astype(jnp.int32)
    grid = members.reshape(top, rows).T
    grid = grid[jax.random.permutation(jax.random.fold_in(own, 1), rows)]
    rotation = jax.random.randint(jax.random.fold_in(own, 2), (rows, 1), 0, top)
    return jnp.take_along_axis(grid, (jnp.arange(top)[None, :] + rotation) % top, axis=1)


def portions_of(amount, total, most, lean, full):
    loads = [(1 << 20) // math.isqrt(standing ** lean) + 1 for standing in range(1, amount + 1)]
    largest = most if full else min(most, max(-(-total // amount), total * loads[0] // sum(loads)))
    least = 1 if total - largest >= amount - 1 else 0
    holding, spare = [largest] + [least] * (amount - 1), total - largest - least * (amount - 1)
    while spare > 0:
        movable = [i for i in range(1, amount) if holding[i] < largest] or [i for i in range(1, amount) if holding[i] < most]
        mass, remaining = sum([loads[i] for i in movable]), spare
        for i in movable:
            extra = min(most - holding[i], max(1, remaining * loads[i] // mass), spare)
            holding[i] = holding[i] + extra
            spare = spare - extra
    return np.array(holding)


def noise(rng, extent, spread, most, split=(), kind=jnp.bfloat16):
    array = jax.random.normal(rng, extent, jnp.float32) * spread
    if len(split) > 0:
        array = shard_levels(rng, extent, split, -0.22, 0.18) * array
    return jnp.clip(array, min=-most, max=most).astype(kind)


def setup_inputs(seed: int = 0) -> dict:
    key_of = jax.random.split(jax.random.key(seed), 17)
    inputs = noise(key_of[0], (TOKENS, D), 1.0, 6.0, ((0, 64),))
    blocks = jnp.searchsorted(jnp.cumsum(uneven(key_of[1], 2 * TOKENS // BLOCK, TOKENS, BLOCK, 1)), jnp.arange(TOKENS), side="right").astype(jnp.int32)
    expert_ids_keys = jax.random.split(jax.random.fold_in(key_of[2], 1), TOKENS // TOK_CTX)
    expert_ids_turns = jax.random.permutation(jax.random.fold_in(key_of[2], 3), TOKENS // TOK_CTX)
    expert_ids = jax.vmap(lambda own, number: assign_block(jax.random.fold_in(key_of[2], 2), own, number, TOK_CTX, E, TOPK, CAP, 1))(expert_ids_keys, expert_ids_turns).reshape((TOKENS, TOPK))
    attention_gain = jnp.clip(1.0 + 0.1 * jax.random.normal(key_of[3], (D,), jnp.float32), 0.5, 1.5).astype(jnp.bfloat16)
    query_weight = noise(key_of[4], (D, H * HD), D ** -0.5, 0.125, ((0, 64), (1, 2)))
    key_weight = noise(key_of[5], (D, H * HD), D ** -0.5, 0.125, ((0, 64), (1, 2)))
    value_weight = noise(key_of[6], (D, H * HD), D ** -0.5, 0.125, ((0, 64), (1, 2)))
    query_gain = jnp.clip(1.0 + 0.1 * jax.random.normal(key_of[7], (H * HD,), jnp.float32), 0.5, 1.5).astype(jnp.bfloat16)
    key_gain = jnp.clip(1.0 + 0.1 * jax.random.normal(key_of[8], (H * HD,), jnp.float32), 0.5, 1.5).astype(jnp.bfloat16)
    output_weight = noise(key_of[9], (H * HD, D), (H * HD // 16) ** -0.5, 0.5, ((0, 2), (1, 64)))
    mixture_gain = jnp.clip(1.0 + 0.1 * jax.random.normal(key_of[10], (D,), jnp.float32), 0.5, 1.5).astype(jnp.bfloat16)
    router_weight = noise(key_of[11], (D, E), (4 * D) ** -0.5, 0.0625, ((0, 64),))
    gate_weight = noise(key_of[12], (E, D, FF), D ** -0.5, 0.125, ((0, 64), (2, 2)))
    up_weight = noise(key_of[13], (E, D, FF), D ** -0.5, 0.125, ((0, 64), (2, 2)))
    down_weight = noise(key_of[14], (E, FF, D), (max(1, FF * 4 // (E * E))) ** -0.5, 6.0, ((0, 64), (1, 2)))
    cotangent = noise(key_of[15], (TOKENS, D), 1.0, 6.0, ((0, 64),))
    return dict(inputs=inputs, blocks=blocks, expert_ids=expert_ids, attention_gain=attention_gain, query_weight=query_weight, key_weight=key_weight, value_weight=value_weight, query_gain=query_gain, key_gain=key_gain, output_weight=output_weight, mixture_gain=mixture_gain, router_weight=router_weight, gate_weight=gate_weight, up_weight=up_weight, down_weight=down_weight, cotangent=cotangent)


epsilon = 1e-05
rotary_base = 10000.0
highest = lax.Precision.HIGHEST

@jax.custom_vjp
def low(v):
    return lax.optimization_barrier(v.astype(jnp.bfloat16)).astype(jnp.float32)

@jax.custom_vjp
def low_back(v):
    return v

def low_keep(v):
    return (low(v), None)

def low_pass(kept, grad):
    return (grad,)

def back_keep(v):
    return (v, None)

def back_low(kept, grad):
    return (low(grad),)
low.defvjp(low_keep, low_pass)
low_back.defvjp(back_keep, back_low)

def rms_norm(value, gain):
    return value * lax.rsqrt(lax.optimization_barrier(jnp.mean(value * value, axis=-1, keepdims=True)) + epsilon) * gain

def rotary(value, positions):
    half = value.shape[-1] // 2
    frequency = rotary_base ** (-jnp.arange(half).astype(jnp.float32) / half)
    angles = positions.astype(jnp.float32)[:, None] * frequency[None, :]
    cosine = jnp.cos(angles)[:, None, :]
    sine = jnp.sin(angles)[:, None, :]
    first = value[..., :half]
    second = value[..., half:]
    return jnp.concatenate([first * cosine - second * sine, second * cosine + first * sine], axis=-1)

def attention(queries, keys, values, blocks):
    count = queries.shape[0]
    group_rows = min(512, count)
    scale = HD ** (-0.5)
    query_groups = queries.reshape(count // group_rows, group_rows, H, HD)
    block_groups = blocks.reshape(count // group_rows, group_rows)

    def one_group(item):
        query_part, query_blocks = item
        scores = low_back(jnp.einsum('qhd,khd->hqk', query_part, keys, precision=highest)) * scale
        visible = blocks[None, None, :] <= query_blocks[None, :, None]
        scores = jnp.where(visible, scores, -1e+30)
        shifted = jnp.exp(scores - lax.optimization_barrier(jnp.max(scores, axis=-1, keepdims=True)))
        weights = low(shifted / lax.optimization_barrier(jnp.sum(shifted, axis=-1, keepdims=True)))
        return jnp.einsum('hqk,khd->qhd', weights, values, precision=highest)
    return lax.map(jax.checkpoint(one_group), (query_groups, block_groups)).reshape(count, H, HD)

def slot_tables(expert_ids):
    tokens = expert_ids.shape[0]
    groups = tokens // TOK_CTX
    flat = expert_ids.reshape(groups, TOK_CTX * TOPK)
    indicator = (flat[:, :, None] == jnp.arange(E, dtype=jnp.int32)[None, None, :]).astype(jnp.int32)
    ranks = lax.optimization_barrier(jnp.sum((jnp.cumsum(indicator, axis=1) - 1) * indicator, axis=2))
    slots = ranks + CAP * jnp.arange(groups, dtype=jnp.int32)[:, None]
    return (flat.reshape(-1).astype(jnp.int32), slots.reshape(-1).astype(jnp.int32))

def experts_apply(mixed, expert_ids, gate_weight, up_weight, down_weight):
    tokens = mixed.shape[0]
    expert_flat, slot_flat = slot_tables(expert_ids)
    row_count = tokens * TOPK
    token_of_row = jnp.arange(row_count, dtype=jnp.int32) // TOPK
    table = jnp.full((E, N_CTX * CAP), tokens, jnp.int32).at[expert_flat, slot_flat].set(token_of_row)
    padded = jnp.concatenate([mixed, jnp.zeros((1, mixed.shape[1]), jnp.float32)], axis=0)
    group_width = FF // N_EP

    def one_expert(item):
        token_rows, gate_matrix, up_matrix, down_matrix = item
        entry = padded[token_rows]
        total = jnp.zeros((token_rows.shape[0], mixed.shape[1]), jnp.float32)
        for group in range(N_EP):
            begin = group * group_width
            finish = begin + group_width
            own = low_back(entry)
            gate = low_back(jnp.dot(own, gate_matrix[:, begin:finish], precision=highest))
            upward = low_back(jnp.dot(own, up_matrix[:, begin:finish], precision=highest))
            hidden = low(jax.nn.silu(gate) * upward)
            total = total + low(low_back(jnp.dot(hidden, down_matrix[begin:finish, :], precision=highest)))
        return total
    parts = lax.map(jax.checkpoint(one_expert), (table, gate_weight, up_weight, down_weight))
    return parts[expert_flat, slot_flat].reshape(tokens, TOPK, mixed.shape[1])

def layer(inputs, attention_gain, query_weight, key_weight, value_weight, query_gain, key_gain, output_weight, mixture_gain, router_weight, gate_weight, up_weight, down_weight, blocks, expert_ids):
    tokens = inputs.shape[0]
    positions = jnp.arange(tokens, dtype=jnp.int32)
    normed = low(rms_norm(inputs, attention_gain))
    query_raw = low_back(jnp.dot(normed, query_weight, precision=highest))
    key_raw = low_back(jnp.dot(normed, key_weight, precision=highest))
    values = low(low_back(jnp.dot(normed, value_weight, precision=highest))).reshape(tokens, H, HD)
    queries = low(rotary(rms_norm(query_raw, query_gain).reshape(tokens, H, HD), positions))
    keys = low(rotary(rms_norm(key_raw, key_gain).reshape(tokens, H, HD), positions))
    attended = low(low_back(attention(queries, keys, values, blocks))).reshape(tokens, H * HD)
    residual = inputs + low_back(jnp.dot(attended, output_weight, precision=highest))
    mixed = low(rms_norm(residual, mixture_gain))
    logits = low_back(jnp.dot(mixed, router_weight, precision=highest))
    shifted = jnp.exp(logits - lax.optimization_barrier(jnp.max(logits, axis=-1, keepdims=True)))
    probability = shifted / lax.optimization_barrier(jnp.sum(shifted, axis=-1, keepdims=True))
    chosen = (expert_ids[:, :, None] == jnp.arange(E, dtype=jnp.int32)[None, None, :]).astype(jnp.float32)
    gates = lax.optimization_barrier(jnp.sum(chosen * probability[:, None, :], axis=-1))
    parts = experts_apply(mixed, expert_ids, gate_weight, up_weight, down_weight)
    return residual + lax.optimization_barrier(jnp.sum(gates[:, :, None] * parts, axis=1))

def reference(inputs, blocks, expert_ids, attention_gain, query_weight, key_weight, value_weight, query_gain, key_gain, output_weight, mixture_gain, router_weight, gate_weight, up_weight, down_weight, cotangent):
    floats = tuple((item.astype(jnp.float32) for item in (inputs, attention_gain, query_weight, key_weight, value_weight, query_gain, key_gain, output_weight, mixture_gain, router_weight, gate_weight, up_weight, down_weight)))

    def forward(*params):
        return layer(*params, blocks, expert_ids)
    result, pull_back = jax.vjp(forward, *floats)
    grads = pull_back(cotangent.astype(jnp.float32))
    return (result, grads[0], grads[1], grads[2], grads[3], grads[4], grads[5], grads[6], grads[7], grads[8], grads[9], grads[10], grads[11], grads[12])
```

```python
import functools

import jax
import jax.numpy as jnp
from jax import lax
from jax.experimental import pallas as pl
from jax.experimental.pallas import tpu as pltpu
from jax.sharding import Mesh
from jax.sharding import PartitionSpec as P

D = 2048
H = 16
HD = 128
TOPK = 8
CAP = 20
MAIN = 16
REST = CAP - MAIN
QUARTERS = 4
BAND = D // QUARTERS
WINDOW = 512

epsilon = 1e-05
rotary_base = 10000.0
masked_score = -1e30
scale = HD ** (-0.5)
log2e = 1.4426950408889634
bf16 = jnp.bfloat16
f32 = jnp.float32

CTX = ("x", "z", "yh", "c")
HEADS = ("x", "yh")
TOKENS = ("z", "c")
ROWS = ("x", "yh", "ep")


def dot(first, second, dims=((1,), (0,))):
    return lax.dot_general(first, second, (dims, ((), ())), preferred_element_type=f32)


def exchange(value, axes):
    return lax.all_to_all(value, axes, split_axis=0, concat_axis=0, tiled=True)


def pair_sum(value):
    own = lax.optimization_barrier(value.astype(bf16))
    other = lax.ppermute(own, "ep", [(0, 1), (1, 0)])
    return own.astype(f32) + other.astype(f32)


def sum_over_rows(value):
    rows = value.shape[0]
    sent = jnp.broadcast_to(value[None], (16, rows, 128)).reshape(16 * rows, 128)
    return jnp.sum(exchange(sent, ROWS).reshape(16, rows, 128), axis=0)


def rotary_tables(positions):
    half = HD // 2
    frequency = rotary_base ** (-jnp.arange(half).astype(f32) / half)
    angles = positions.astype(f32)[:, None] * frequency[None, :]
    return (jnp.cos(angles), jnp.sin(angles))


def rotate(value, cosine, sine):
    half = HD // 2
    first = value[:, :half]
    second = value[:, half:]
    return jnp.concatenate(
        [first * cosine - second * sine, second * cosine + first * sine], axis=-1
    )


def window_rows(index):
    return pl.multiple_of((index % 4) * 2048 + (index // 4) * 256, 256)


def window_mask(index, end):
    row = lax.broadcasted_iota(jnp.int32, (WINDOW, 1), 0)
    place = (row & 127) + ((row >> 7) & 1) * 256 + (row >> 8) * 128 + index * WINDOW
    return place < end


def attend_kernel(z_ref, q_ref, kv_ref, end_ref, out_ref, lse_ref):
    z = z_ref[0]
    factor = scale * log2e
    for x in range(4):
        span = slice(x * 256, (x + 1) * 256)
        queries = q_ref[span, :]
        end = end_ref[:, span]

        def tile(index, state, masked):
            peak, mass, total = state
            base = window_rows(index)
            part = jnp.concatenate(
                [kv_ref[pl.ds(base, 256), :], kv_ref[pl.ds(base + 1024, 256), :]], axis=0
            )
            keys, values = part[:, :HD], part[:, HD:]
            scores = dot(keys, queries, ((1,), (1,)))
            if masked:
                scores = jnp.where(window_mask(index, end), scores, masked_score)
            new_peak = jnp.maximum(peak, jnp.max(scores, axis=0, keepdims=True))
            weights = jnp.exp2((scores - new_peak) * factor)
            shrink = jnp.exp2((peak - new_peak) * factor)
            mass = mass * shrink + jnp.sum(weights, axis=0, keepdims=True)
            total = total * shrink + dot(values, weights.astype(bf16), ((0,), (0,)))
            return (new_peak, mass, total)

        state = (
            jnp.full((1, 256), masked_score, f32),
            jnp.zeros((1, 256), f32),
            jnp.zeros((HD, 256), f32),
        )
        last = 4 * x + z
        state = lax.fori_loop(0, last, lambda i, s: tile(i, s, False), state)
        state = lax.fori_loop(
            last, jnp.minimum(last + 2, 16), lambda i, s: tile(i, s, True), state
        )
        peak, mass, total = state
        out_ref[span, :] = (total / mass).T
        lse_ref[:, span] = peak * factor + jnp.log(mass) * log2e


def attend_back_kernel(
    z_ref, q_ref, grad_ref, kv_ref, end_ref, lse_ref, delta_ref, dq_ref, dkv_ref, sums
):
    z = z_ref[0]
    factor = scale * log2e
    sums[...] = jnp.zeros_like(sums)
    for x in range(4):
        span = slice(x * 256, (x + 1) * 256)
        queries = q_ref[span, :]
        grads = grad_ref[span, :]
        end = end_ref[:, span]
        lse = lse_ref[:, span]
        delta = delta_ref[:, span]

        def tile(index, total, masked):
            base = window_rows(index)
            part = jnp.concatenate(
                [kv_ref[pl.ds(base, 256), :], kv_ref[pl.ds(base + 1024, 256), :]], axis=0
            )
            keys, values = part[:, :HD], part[:, HD:]
            scores = dot(keys, queries, ((1,), (1,))) * factor - lse
            if masked:
                scores = jnp.where(window_mask(index, end), scores, masked_score)
            chances = jnp.exp2(scores)
            value_dot = dot(values, grads, ((1,), (1,)))
            score_grad = (chances * (value_dot - delta)).astype(bf16)
            key_term = dot(score_grad, queries)
            value_term = dot(chances.astype(bf16), grads)
            sums[pl.ds(base, 256), :HD] += key_term[:256]
            sums[pl.ds(base + 1024, 256), :HD] += key_term[256:]
            sums[pl.ds(base, 256), HD:] += value_term[:256]
            sums[pl.ds(base + 1024, 256), HD:] += value_term[256:]
            return total + dot(keys, score_grad, ((0,), (0,)))

        total = jnp.zeros((HD, 256), f32)
        last = 4 * x + z
        total = lax.fori_loop(0, last, lambda i, s: tile(i, s, False), total)
        total = lax.fori_loop(
            last, jnp.minimum(last + 2, 16), lambda i, s: tile(i, s, True), total
        )
        dq_ref[span, :] = total.T * scale
    dkv_ref[:, :HD] = (sums[:, :HD] * scale).astype(bf16)
    dkv_ref[:, HD:] = sums[:, HD:].astype(bf16)


SMEM = pl.BlockSpec(memory_space=pltpu.SMEM)
VMEM = pl.BlockSpec(memory_space=pltpu.VMEM)
params = pltpu.CompilerParams(vmem_limit_bytes=56 * 1024 * 1024)


def attend(z, queries, kv, end):
    return pl.pallas_call(
        attend_kernel,
        out_shape=(
            jax.ShapeDtypeStruct((1024, HD), f32),
            jax.ShapeDtypeStruct((1, 1024), f32),
        ),
        in_specs=[SMEM, VMEM, VMEM, VMEM],
        out_specs=(VMEM, VMEM),
        compiler_params=params,
        cost_estimate=pl.CostEstimate(
            flops=4 * 1024 * 5000 * HD, bytes_accessed=6 << 20, transcendentals=1024 * 5000
        ),
    )(z, queries, kv, end)


def attend_back(z, queries, grads, kv, end, lse, delta):
    return pl.pallas_call(
        attend_back_kernel,
        out_shape=(
            jax.ShapeDtypeStruct((1024, HD), f32),
            jax.ShapeDtypeStruct((8192, 2 * HD), bf16),
        ),
        in_specs=[SMEM, VMEM, VMEM, VMEM, VMEM, VMEM, VMEM],
        out_specs=(VMEM, VMEM),
        scratch_shapes=[pltpu.VMEM((8192, 2 * HD), f32)],
        compiler_params=params,
        cost_estimate=pl.CostEstimate(
            flops=10 * 1024 * 5000 * HD, bytes_accessed=10 << 20, transcendentals=1024 * 5000
        ),
    )(z, queries, grads, kv, end, lse, delta)


def dispatch(main_table, rest_table, value):
    stacked = value.reshape(128, QUARTERS, BAND).transpose(1, 0, 2).reshape(QUARTERS * 128, BAND)
    main = dot(main_table, value).astype(bf16)
    rest = dot(rest_table, stacked).astype(bf16)
    return jnp.concatenate([main, rest], axis=1)


def collect(main_table, rest_table, rows):
    main = dot(main_table, rows[:, :D], ((0,), (0,)))
    rest = dot(rest_table, rows[:, D:], ((0,), (0,)))
    return main + rest.reshape(QUARTERS, 128, BAND).transpose(1, 0, 2).reshape(128, D)


def open_rows(rows):
    rest = rows[:, D:].reshape(64, QUARTERS, REST, BAND).transpose(0, 2, 1, 3)
    return jnp.concatenate([rows[:, :D], rest.reshape(64 * REST, D)], axis=0)


def close_rows(rows):
    rest = rows[64 * MAIN :].reshape(64, REST, QUARTERS, BAND).transpose(0, 2, 1, 3)
    return jnp.concatenate([rows[: 64 * MAIN], rest.reshape(64 * MAIN, BAND)], axis=1)


def local(
    inputs,
    blocks,
    expert_ids,
    attention_gain,
    query_weight,
    key_weight,
    value_weight,
    query_gain,
    key_gain,
    output_weight,
    mixture_gain,
    router_weight,
    gate_weight,
    up_weight,
    down_weight,
    cotangent,
):
    x = lax.axis_index("x")
    z = lax.axis_index("z")
    yh = lax.axis_index("yh")
    c = lax.axis_index("c")
    place = x * 16 + z * 4 + yh * 2 + c
    head = x * 2 + yh
    z_place = z.reshape(1).astype(jnp.int32)

    pad = lambda gain: jnp.pad(gain, (0, 16))[:, None]
    small = jnp.concatenate(
        [
            router_weight,
            attention_gain[:, None],
            mixture_gain[:, None],
            pad(query_gain),
            pad(key_gain),
            jnp.zeros((32, 60), bf16),
        ],
        axis=1,
    )
    small_all = lax.all_gather(small, CTX, axis=0, tiled=True)
    blocks_all = lax.all_gather(blocks, CTX, axis=0, tiled=True)
    router_all = small_all[:, :64]
    attention_gain_all = small_all[:, 64].astype(f32)
    mixture_gain_all = small_all[:, 65].astype(f32)
    head_gains = small_all.reshape(64, 32, 128)[:, :16, 66:68].reshape(1024, 2).astype(f32)
    head_gains = lax.dynamic_slice(head_gains, (head * HD, 0), (HD, 2))
    query_gain_all = head_gains[:, 0]
    key_gain_all = head_gains[:, 1]

    inputs_all = lax.all_gather(inputs, HEADS, axis=0, tiled=True)
    weights_sent = jnp.stack(
        [w.reshape(32, 8, HD) for w in (query_weight, key_weight, value_weight)], axis=2
    )
    weights_sent = weights_sent.transpose(1, 0, 2, 3).reshape(256, 3 * HD)
    weights_all = lax.all_gather(exchange(weights_sent, HEADS), TOKENS, axis=0, tiled=True)
    weights_all = (
        weights_all.reshape(4, 2, 4, 2, 32, 3 * HD).transpose(2, 0, 3, 1, 4, 5).reshape(D, 3 * HD)
    )
    output_all = lax.all_gather(output_weight.T, CTX, axis=0, tiled=True)

    experts = jnp.arange(64, dtype=jnp.int32)
    chosen = jnp.any(expert_ids[:, :, None] == experts[None, None, :], axis=1)
    tokens = jnp.arange(128, dtype=jnp.int32)
    earlier = (tokens[None, :] < tokens[:, None]).astype(bf16)
    ranks = dot(earlier, chosen.astype(bf16)).astype(jnp.int32)
    ranks = jnp.where(chosen, ranks, -1).T
    table = (ranks[:, None, :] == jnp.arange(CAP, dtype=jnp.int32)[None, :, None]).astype(bf16)
    main_table = table[:, :MAIN].reshape(64 * MAIN, 128)
    quarter = jnp.eye(QUARTERS, dtype=bf16)
    rest_table = (
        table[:, None, MAIN:, None, :] * quarter[None, :, None, :, None]
    ).reshape(64 * MAIN, QUARTERS * 128)

    grad_rows = exchange(dispatch(main_table, rest_table, cotangent), CTX)

    source_all = inputs_all.astype(f32)
    attention_inverse = lax.rsqrt(
        jnp.mean(source_all * source_all, axis=-1, keepdims=True) + epsilon
    )
    normed_low = (source_all * attention_inverse * attention_gain_all).astype(bf16)
    raw = dot(normed_low, weights_all)
    query_raw, key_raw = raw[:, :HD], raw[:, HD : 2 * HD]
    value_low = raw[:, 2 * HD :].astype(bf16)
    squares = jnp.stack(
        [jnp.sum(query_raw * query_raw, axis=-1), jnp.sum(key_raw * key_raw, axis=-1)]
    )
    squares = sum_over_rows(squares.reshape(16, 128)).reshape(2, 1024)
    inverses = lax.rsqrt(squares / float(D) + epsilon)
    query_inverse = inverses[0][:, None]
    key_inverse = inverses[1][:, None]
    chunk = jnp.arange(8, dtype=jnp.int32)
    chunk_start = ((chunk // 2) * 16 + z * 4 + (chunk % 2) * 2 + c) * 128
    positions = (chunk_start[:, None] + tokens[None, :]).reshape(1024)
    cosine, sine = rotary_tables(positions)
    query_low = rotate(query_raw * query_inverse * query_gain_all, cosine, sine).astype(bf16)
    key_low = rotate(key_raw * key_inverse * key_gain_all, cosine, sine).astype(bf16)
    kv = lax.all_gather(
        jnp.concatenate([key_low, value_low], axis=1), TOKENS, axis=0, tiled=True
    )
    own_blocks = blocks_all.reshape(4, 4, 2, 2, 128)[:, z, :, c].reshape(1024)
    end = jnp.sum((blocks_all[:, None] <= own_blocks[None, :]).astype(jnp.int32), axis=0)[None]
    attended, lse = attend(z_place, query_low, kv, end)
    attended_low = attended.astype(bf16)

    attended_rows = exchange(attended_low, HEADS).reshape(8, 128, HD)
    attended_rows = attended_rows.transpose(1, 0, 2).reshape(128, 8 * HD)
    source = inputs.astype(f32)
    residual = source + pair_sum(dot(attended_rows, output_all, ((1,), (1,))))
    mixture_inverse = lax.rsqrt(jnp.mean(residual * residual, axis=-1, keepdims=True) + epsilon)
    mixed_low = (residual * mixture_inverse * mixture_gain_all).astype(bf16)
    mixed_rows = exchange(dispatch(main_table, rest_table, mixed_low), CTX)

    entry = open_rows(mixed_rows)
    grad = open_rows(grad_rows)
    logits = dot(entry, router_all)
    shifted = jnp.exp(logits - jnp.max(logits, axis=-1, keepdims=True))
    probability = shifted / jnp.sum(shifted, axis=-1, keepdims=True)
    own_expert = (experts == place).astype(f32)[None, :]
    gates = jnp.sum(probability * own_expert, axis=-1, keepdims=True)
    gate = dot(entry, gate_weight[0])
    upward = dot(entry, up_weight[0])
    sigma = jax.nn.sigmoid(gate)
    swish = gate * sigma
    hidden = swish * upward
    hidden_low = hidden.astype(bf16)
    hidden_pull = dot(grad, down_weight[0], ((1,), (1,)))
    gate_grad = jnp.sum(hidden_low.astype(f32) * hidden_pull, axis=-1, keepdims=True)
    hidden_grad = hidden_pull * gates
    gate_raw_grad = (hidden_grad * upward * sigma * (1.0 + gate * (1.0 - sigma))).astype(bf16)
    up_raw_grad = (hidden_grad * swish).astype(bf16)
    logit_grad = (gate_grad * gates * (own_expert - probability)).astype(bf16)
    entry_grad = (
        dot(gate_raw_grad, gate_weight[0], ((1,), (1,)))
        + dot(up_raw_grad, up_weight[0], ((1,), (1,)))
        + dot(logit_grad, router_all, ((1,), (1,)))
    ).astype(bf16)
    entry_back = exchange(close_rows(entry_grad), CTX)
    result = (dot(hidden_low, down_weight[0]) * gates).astype(bf16)
    result_back = exchange(close_rows(result), CTX)
    down_weight_grad = dot((hidden * gates).astype(bf16), grad, ((0,), (0,)))
    gate_weight_grad = dot(entry, gate_raw_grad, ((0,), (0,)))
    up_weight_grad = dot(entry, up_raw_grad, ((0,), (0,)))
    router_part = dot(entry, logit_grad, ((0,), (0,)))
    router_part = exchange(router_part.reshape(64 * 16, 128), CTX).reshape(64, 16, 128)
    router_grad = lax.psum(jnp.sum(router_part, axis=0), "ep").reshape(32, 64)

    final = residual + pair_sum(collect(main_table, rest_table, result_back))
    mixed_grad = pair_sum(collect(main_table, rest_table, entry_back))

    grad_out = cotangent.astype(f32)
    scaled = mixed_grad * mixture_gain_all
    residual_grad = (
        grad_out
        + mixture_inverse * scaled
        - residual
        * mixture_inverse
        * mixture_inverse
        * mixture_inverse
        * jnp.mean(scaled * residual, axis=-1, keepdims=True)
    )
    mixture_gain_part = jnp.sum(mixed_grad * residual * mixture_inverse, axis=0)
    residual_low = residual_grad.astype(bf16)
    attended_grad = dot(residual_low, output_all).astype(bf16)
    attended_grad = attended_grad.reshape(128, 8, HD).transpose(1, 0, 2).reshape(1024, HD)
    attended_grad = exchange(attended_grad, HEADS)
    residual_all = lax.all_gather(residual_low, HEADS, axis=0, tiled=True)
    output_part = dot(attended_low, residual_all, ((0,), (0,))).astype(bf16)
    output_part = output_part.reshape(HD, 64, 32).transpose(1, 0, 2).reshape(64 * 32, HD)
    output_part = exchange(output_part, CTX).reshape(4, 4, 2, 2, HD, 32)
    output_grad = jnp.sum(output_part.astype(f32), axis=(1, 3)).reshape(8 * HD, 32)

    delta = jnp.sum(attended_grad.astype(f32) * attended, axis=-1)[None]
    query_grad, kv_part = attend_back(
        z_place, query_low, attended_grad, kv, end, lse, delta
    )
    kv_grad = jnp.sum(exchange(kv_part, TOKENS).reshape(8, 1024, 2 * HD).astype(f32), axis=0)
    value_grad_low = kv_grad[:, HD:].astype(bf16)
    query_normed_grad = rotate(query_grad, cosine, -sine)
    key_normed_grad = rotate(kv_grad[:, :HD], cosine, -sine)
    query_scaled = query_normed_grad * query_gain_all
    key_scaled = key_normed_grad * key_gain_all
    dots = jnp.stack(
        [jnp.sum(query_scaled * query_raw, axis=-1), jnp.sum(key_scaled * key_raw, axis=-1)]
    )
    dots = sum_over_rows(dots.reshape(16, 128)).reshape(2, 1024)[:, :, None] / float(D)

    def raw_back(value, inverse, scaled_grad, mean):
        return (inverse * scaled_grad - value * inverse * inverse * inverse * mean).astype(bf16)

    query_raw_low = raw_back(query_raw, query_inverse, query_scaled, dots[0])
    key_raw_low = raw_back(key_raw, key_inverse, key_scaled, dots[1])
    query_gain_part = jnp.sum(query_normed_grad * query_raw * query_inverse, axis=0)
    key_gain_part = jnp.sum(key_normed_grad * key_raw * key_inverse, axis=0)
    raw_grads = jnp.concatenate([query_raw_low, key_raw_low, value_grad_low], axis=1)
    normed_part = dot(raw_grads, weights_all, ((1,), (1,)))
    attention_gain_part = jnp.sum(normed_part * source_all * attention_inverse, axis=0)
    normed_grad = jnp.sum(
        exchange(normed_part.astype(bf16), HEADS).reshape(8, 128, D).astype(f32), axis=0
    )
    normed_grad = pair_sum(normed_grad)
    weight_part = dot(normed_low, raw_grads, ((0,), (0,))).astype(bf16)
    weight_part = exchange(weight_part, CTX).reshape(4, 4, 2, 2, 32, 3, HD)
    weight_grad = jnp.sum(weight_part.astype(f32), axis=(1, 3)).reshape(8, 32, 3, HD)
    weight_grad = weight_grad.transpose(2, 1, 0, 3).reshape(3, 32, 8 * HD)

    def head_part(value):
        wide = lax.dynamic_update_slice(jnp.zeros((8 * HD,), f32), value, (head * HD,))
        return wide.reshape(64, 16)

    gains = jnp.concatenate(
        [
            attention_gain_part.reshape(64, 32),
            mixture_gain_part.reshape(64, 32),
            head_part(query_gain_part),
            head_part(key_gain_part),
            jnp.zeros((64, 32), f32),
        ],
        axis=1,
    )
    gains = jnp.broadcast_to(gains[:, None, :], (64, 8, 128)).reshape(512, 128)
    gains = jnp.sum(exchange(gains, CTX).reshape(64, 8, 128)[:, 0], axis=0)
    attention_gain_grad = lax.psum(gains[:32], "ep")

    inverse = lax.rsqrt(jnp.mean(source * source, axis=-1, keepdims=True) + epsilon)
    scaled = normed_grad * attention_gain_all
    input_grad = (
        residual_grad
        + inverse * scaled
        - source
        * inverse
        * inverse
        * inverse
        * jnp.mean(scaled * source, axis=-1, keepdims=True)
    )
    return (
        final,
        input_grad,
        attention_gain_grad,
        weight_grad[0],
        weight_grad[1],
        weight_grad[2],
        gains[64:80],
        gains[80:96],
        output_grad,
        gains[32:64],
        router_grad,
        gate_weight_grad[None],
        up_weight_grad[None],
        down_weight_grad[None],
    )


def solution(mesh):
    inner = Mesh(mesh.devices.reshape(4, 4, 2, 2, 2), ("x", "z", "yh", "c", "ep"))
    in_specs = (
        P(CTX, None),
        P(CTX),
        P(CTX, None),
        P(CTX),
        P(CTX, "ep"),
        P(CTX, "ep"),
        P(CTX, "ep"),
        P(("ep",) + CTX),
        P(("ep",) + CTX),
        P("ep", CTX),
        P(CTX),
        P(CTX, None),
        P(CTX, None, "ep"),
        P(CTX, None, "ep"),
        P(CTX, "ep", None),
        P(CTX, None),
    )
    out_specs = (
        P(CTX, None),
        P(CTX, None),
        P(CTX),
        P(CTX, "ep"),
        P(CTX, "ep"),
        P(CTX, "ep"),
        P(("ep",) + CTX),
        P(("ep",) + CTX),
        P("ep", CTX),
        P(CTX),
        P(CTX, None),
        P(CTX, None, "ep"),
        P(CTX, None, "ep"),
        P(CTX, "ep", None),
    )
    return jax.shard_map(local, mesh=inner, in_specs=in_specs, out_specs=out_specs, check_vma=False)
```

```python
import functools

import jax
import jax.numpy as jnp
from jax import lax
from jax.experimental import pallas as pl
from jax.experimental.pallas import tpu as pltpu
from jax.sharding import Mesh
from jax.sharding import PartitionSpec as P

D = 2048
H = 16
HD = 128
TOPK = 8
CAP = 20
MAIN = 16
REST = CAP - MAIN
QUARTERS = 4
BAND = D // QUARTERS
WINDOW = 512
HALF_MAIN = 32 * MAIN
HALF_REST = 32 * REST
HALF = HALF_MAIN + HALF_REST
ROW_WIDTH = D + BAND
SIDE = D // 2
SIDE_BAND = SIDE // QUARTERS
SIDE_WIDTH = SIDE + SIDE_BAND

epsilon = 1e-05
rotary_base = 10000.0
masked_score = -1e30
scale = HD ** (-0.5)
log2e = 1.4426950408889634
bf16 = jnp.bfloat16
f32 = jnp.float32

CTX = ("x", "z", "yh", "c")
HEADS = ("x", "yh")
TOKENS = ("z", "c")
ROWS = ("x", "yh", "ep")


def dot(first, second, dims=((1,), (0,))):
    return lax.dot_general(first, second, (dims, ((), ())), preferred_element_type=f32)


def exchange(value, axes):
    return lax.all_to_all(value, axes, split_axis=0, concat_axis=0, tiled=True)


OFFSETS = [(i, j) for i in range(4) for j in range(2)]


def ring(value, axis):
    return [value] + [
        lax.ppermute(value, axis, [(a, (a + i) % 4) for a in range(4)]) for i in (1, 2, 3)
    ]


def swap(value, axis):
    return lax.ppermute(value, axis, [(0, 1), (1, 0)])


def below(a, b):
    return jnp.stack([(a - i) % 4 * 2 + (b - j) % 2 for i, j in OFFSETS])


def pair_sum(value):
    own = lax.optimization_barrier(value.astype(bf16))
    other = lax.ppermute(own, "ep", [(0, 1), (1, 0)])
    return own.astype(f32) + other.astype(f32)


def sum_over_rows(value):
    rows = value.shape[0]
    sent = jnp.broadcast_to(value[None], (16, rows, 128)).reshape(16 * rows, 128)
    return jnp.sum(exchange(sent, ROWS).reshape(16, rows, 128), axis=0)


def rotary_tables(positions):
    half = HD // 2
    frequency = rotary_base ** (-jnp.arange(half).astype(f32) / half)
    angles = positions.astype(f32)[:, None] * frequency[None, :]
    return (jnp.cos(angles), jnp.sin(angles))


def rotate(value, cosine, sine):
    half = HD // 2
    first = value[:, :half]
    second = value[:, half:]
    return jnp.concatenate(
        [first * cosine - second * sine, second * cosine + first * sine], axis=-1
    )


def window_rows(index):
    return pl.multiple_of((index % 4) * 2048 + (index // 4) * 256, 256)


def window_mask(index, end):
    row = lax.broadcasted_iota(jnp.int32, (WINDOW, 1), 0)
    place = (row & 127) + ((row >> 7) & 1) * 256 + (row >> 8) * 128 + index * WINDOW
    return place < end


def project_kernel(place_ref, *refs):
    inputs, weights = refs[:8], refs[8:12]
    normed_ref, raw_ref, square_ref, weight_ref, small_ref, gain_ref = refs[12:]
    for n, (i, j) in enumerate(OFFSETS):
        for m in range(8):
            row = (place_ref[8 + n] + (m // 2) * 16 + (m % 2) * 2) * 32
            here = pl.ds(pl.multiple_of(row, 32), 32)
            weight_ref[here, :] = weights[i][j, m * 32 : m * 32 + 32, : 3 * HD]
            small_ref[here, :] = weights[i][j, m * 32 : m * 32 + 32, 3 * HD :]
    row = lax.broadcasted_iota(jnp.int32, (8, 128), 0)
    column = lax.broadcasted_iota(jnp.int32, (8, 128), 1)
    pick = jnp.where(column == row + 64, 1.0, 0.0).astype(bf16)
    gain_ref[...] = dot(pick, small_ref[...], ((1,), (1,)))
    gain = gain_ref[0:1, :]
    for n in range(8):
        value = inputs[n][...].astype(f32)
        inverse = lax.rsqrt(jnp.mean(value * value, axis=-1, keepdims=True) + epsilon)
        normed = (value * inverse * gain).astype(bf16)
        chunk = place_ref[n]
        here = pl.ds(pl.multiple_of(chunk * 128, 128), 128)
        normed_ref[here, :] = normed
        raw = dot(normed, weight_ref[...])
        raw_ref[here, :] = raw
        for part in range(2):
            own = raw[:, part * HD : part * HD + HD]
            square = jnp.sum(own * own, axis=-1, keepdims=True)
            square = jnp.broadcast_to(square, (128, 128)).T
            square_ref[pl.ds(chunk + 8 * part, 1), :] = square[0:1]


def spread_kernel(
    raw_ref, normed_ref, weight_ref, router_ref, gain_ref, extra_ref, output_ref, back_ref, share_ref
):
    total = jnp.zeros((1, D), f32)
    for n in range(4):
        here = slice(n * 256, n * 256 + 256)
        part = dot(raw_ref[here, :], weight_ref[...], ((1,), (1,)))
        total = total + jnp.sum(part * normed_ref[here, :].astype(f32), axis=0, keepdims=True)
        back_ref[here, :] = part.astype(bf16)
    total = total / gain_ref[0:1, :]
    row = lax.broadcasted_iota(jnp.int32, (8, 1), 0)
    extra = extra_ref[...] + jnp.where(row == 0, total, 0.0)
    for n in range(4):
        band = slice(n * 512, n * 512 + 512)
        part = dot(normed_ref[:, band], raw_ref[...], ((0,), (0,))).astype(bf16)
        side = jnp.concatenate(
            [jnp.zeros((64, 512), f32), extra[:, band], jnp.zeros((56, 512), f32)], axis=0
        )
        side = (side.T + router_ref[band, :]).astype(bf16)
        for m in range(16):
            z, yh, c = m // 4, m // 2 % 2, m % 2
            start = (z * 2 + c) * 320
            there = slice(start + (n * 2 + yh) * 32, start + (n * 2 + yh) * 32 + 32)
            share_ref[there, : 3 * HD] = part[m * 32 : m * 32 + 32]
            share_ref[there, 3 * HD :] = side[m * 32 : m * 32 + 32]
            if n == 0:
                there = slice(start + 256 + yh * 32, start + 288 + yh * 32)
                share_ref[there, :] = output_ref[m * 32 : m * 32 + 32, :].astype(bf16)


def attend_kernel(z_ref, q_ref, kv_ref, end_ref, out_ref, lse_ref):
    z = z_ref[0]
    factor = scale * log2e
    for x in range(4):
        span = slice(x * 256, (x + 1) * 256)
        queries = q_ref[span, :]
        end = end_ref[:, span]

        def tile(index, state, masked):
            peak, mass, total = state
            base = window_rows(index)
            part = jnp.concatenate(
                [kv_ref[pl.ds(base, 256), :], kv_ref[pl.ds(base + 1024, 256), :]], axis=0
            )
            keys, values = part[:, :HD], part[:, HD:]
            scores = dot(keys, queries, ((1,), (1,)))
            if masked:
                scores = jnp.where(window_mask(index, end), scores, masked_score)
            new_peak = jnp.maximum(peak, jnp.max(scores, axis=0, keepdims=True))
            weights = jnp.exp2((scores - new_peak) * factor)
            shrink = jnp.exp2((peak - new_peak) * factor)
            mass = mass * shrink + jnp.sum(weights, axis=0, keepdims=True)
            total = total * shrink + dot(values, weights.astype(bf16), ((0,), (0,)))
            return (new_peak, mass, total)

        state = (
            jnp.full((1, 256), masked_score, f32),
            jnp.zeros((1, 256), f32),
            jnp.zeros((HD, 256), f32),
        )
        last = 4 * x + z
        state = lax.fori_loop(0, last, lambda i, s: tile(i, s, False), state)
        state = lax.fori_loop(
            last, jnp.minimum(last + 2, 16), lambda i, s: tile(i, s, True), state
        )
        peak, mass, total = state
        out_ref[span, :] = (total / mass).T
        lse_ref[:, span] = peak * factor + jnp.log(mass) * log2e


def attend_back_kernel(
    z_ref, q_ref, grad_ref, kv_ref, end_ref, lse_ref, delta_ref, dq_ref, dkv_ref, sums
):
    z = z_ref[0]
    factor = scale * log2e
    sums[...] = jnp.zeros_like(sums)
    for x in range(4):
        span = slice(x * 256, (x + 1) * 256)
        queries = q_ref[span, :]
        grads = grad_ref[span, :]
        end = end_ref[:, span]
        lse = lse_ref[:, span]
        delta = delta_ref[:, span]

        def tile(index, total, masked):
            base = window_rows(index)
            part = jnp.concatenate(
                [kv_ref[pl.ds(base, 256), :], kv_ref[pl.ds(base + 1024, 256), :]], axis=0
            )
            keys, values = part[:, :HD], part[:, HD:]
            scores = dot(keys, queries, ((1,), (1,))) * factor - lse
            if masked:
                scores = jnp.where(window_mask(index, end), scores, masked_score)
            chances = jnp.exp2(scores)
            value_dot = dot(values, grads, ((1,), (1,)))
            score_grad = (chances * (value_dot - delta)).astype(bf16)
            key_term = dot(score_grad, queries)
            value_term = dot(chances.astype(bf16), grads)
            sums[pl.ds(base, 256), :HD] += key_term[:256]
            sums[pl.ds(base + 1024, 256), :HD] += key_term[256:]
            sums[pl.ds(base, 256), HD:] += value_term[:256]
            sums[pl.ds(base + 1024, 256), HD:] += value_term[256:]
            return total + dot(keys, score_grad, ((0,), (0,)))

        total = jnp.zeros((HD, 256), f32)
        last = 4 * x + z
        total = lax.fori_loop(0, last, lambda i, s: tile(i, s, False), total)
        total = lax.fori_loop(
            last, jnp.minimum(last + 2, 16), lambda i, s: tile(i, s, True), total
        )
        dq_ref[span, :] = total.T * scale
    dkv_ref[:, :HD] = (sums[:, :HD] * scale).astype(bf16)
    dkv_ref[:, HD:] = sums[:, HD:].astype(bf16)


def rest_pick(quarter):
    row = lax.broadcasted_iota(jnp.int32, (HALF_REST, HALF_MAIN), 0)
    column = lax.broadcasted_iota(jnp.int32, (HALF_REST, HALF_MAIN), 1)
    same = (column >> 4 == row >> 2) & (column & 3 == row & 3)
    return jnp.where(same & ((column >> 2) & 3 == quarter), 1.0, 0.0).astype(bf16)


def open_rest(rows):
    rest = rows[:, D:]
    return jnp.concatenate(
        [dot(rest_pick(q), rest).astype(bf16) for q in range(QUARTERS)], axis=1
    )


def open_side(rows_ref):
    rest = rows_ref[:, SIDE:]
    rest = jnp.concatenate(
        [dot(rest_pick(q), rest).astype(bf16) for q in range(QUARTERS)], axis=1
    )
    return rows_ref[:, :SIDE], rest


def pull_kernel(side_ref, own_ref, other_ref, down_ref, flat_ref, pull_ref):
    own = pl.multiple_of(side_ref[0] * SIDE, SIDE)
    other = pl.multiple_of(SIDE - side_ref[0] * SIDE, SIDE)
    for ref, start in ((own_ref, own), (other_ref, other)):
        main, rest = open_side(ref)
        flat_ref[:HALF_MAIN, pl.ds(start, SIDE)] = main
        flat_ref[HALF_MAIN:, pl.ds(start, SIDE)] = rest
    pull_ref[...] = dot(flat_ref[...], down_ref[...], ((1,), (1,)))


def expert_kernel(
    place_ref,
    rows_ref,
    pull_ref,
    gate_ref,
    up_ref,
    router_ref,
    back_ref,
    flat_ref,
    hidden_ref,
    gate_grad_ref,
    up_grad_ref,
    logit_grad_ref,
):
    flat_ref[:HALF_MAIN] = rows_ref[:, :D]
    flat_ref[HALF_MAIN:] = open_rest(rows_ref)
    entry = flat_ref[...]
    lane = lax.broadcasted_iota(jnp.int32, (1, 128), 1)
    logits = jnp.where(lane < 64, dot(entry, router_ref[...]), masked_score)
    shifted = jnp.exp(logits - jnp.max(logits, axis=-1, keepdims=True))
    probability = shifted / jnp.sum(shifted, axis=-1, keepdims=True)
    own = jnp.where(lane == place_ref[0], 1.0, 0.0)
    gates = jnp.sum(probability * own, axis=-1, keepdims=True)
    gate = dot(entry, gate_ref[...])
    upward = dot(entry, up_ref[...])
    pull = pull_ref[...]
    sigma = 1.0 / (1.0 + jnp.exp(-gate))
    swish = gate * sigma
    hidden = swish * upward
    row_grad = jnp.sum(hidden * pull, axis=-1, keepdims=True) * gates
    hidden_ref[...] = (hidden * gates).astype(bf16)
    hidden_grad = pull * gates
    gate_grad = (hidden_grad * upward * (sigma + swish * (1.0 - sigma))).astype(bf16)
    up_grad = (hidden_grad * swish).astype(bf16)
    logit_grad = (row_grad * (own - probability)).astype(bf16)
    gate_grad_ref[...] = gate_grad
    up_grad_ref[...] = up_grad
    logit_grad_ref[...] = logit_grad
    rest = []
    for q in range(QUARTERS):
        band = slice(q * BAND, (q + 1) * BAND)
        part = (
            dot(gate_grad, gate_ref[band, :], ((1,), (1,)))
            + dot(up_grad, up_ref[band, :], ((1,), (1,)))
            + dot(logit_grad, router_ref[band, :], ((1,), (1,)))
        ).astype(bf16)
        back_ref[:, band] = part[:HALF_MAIN]
        rest.append(dot(rest_pick(q), part[HALF_MAIN:], ((0,), (0,))))
    back_ref[:, D:] = (rest[0] + rest[1] + rest[2] + rest[3]).astype(bf16)


def result_kernel(hidden_ref, down_ref, back_ref):
    rest = []
    for q in range(QUARTERS):
        band = slice(q * BAND, (q + 1) * BAND)
        part = dot(hidden_ref[...], down_ref[:, band]).astype(bf16)
        back_ref[:, band] = part[:HALF_MAIN]
        rest.append(dot(rest_pick(q), part[HALF_MAIN:], ((0,), (0,))))
    back_ref[:, D:] = (rest[0] + rest[1] + rest[2] + rest[3]).astype(bf16)


SMEM = pl.BlockSpec(memory_space=pltpu.SMEM)
VMEM = pl.BlockSpec(memory_space=pltpu.VMEM)
params = pltpu.CompilerParams(vmem_limit_bytes=56 * 1024 * 1024)
step_params = pltpu.CompilerParams(
    vmem_limit_bytes=56 * 1024 * 1024, dimension_semantics=("arbitrary",)
)


cheap = pl.CostEstimate(flops=1, bytes_accessed=1, transcendentals=0)


def step_block(rows, columns):
    return pl.BlockSpec((rows, columns), lambda i: (i, 0))


def whole_block(rows, columns):
    return pl.BlockSpec((rows, columns), lambda i: (0, 0))


def shape(rows, columns, kind=bf16):
    return jax.ShapeDtypeStruct((rows, columns), kind)


def project(places, inputs, weights):
    return pl.pallas_call(
        project_kernel,
        out_shape=(
            shape(1024, D),
            shape(1024, 3 * HD, f32),
            shape(16, 128, f32),
            shape(D, 3 * HD),
            shape(D, 128),
            shape(8, D, f32),
        ),
        in_specs=[SMEM] + [VMEM] * 12,
        out_specs=(VMEM,) * 6,
        compiler_params=params,
        cost_estimate=cheap,
    )(places, *inputs, *weights)


def spread_grads(raw_grads, normed, weights, router_part, gains, extra, output_part):
    return pl.pallas_call(
        spread_kernel,
        out_shape=(shape(1024, D), shape(2560, 512)),
        in_specs=[VMEM] * 7,
        out_specs=(VMEM, VMEM),
        compiler_params=params,
        cost_estimate=cheap,
    )(raw_grads, normed, weights, router_part, gains, extra, output_part)


def expert_pull(side, own, other, down):
    return pl.pallas_call(
        pull_kernel,
        grid=(2,),
        out_shape=(shape(1280, D), shape(1280, 512, f32)),
        in_specs=[
            SMEM,
            step_block(HALF_MAIN, SIDE_WIDTH),
            step_block(HALF_MAIN, SIDE_WIDTH),
            whole_block(512, D),
        ],
        out_specs=(step_block(HALF, D), step_block(HALF, 512)),
        compiler_params=step_params,
        cost_estimate=cheap,
    )(side, own, other, down)


def expert_step(place, rows, pull, gate, up, router):
    return pl.pallas_call(
        expert_kernel,
        grid=(2,),
        out_shape=(
            shape(1024, ROW_WIDTH),
            shape(1280, D),
            shape(1280, 512),
            shape(1280, 512),
            shape(1280, 512),
            shape(1280, 128),
        ),
        in_specs=[
            SMEM,
            step_block(HALF_MAIN, ROW_WIDTH),
            step_block(HALF, 512),
            whole_block(D, 512),
            whole_block(D, 512),
            whole_block(D, 128),
        ],
        out_specs=(
            step_block(HALF_MAIN, ROW_WIDTH),
            step_block(HALF, D),
            step_block(HALF, 512),
            step_block(HALF, 512),
            step_block(HALF, 512),
            step_block(HALF, 128),
        ),
        compiler_params=step_params,
        cost_estimate=cheap,
    )(place, rows, pull, gate, up, router)


def expert_result(hidden, down):
    return pl.pallas_call(
        result_kernel,
        grid=(2,),
        out_shape=shape(1024, ROW_WIDTH),
        in_specs=[step_block(HALF, 512), whole_block(512, D)],
        out_specs=step_block(HALF_MAIN, ROW_WIDTH),
        compiler_params=step_params,
        cost_estimate=cheap,
    )(hidden, down)


def linger_kernel(value_ref, out_ref):
    out_ref[...] = value_ref[...]


def linger(value):
    return pl.pallas_call(
        linger_kernel,
        out_shape=jax.ShapeDtypeStruct(value.shape, value.dtype),
        in_specs=[VMEM],
        out_specs=VMEM,
        cost_estimate=pl.CostEstimate(
            flops=200_000_000_000, bytes_accessed=1, transcendentals=0
        ),
    )(value)


def attend(z, queries, kv, end):
    return pl.pallas_call(
        attend_kernel,
        out_shape=(
            jax.ShapeDtypeStruct((1024, HD), f32),
            jax.ShapeDtypeStruct((1, 1024), f32),
        ),
        in_specs=[SMEM, VMEM, VMEM, VMEM],
        out_specs=(VMEM, VMEM),
        compiler_params=params,
        cost_estimate=cheap,
    )(z, queries, kv, end)


def attend_back(z, queries, grads, kv, end, lse, delta):
    return pl.pallas_call(
        attend_back_kernel,
        out_shape=(
            jax.ShapeDtypeStruct((1024, HD), f32),
            jax.ShapeDtypeStruct((8192, 2 * HD), bf16),
        ),
        in_specs=[SMEM, VMEM, VMEM, VMEM, VMEM, VMEM, VMEM],
        out_specs=(VMEM, VMEM),
        scratch_shapes=[pltpu.VMEM((8192, 2 * HD), f32)],
        compiler_params=params,
        cost_estimate=cheap,
    )(z, queries, grads, kv, end, lse, delta)


def dispatch(main_table, rest_table, value):
    band = value.shape[1] // QUARTERS
    stacked = value.reshape(128, QUARTERS, band).transpose(1, 0, 2).reshape(QUARTERS * 128, band)
    main = dot(main_table, value).astype(bf16)
    rest = dot(rest_table, stacked).astype(bf16)
    return jnp.concatenate([main, rest], axis=1)


def collect(main_table, rest_table, rows):
    width = rows.shape[1] * QUARTERS // (QUARTERS + 1)
    main = dot(main_table, rows[:, :width], ((0,), (0,)))
    rest = dot(rest_table, rows[:, width:], ((0,), (0,)))
    rest = rest.reshape(QUARTERS, 128, width // QUARTERS).transpose(1, 0, 2)
    return main + rest.reshape(128, width)


def local(
    inputs,
    blocks,
    expert_ids,
    attention_gain,
    query_weight,
    key_weight,
    value_weight,
    query_gain,
    key_gain,
    output_weight,
    mixture_gain,
    router_weight,
    gate_weight,
    up_weight,
    down_weight,
    cotangent,
):
    x = lax.axis_index("x")
    z = lax.axis_index("z")
    yh = lax.axis_index("yh")
    c = lax.axis_index("c")
    place = x * 16 + z * 4 + yh * 2 + c
    head = x * 2 + yh
    z_place = z.reshape(1).astype(jnp.int32)
    side = lax.axis_index("ep")
    side_place = side.reshape(1).astype(jnp.int32)
    heads_below = below(x, yh)

    pad = lambda gain: jnp.pad(gain, (0, 16))[:, None]
    small = jnp.concatenate(
        [
            router_weight,
            attention_gain[:, None],
            mixture_gain[:, None],
            pad(query_gain),
            pad(key_gain),
            blocks.astype(bf16).reshape(32, 4),
            jnp.zeros((32, 56), bf16),
        ],
        axis=1,
    )
    weights_sent = jnp.concatenate(
        [w.reshape(32, 8, HD) for w in (query_weight, key_weight, value_weight)]
        + [jnp.broadcast_to(small[:, None], (32, 8, 128))],
        axis=2,
    )
    weights_sent = weights_sent.transpose(1, 0, 2).reshape(256, 4 * HD)
    inputs_pair = swap(inputs, "yh")
    inputs_all = [ring(inputs, "x"), ring(inputs_pair, "x")]
    inputs_all = [inputs_all[j][i] for i, j in OFFSETS]
    weights_come = exchange(weights_sent, HEADS)
    weights_all = ring(jnp.stack([weights_come, swap(weights_come, "c")]), "z")
    output_all = lax.all_gather(output_weight.T, CTX, axis=0, tiled=True)

    experts = jnp.arange(64, dtype=jnp.int32)
    chosen = jnp.any(expert_ids[:, :, None] == experts[None, None, :], axis=1)
    tokens = jnp.arange(128, dtype=jnp.int32)
    earlier = (tokens[None, :] < tokens[:, None]).astype(bf16)
    ranks = dot(earlier, chosen.astype(bf16)).astype(jnp.int32)
    ranks = jnp.where(chosen, ranks, -1).T
    quarter = jnp.eye(QUARTERS, dtype=bf16)

    table = (ranks[:, None, :] == jnp.arange(CAP, dtype=jnp.int32)[None, :, None]).astype(bf16)
    main_table = table[:, :MAIN].reshape(64 * MAIN, 128)
    rest_table = table[:, None, MAIN:, None, :] * quarter[None, :, None, :, None]
    rest_table = rest_table.reshape(64 * MAIN, QUARTERS * 128)

    cotangent_side, _ = lax.optimization_barrier((cotangent, inputs_pair))
    cotangent_side = lax.dynamic_slice(cotangent_side, (0, side * SIDE), (128, SIDE))
    grad_rows = exchange(dispatch(main_table, rest_table, cotangent_side), CTX)
    inputs_all, grad_rows, weights_all, output_all = lax.optimization_barrier(
        (inputs_all, grad_rows, weights_all, output_all)
    )
    places = jnp.concatenate([heads_below, below(z, c) // 2 * 4 + below(z, c) % 2])
    normed_low, raw, squares, weights_all, small_all, gain_rows = project(
        places.astype(jnp.int32), inputs_all, weights_all
    )
    blocks_all = small_all[:, 68:72].astype(jnp.int32).reshape(8192)
    attention_gain_all = gain_rows[0]
    mixture_gain_all = gain_rows[1]
    head_gains = small_all.reshape(64, 32, 128)[:, :16, 66:68].reshape(1024, 2).astype(f32)
    head_gains = lax.dynamic_slice(head_gains, (head * HD, 0), (HD, 2))
    query_gain_all = head_gains[:, 0]
    key_gain_all = head_gains[:, 1]

    query_raw, key_raw = raw[:, :HD], raw[:, HD : 2 * HD]
    value_low = raw[:, 2 * HD :].astype(bf16)
    squares = sum_over_rows(squares).reshape(2, 1024)
    grad_rows, squares = lax.optimization_barrier((grad_rows, squares))
    grad_other = swap(grad_rows, "ep")
    inverses = lax.rsqrt(squares / float(D) + epsilon)
    query_inverse = inverses[0][:, None]
    key_inverse = inverses[1][:, None]
    chunk = jnp.arange(8, dtype=jnp.int32)
    chunk_start = ((chunk // 2) * 16 + z * 4 + (chunk % 2) * 2 + c) * 128
    positions = (chunk_start[:, None] + tokens[None, :]).reshape(1024)
    cosine, sine = rotary_tables(positions)
    query_low = rotate(query_raw * query_inverse * query_gain_all, cosine, sine).astype(bf16)
    key_low = rotate(key_raw * key_inverse * key_gain_all, cosine, sine).astype(bf16)
    kv = lax.all_gather(
        jnp.concatenate([key_low, value_low], axis=1), TOKENS, axis=0, tiled=True
    )
    own_blocks = blocks_all.reshape(4, 4, 2, 2, 128)[:, z, :, c].reshape(1024)
    end = jnp.sum((blocks_all[:, None] <= own_blocks[None, :]).astype(jnp.int32), axis=0)[None]
    attended, lse = attend(z_place, query_low, kv, end)
    attended_low, grad_other = lax.optimization_barrier((attended.astype(bf16), grad_other))
    heads_all = lax.all_gather(attended_low, "x", axis=0, tiled=True)
    grad_other, heads_all = lax.optimization_barrier((grad_other, heads_all))
    grad_flat, hidden_pull = expert_pull(
        side_place, grad_rows, grad_other, down_weight[0]
    )

    attended_rows = exchange(attended_low, HEADS).reshape(8, 128, HD)
    attended_rows = attended_rows.transpose(1, 0, 2).reshape(128, 8 * HD)
    source = inputs.astype(f32)
    residual = source + pair_sum(dot(attended_rows, output_all, ((1,), (1,))))
    mixture_inverse = lax.rsqrt(jnp.mean(residual * residual, axis=-1, keepdims=True) + epsilon)
    mixed_low = (residual * mixture_inverse * mixture_gain_all).astype(bf16)
    mixed_rows = exchange(dispatch(main_table, rest_table, mixed_low), CTX)

    entry_sent, entry, hidden_low, gate_raw_grad, up_raw_grad, logit_grad = expert_step(
        place.reshape(1).astype(jnp.int32),
        mixed_rows,
        hidden_pull,
        gate_weight[0],
        up_weight[0],
        small_all,
    )
    entry_back = exchange(entry_sent, CTX)
    result_sent = expert_result(hidden_low, down_weight[0])
    down_weight_grad = dot(hidden_low, grad_flat, ((0,), (0,)))
    gate_weight_grad = dot(entry, gate_raw_grad, ((0,), (0,)))
    up_weight_grad = dot(entry, up_raw_grad, ((0,), (0,)))
    router_part = dot(entry, logit_grad, ((0,), (0,)))
    entry_back, down_weight_grad, gate_weight_grad, up_weight_grad, router_part = (
        lax.optimization_barrier(
            (entry_back, down_weight_grad, gate_weight_grad, up_weight_grad, router_part)
        )
    )

    mixed_grad = pair_sum(collect(main_table, rest_table, entry_back))

    grad_out = cotangent.astype(f32)
    scaled = mixed_grad * mixture_gain_all
    residual_grad = (
        grad_out
        + mixture_inverse * scaled
        - residual
        * mixture_inverse
        * mixture_inverse
        * mixture_inverse
        * jnp.mean(scaled * residual, axis=-1, keepdims=True)
    )
    mixture_gain_part = jnp.sum(mixed_grad * residual * mixture_inverse, axis=0)
    residual_low = residual_grad.astype(bf16)
    attended_grad = dot(residual_low, output_all).astype(bf16)
    attended_grad = attended_grad.reshape(128, 8, HD).transpose(1, 0, 2)
    residual_bands = residual_low.reshape(128, 4, 1, BAND).transpose(1, 2, 0, 3)
    residual_bands = jnp.broadcast_to(residual_bands, (4, 2, 128, BAND)).reshape(8, 128, BAND)
    attended_grad = exchange(
        jnp.concatenate([attended_grad, residual_bands], axis=2).reshape(1024, HD + BAND), HEADS
    )
    residual_band = attended_grad[:, HD:]
    attended_grad = attended_grad[:, :HD]
    result_sent, attended_grad = lax.optimization_barrier((result_sent, attended_grad))
    result_back = exchange(result_sent, CTX)
    output_part = dot(
        residual_band,
        heads_all.reshape(4, 1024, HD).transpose(1, 0, 2).reshape(1024, 4 * HD),
        ((0,), (0,)),
    )

    delta = jnp.sum(attended_grad.astype(f32) * attended, axis=-1)[None]
    query_grad, kv_part = attend_back(
        z_place, query_low, attended_grad, kv, end, lse, delta
    )
    kv_grad = lax.psum_scatter(kv_part, TOKENS, scatter_dimension=0, tiled=True)
    query_grad, result_back = lax.optimization_barrier((query_grad, result_back))
    query_grad = linger(query_grad)
    kv_grad = kv_grad.astype(f32)
    final = residual + pair_sum(collect(main_table, rest_table, result_back))
    value_grad_low = kv_grad[:, HD:].astype(bf16)
    query_normed_grad = rotate(query_grad, cosine, -sine)
    key_normed_grad = rotate(kv_grad[:, :HD], cosine, -sine)
    query_scaled = query_normed_grad * query_gain_all
    key_scaled = key_normed_grad * key_gain_all
    dots = jnp.stack(
        [jnp.sum(query_scaled * query_raw, axis=-1), jnp.sum(key_scaled * key_raw, axis=-1)]
    )
    dots = sum_over_rows(dots.reshape(16, 128)).reshape(2, 1024)[:, :, None] / float(D)

    def raw_back(value, inverse, scaled_grad, mean):
        return (inverse * scaled_grad - value * inverse * inverse * inverse * mean).astype(bf16)

    query_raw_low = raw_back(query_raw, query_inverse, query_scaled, dots[0])
    key_raw_low = raw_back(key_raw, key_inverse, key_scaled, dots[1])
    query_gain_part = jnp.sum(query_normed_grad * query_raw * query_inverse, axis=0)
    key_gain_part = jnp.sum(key_normed_grad * key_raw * key_inverse, axis=0)
    raw_grads = jnp.concatenate([query_raw_low, key_raw_low, value_grad_low], axis=1)

    def head_part(value):
        wide = lax.dynamic_update_slice(jnp.zeros((8 * HD,), f32), value, (head * HD,))
        return jnp.pad(wide.reshape(64, 16), ((0, 0), (0, 16))).reshape(1, D)

    extra = jnp.concatenate(
        [
            jnp.zeros((1, D), f32),
            mixture_gain_part[None],
            head_part(query_gain_part),
            head_part(key_gain_part),
            jnp.zeros((4, D), f32),
        ],
        axis=0,
    )
    normed_part, shares = spread_grads(
        raw_grads, normed_low, weights_all, router_part, gain_rows, extra, output_part
    )
    normed_grad = jnp.sum(exchange(normed_part, HEADS).reshape(8, 128, D).astype(f32), axis=0)
    normed_grad = pair_sum(normed_grad)

    summed = lax.psum_scatter(shares, TOKENS, scatter_dimension=0, tiled=True)
    output_sum = jnp.broadcast_to(summed[256:].reshape(1, 2, 32, 512), (4, 2, 32, 512))
    shares = jnp.concatenate(
        [summed[:256].reshape(8, 32, 512), output_sum.reshape(8, 32, 512)], axis=1
    )
    shares = exchange(shares.reshape(512, 512), HEADS).reshape(8, 64, 512).astype(f32)
    weight_grad = shares[:, :32, : 3 * HD].reshape(8, 32, 3, HD)
    weight_grad = weight_grad.transpose(2, 1, 0, 3).reshape(3, 32, 8 * HD)
    extra = jnp.sum(shares[:, :32, 3 * HD :], axis=0)
    pair = extra + lax.ppermute(extra, "ep", [(0, 1), (1, 0)])
    router_grad = pair[:, :64]
    attention_gain_grad = pair[:, 64]
    output_grad = lax.dynamic_slice(shares, (x * 2, 32, 0), (2, 32, 512))
    output_grad = output_grad.reshape(2, 32, 4, HD).transpose(2, 0, 3, 1).reshape(8 * HD, 32)

    inverse = lax.rsqrt(jnp.mean(source * source, axis=-1, keepdims=True) + epsilon)
    scaled = normed_grad * attention_gain_all
    input_grad = (
        residual_grad
        + inverse * scaled
        - source
        * inverse
        * inverse
        * inverse
        * jnp.mean(scaled * source, axis=-1, keepdims=True)
    )
    return (
        final,
        input_grad,
        attention_gain_grad,
        weight_grad[0],
        weight_grad[1],
        weight_grad[2],
        extra[:16, 66],
        extra[:16, 67],
        output_grad,
        extra[:, 65],
        router_grad,
        gate_weight_grad[None],
        up_weight_grad[None],
        down_weight_grad[None],
    )


def solution(mesh):
    inner = Mesh(mesh.devices.reshape(4, 4, 2, 2, 2), ("x", "z", "yh", "c", "ep"))
    in_specs = (
        P(CTX, None),
        P(CTX),
        P(CTX, None),
        P(CTX),
        P(CTX, "ep"),
        P(CTX, "ep"),
        P(CTX, "ep"),
        P(("ep",) + CTX),
        P(("ep",) + CTX),
        P("ep", CTX),
        P(CTX),
        P(CTX, None),
        P(CTX, None, "ep"),
        P(CTX, None, "ep"),
        P(CTX, "ep", None),
        P(CTX, None),
    )
    out_specs = (
        P(CTX, None),
        P(CTX, None),
        P(CTX),
        P(CTX, "ep"),
        P(CTX, "ep"),
        P(CTX, "ep"),
        P(("ep",) + CTX),
        P(("ep",) + CTX),
        P("ep", CTX),
        P(CTX),
        P(CTX, None),
        P(CTX, None, "ep"),
        P(CTX, None, "ep"),
        P(CTX, "ep", None),
    )
    return jax.shard_map(local, mesh=inner, in_specs=in_specs, out_specs=out_specs, check_vma=False)
```

```python
import functools

import jax
import jax.numpy as jnp
from jax import lax
from jax.experimental import pallas as pl
from jax.experimental.pallas import tpu as pltpu
from jax.sharding import Mesh
from jax.sharding import PartitionSpec as P

D = 2048
H = 16
HD = 128
TOPK = 8
CAP = 20
MAIN = 16
REST = CAP - MAIN
QUARTERS = 4
BAND = D // QUARTERS
WINDOW = 512
HALF_MAIN = 32 * MAIN
HALF_REST = 32 * REST
HALF = HALF_MAIN + HALF_REST
ROW_WIDTH = D + BAND
SIDE = D // 2
SIDE_BAND = SIDE // QUARTERS
SIDE_WIDTH = SIDE + SIDE_BAND

epsilon = 1e-05
rotary_base = 10000.0
masked_score = -1e30
scale = HD ** (-0.5)
log2e = 1.4426950408889634
bf16 = jnp.bfloat16
f32 = jnp.float32

CTX = ("x", "z", "yh", "c")
HEADS = ("x", "yh")
TOKENS = ("z", "c")
ROWS = ("x", "yh", "ep")


def dot(first, second, dims=((1,), (0,))):
    return lax.dot_general(first, second, (dims, ((), ())), preferred_element_type=f32)


def exchange(value, axes):
    return lax.all_to_all(value, axes, split_axis=0, concat_axis=0, tiled=True)


OFFSETS = [(i, j) for i in range(4) for j in range(2)]


def ahead(value, axis, steps):
    return lax.ppermute(value, axis, [(a, (a + steps) % 4) for a in range(4)])


def ring(value, axis):
    half = value.shape[0] // 2
    behind = ahead(value, axis, 1)
    front = ahead(value, axis, 3)
    far = [ahead(behind[:half], axis, 1), ahead(front[half:], axis, 3)]
    return [[value], [behind], far, [front]]


def swap(value, axis):
    return lax.ppermute(value, axis, [(0, 1), (1, 0)])


def below(a, b):
    return jnp.stack([(a - i) % 4 * 2 + (b - j) % 2 for i, j in OFFSETS])


def pair_sum(value):
    own = lax.optimization_barrier(value.astype(bf16))
    other = lax.ppermute(own, "ep", [(0, 1), (1, 0)])
    return own.astype(f32) + other.astype(f32)


def sum_over_rows(value):
    rows = value.shape[0]
    sent = jnp.broadcast_to(value[None], (16, rows, 128)).reshape(16 * rows, 128)
    return jnp.sum(exchange(sent, ROWS).reshape(16, rows, 128), axis=0)


def rotary_tables(positions):
    half = HD // 2
    frequency = rotary_base ** (-jnp.arange(half).astype(f32) / half)
    angles = positions.astype(f32)[:, None] * frequency[None, :]
    return (jnp.cos(angles), jnp.sin(angles))


def rotate(value, cosine, sine):
    half = HD // 2
    first = value[:, :half]
    second = value[:, half:]
    return jnp.concatenate(
        [first * cosine - second * sine, second * cosine + first * sine], axis=-1
    )


def window_rows(index):
    return pl.multiple_of((index % 4) * 2048 + (index // 4) * 256, 256)


def window_mask(index, end):
    row = lax.broadcasted_iota(jnp.int32, (WINDOW, 1), 0)
    place = (row & 127) + ((row >> 7) & 1) * 256 + (row >> 8) * 128 + index * WINDOW
    return place < end


def project_kernel(place_ref, *refs):
    refs = list(refs)
    inputs = [[refs.pop(0) for _ in range(2 if i == 2 else 1)] for i, _ in OFFSETS]
    weights = [[refs.pop(0) for _ in range(2 if i == 2 else 1)] for i in range(4)]
    cosine_ref, sine_ref, normed_ref, raw_ref, query_ref, kv_ref = refs[:6]
    square_ref, weight_ref, small_ref, gain_ref = refs[6:]
    for n, (i, j) in enumerate(OFFSETS):
        piece = weights[2][j].at[0] if i == 2 else weights[i][0].at[j]
        for m in range(8):
            row = (place_ref[8 + n] + (m // 2) * 16 + (m % 2) * 2) * 32
            here = pl.ds(pl.multiple_of(row, 32), 32)
            weight_ref[here, :] = piece[m * 32 : m * 32 + 32, : 3 * HD]
            small_ref[here, :] = piece[m * 32 : m * 32 + 32, 3 * HD :]
    row = lax.broadcasted_iota(jnp.int32, (8, 128), 0)
    column = lax.broadcasted_iota(jnp.int32, (8, 128), 1)
    pick = jnp.where(column == row + 64, 1.0, 0.0).astype(bf16)
    gain_ref[...] = dot(pick, small_ref[...], ((1,), (1,)))
    gain = gain_ref[0:1, :]
    head_gains = jnp.concatenate(
        [
            small_ref[pl.ds(pl.multiple_of((place_ref[16] * 8 + m) * 32, 32), 16), :]
            for m in range(8)
        ],
        axis=0,
    )
    head_gains = head_gains.astype(f32).T
    for n in range(8):
        value = jnp.concatenate([part[...] for part in inputs[n]], axis=0).astype(f32)
        inverse = lax.rsqrt(jnp.mean(value * value, axis=-1, keepdims=True) + epsilon)
        normed = (value * inverse * gain).astype(bf16)
        chunk = place_ref[n]
        here = pl.ds(pl.multiple_of(chunk * 128, 128), 128)
        normed_ref[here, :] = normed
        raw = dot(normed, weight_ref[...])
        raw_ref[here, :] = raw[:, : 2 * HD]
        for part in range(2):
            own = raw[:, part * HD : part * HD + HD]
            square = jnp.sum(own * own, axis=-1, keepdims=True)
            square = jnp.broadcast_to(square, (128, 128)).T
            square_ref[pl.ds(chunk + 8 * part, 1), :] = square[0:1]
            own = own * head_gains[66 + part : 67 + part]
            own = own * cosine_ref[here, :] + pltpu.roll(own, HD // 2, 1) * sine_ref[here, :]
            if part == 0:
                query_ref[here, :] = own.astype(bf16)
            else:
                kv_ref[here, :HD] = own.astype(bf16)
        kv_ref[here, HD:] = raw[:, 2 * HD :].astype(bf16)


def back_kernel(raw_ref, normed_ref, weight_ref, gain_ref, back_ref, total_ref):
    total = jnp.zeros((1, D), f32)
    for n in range(4):
        here = slice(n * 256, n * 256 + 256)
        part = dot(raw_ref[here, :], weight_ref[...], ((1,), (1,)))
        total = total + jnp.sum(part * normed_ref[here, :].astype(f32), axis=0, keepdims=True)
        back_ref[here, :] = part.astype(bf16)
    total_ref[...] = total / gain_ref[0:1, :]


def share_kernel(raw_ref, normed_ref, router_ref, extra_ref, total_ref, output_ref, share_ref):
    row = lax.broadcasted_iota(jnp.int32, (8, 1), 0)
    extra = extra_ref[...] + jnp.where(row == 0, total_ref[...], 0.0)
    for n in range(4):
        band = slice(n * 512, n * 512 + 512)
        part = dot(normed_ref[:, band], raw_ref[...], ((0,), (0,))).astype(bf16)
        side = jnp.concatenate(
            [jnp.zeros((64, 512), f32), extra[:, band], jnp.zeros((56, 512), f32)], axis=0
        )
        side = (side.T + router_ref[band, :]).astype(bf16)
        for m in range(16):
            z, yh, c = m // 4, m // 2 % 2, m % 2
            start = (z * 2 + c) * 320
            there = slice(start + (n * 2 + yh) * 32, start + (n * 2 + yh) * 32 + 32)
            share_ref[there, : 3 * HD] = part[m * 32 : m * 32 + 32]
            share_ref[there, 3 * HD :] = side[m * 32 : m * 32 + 32]
            if n == 0:
                there = slice(start + 256 + yh * 32, start + 288 + yh * 32)
                share_ref[there, :] = output_ref[m * 32 : m * 32 + 32, :].astype(bf16)


def finish_kernel(place_ref, share_ref, query_ref, key_ref, value_ref, output_ref, extra_ref):
    total = None
    for n in range(8):
        rows = share_ref[n * 64 : n * 64 + 32, :].astype(f32)
        for part, ref in enumerate((query_ref, key_ref, value_ref)):
            ref[:, n * HD : n * HD + HD] = rows[:, part * HD : part * HD + HD]
        total = rows[:, 3 * HD :] if n == 0 else total + rows[:, 3 * HD :]
    extra_ref[...] = total
    for yh in range(2):
        start = pl.multiple_of((place_ref[0] * 2 + yh) * 64 + 32, 32)
        rows = share_ref[pl.ds(start, 32), :].astype(f32)
        rows = jnp.concatenate([rows, jnp.zeros((96, 512), f32)], axis=0).T
        for m in range(4):
            there = (m * 2 + yh) * HD
            output_ref[there : there + HD, :] = rows[m * HD : m * HD + HD, :32]


def attend_kernel(
    z_ref, q_ref, factor_ref, raw_ref, inverse_ref, end_ref, out_ref, lse_ref, kv_ref
):
    z = z_ref[0]
    for n in range(64):
        here = slice(n * 128, n * 128 + 128)
        inverse = inverse_ref[n // 8 : n // 8 + 1, n % 8 * 128 : n % 8 * 128 + 128]
        inverse = jnp.broadcast_to(inverse, (128, 128)).T
        kv_ref[here, :HD] = (raw_ref[here, :HD].astype(f32) * inverse).astype(bf16)
        kv_ref[here, HD:] = raw_ref[here, HD:]
    for x in range(4):
        span = slice(x * 256, (x + 1) * 256)
        queries = q_ref[span, :]
        end = end_ref[:, span]
        factor = factor_ref[:, span]

        def tile(index, state, masked):
            peak, mass, total = state
            base = window_rows(index)
            part = jnp.concatenate(
                [kv_ref[pl.ds(base, 256), :], kv_ref[pl.ds(base + 1024, 256), :]], axis=0
            )
            keys, values = part[:, :HD], part[:, HD:]
            scores = dot(keys, queries, ((1,), (1,)))
            if masked:
                scores = jnp.where(window_mask(index, end), scores, masked_score)
            new_peak = jnp.maximum(peak, jnp.max(scores, axis=0, keepdims=True))
            weights = jnp.exp2((scores - new_peak) * factor)
            shrink = jnp.exp2((peak - new_peak) * factor)
            mass = mass * shrink + jnp.sum(weights, axis=0, keepdims=True)
            total = total * shrink + dot(values, weights.astype(bf16), ((0,), (0,)))
            return (new_peak, mass, total)

        state = (
            jnp.full((1, 256), masked_score, f32),
            jnp.zeros((1, 256), f32),
            jnp.zeros((HD, 256), f32),
        )
        last = 4 * x + z
        state = lax.fori_loop(0, last, lambda i, s: tile(i, s, False), state)
        state = lax.fori_loop(
            last, jnp.minimum(last + 2, 16), lambda i, s: tile(i, s, True), state
        )
        peak, mass, total = state
        out_ref[span, :] = (total / mass).T
        lse_ref[:, span] = peak * factor + jnp.log(mass) * log2e


def attend_back_kernel(
    z_ref,
    raw_ref,
    factor_ref,
    q_ref,
    grad_ref,
    kv_ref,
    end_ref,
    lse_ref,
    delta_ref,
    dq_ref,
    dkv_ref,
    sums,
):
    z = z_ref[0]
    sums[...] = jnp.zeros_like(sums)
    for x in range(4):
        span = slice(x * 256, (x + 1) * 256)
        raw = raw_ref[span, :]
        factor = factor_ref[:, span]
        queries = q_ref[span, :]
        grads = grad_ref[span, :]
        end = end_ref[:, span]
        lse = lse_ref[:, span]
        delta = delta_ref[:, span]

        def tile(index, total, masked):
            base = window_rows(index)
            part = jnp.concatenate(
                [kv_ref[pl.ds(base, 256), :], kv_ref[pl.ds(base + 1024, 256), :]], axis=0
            )
            keys, values = part[:, :HD], part[:, HD:]
            scores = dot(keys, raw, ((1,), (1,))) * factor - lse
            if masked:
                scores = jnp.where(window_mask(index, end), scores, masked_score)
            chances = jnp.exp2(scores)
            value_dot = dot(values, grads, ((1,), (1,)))
            score_grad = (chances * (value_dot - delta)).astype(bf16)
            key_term = dot(score_grad, queries)
            value_term = dot(chances.astype(bf16), grads)
            sums[pl.ds(base, 256), :HD] += key_term[:256]
            sums[pl.ds(base + 1024, 256), :HD] += key_term[256:]
            sums[pl.ds(base, 256), HD:] += value_term[:256]
            sums[pl.ds(base + 1024, 256), HD:] += value_term[256:]
            return total + dot(keys, score_grad, ((0,), (0,)))

        total = jnp.zeros((HD, 256), f32)
        last = 4 * x + z
        total = lax.fori_loop(0, last, lambda i, s: tile(i, s, False), total)
        total = lax.fori_loop(
            last, jnp.minimum(last + 2, 16), lambda i, s: tile(i, s, True), total
        )
        dq_ref[span, :] = total.T * scale
    dkv_ref[:, :HD] = (sums[:, :HD] * scale).astype(bf16)
    dkv_ref[:, HD:] = sums[:, HD:].astype(bf16)


def rest_pick(quarter):
    row = lax.broadcasted_iota(jnp.int32, (HALF_REST, HALF_MAIN), 0)
    column = lax.broadcasted_iota(jnp.int32, (HALF_REST, HALF_MAIN), 1)
    same = (column >> 4 == row >> 2) & (column & 3 == row & 3)
    return jnp.where(same & ((column >> 2) & 3 == quarter), 1.0, 0.0).astype(bf16)


def open_rest(rows):
    rest = rows[:, D:]
    return jnp.concatenate(
        [dot(rest_pick(q), rest).astype(bf16) for q in range(QUARTERS)], axis=1
    )


def open_side(rows_ref):
    rest = rows_ref[:, SIDE:]
    rest = jnp.concatenate(
        [dot(rest_pick(q), rest).astype(bf16) for q in range(QUARTERS)], axis=1
    )
    return rows_ref[:, :SIDE], rest


def pull_kernel(side_ref, own_ref, other_ref, down_ref, flat_ref, pull_ref):
    own = pl.multiple_of(side_ref[0] * SIDE, SIDE)
    other = pl.multiple_of(SIDE - side_ref[0] * SIDE, SIDE)
    for ref, start in ((own_ref, own), (other_ref, other)):
        main, rest = open_side(ref)
        flat_ref[:HALF_MAIN, pl.ds(start, SIDE)] = main
        flat_ref[HALF_MAIN:, pl.ds(start, SIDE)] = rest
    pull_ref[...] = dot(flat_ref[...], down_ref[...], ((1,), (1,)))


def expert_kernel(
    place_ref,
    rows_ref,
    pull_ref,
    gate_ref,
    up_ref,
    router_ref,
    back_ref,
    flat_ref,
    hidden_ref,
    gate_grad_ref,
    up_grad_ref,
    logit_grad_ref,
):
    flat_ref[:HALF_MAIN] = rows_ref[:, :D]
    flat_ref[HALF_MAIN:] = open_rest(rows_ref)
    entry = flat_ref[...]
    lane = lax.broadcasted_iota(jnp.int32, (1, 128), 1)
    logits = jnp.where(lane < 64, dot(entry, router_ref[...]), masked_score)
    shifted = jnp.exp(logits - jnp.max(logits, axis=-1, keepdims=True))
    probability = shifted / jnp.sum(shifted, axis=-1, keepdims=True)
    own = jnp.where(lane == place_ref[0], 1.0, 0.0)
    gates = jnp.sum(probability * own, axis=-1, keepdims=True)
    gate = dot(entry, gate_ref[...])
    upward = dot(entry, up_ref[...])
    pull = pull_ref[...]
    sigma = 1.0 / (1.0 + jnp.exp(-gate))
    swish = gate * sigma
    hidden = swish * upward
    row_grad = jnp.sum(hidden * pull, axis=-1, keepdims=True) * gates
    hidden_ref[...] = (hidden * gates).astype(bf16)
    hidden_grad = pull * gates
    gate_grad = (hidden_grad * upward * (sigma + swish * (1.0 - sigma))).astype(bf16)
    up_grad = (hidden_grad * swish).astype(bf16)
    logit_grad = (row_grad * (own - probability)).astype(bf16)
    gate_grad_ref[...] = gate_grad
    up_grad_ref[...] = up_grad
    logit_grad_ref[...] = logit_grad
    rest = []
    for q in range(QUARTERS):
        band = slice(q * BAND, (q + 1) * BAND)
        part = (
            dot(gate_grad, gate_ref[band, :], ((1,), (1,)))
            + dot(up_grad, up_ref[band, :], ((1,), (1,)))
            + dot(logit_grad, router_ref[band, :], ((1,), (1,)))
        ).astype(bf16)
        back_ref[:, band] = part[:HALF_MAIN]
        rest.append(dot(rest_pick(q), part[HALF_MAIN:], ((0,), (0,))))
    back_ref[:, D:] = (rest[0] + rest[1] + rest[2] + rest[3]).astype(bf16)


def result_kernel(hidden_ref, down_ref, back_ref):
    rest = []
    for q in range(QUARTERS):
        band = slice(q * BAND, (q + 1) * BAND)
        part = dot(hidden_ref[...], down_ref[:, band]).astype(bf16)
        back_ref[:, band] = part[:HALF_MAIN]
        rest.append(dot(rest_pick(q), part[HALF_MAIN:], ((0,), (0,))))
    back_ref[:, D:] = (rest[0] + rest[1] + rest[2] + rest[3]).astype(bf16)


SMEM = pl.BlockSpec(memory_space=pltpu.SMEM)
VMEM = pl.BlockSpec(memory_space=pltpu.VMEM)
params = pltpu.CompilerParams(vmem_limit_bytes=56 * 1024 * 1024)
step_params = pltpu.CompilerParams(
    vmem_limit_bytes=56 * 1024 * 1024, dimension_semantics=("arbitrary",)
)


cheap = pl.CostEstimate(flops=1, bytes_accessed=1, transcendentals=0)
dear = pl.CostEstimate(flops=200_000_000_000, bytes_accessed=1, transcendentals=0)


def step_block(rows, columns):
    return pl.BlockSpec((rows, columns), lambda i: (i, 0))


def whole_block(rows, columns):
    return pl.BlockSpec((rows, columns), lambda i: (0, 0))


def shape(rows, columns, kind=bf16):
    return jax.ShapeDtypeStruct((rows, columns), kind)


def project(places, inputs, weights, cosine, sine):
    return pl.pallas_call(
        project_kernel,
        out_shape=(
            shape(1024, D),
            shape(1024, 2 * HD, f32),
            shape(1024, HD),
            shape(1024, 2 * HD),
            shape(16, 128, f32),
            shape(D, 3 * HD),
            shape(D, 128),
            shape(8, D, f32),
        ),
        in_specs=[SMEM] + [VMEM] * (len(inputs) + len(weights) + 2),
        out_specs=(VMEM,) * 8,
        compiler_params=params,
        cost_estimate=pl.CostEstimate(
            flops=50_000_000_000, bytes_accessed=1, transcendentals=0
        ),
    )(places, *inputs, *weights, cosine, sine)


def back_grads(raw_grads, normed, weights, gains):
    return pl.pallas_call(
        back_kernel,
        out_shape=(shape(1024, D), shape(1, D, f32)),
        in_specs=[VMEM] * 4,
        out_specs=(VMEM, VMEM),
        compiler_params=params,
        cost_estimate=cheap,
    )(raw_grads, normed, weights, gains)


def share_grads(*values):
    return pl.pallas_call(
        share_kernel,
        out_shape=shape(2560, 512),
        in_specs=[VMEM] * 6,
        out_specs=VMEM,
        compiler_params=params,
        cost_estimate=dear,
    )(*values)


def finish(place, shares):
    return pl.pallas_call(
        finish_kernel,
        out_shape=(
            shape(32, 8 * HD, f32),
            shape(32, 8 * HD, f32),
            shape(32, 8 * HD, f32),
            shape(8 * HD, 32, f32),
            shape(32, 128, f32),
        ),
        in_specs=[SMEM, VMEM],
        out_specs=(VMEM,) * 5,
        compiler_params=params,
        cost_estimate=dear,
    )(place, shares)


def expert_pull(side, own, other, down):
    return pl.pallas_call(
        pull_kernel,
        grid=(2,),
        out_shape=(shape(1280, D), shape(1280, 512, f32)),
        in_specs=[
            SMEM,
            step_block(HALF_MAIN, SIDE_WIDTH),
            step_block(HALF_MAIN, SIDE_WIDTH),
            whole_block(512, D),
        ],
        out_specs=(step_block(HALF, D), step_block(HALF, 512)),
        compiler_params=step_params,
        cost_estimate=cheap,
    )(side, own, other, down)


def expert_step(place, rows, pull, gate, up, router):
    return pl.pallas_call(
        expert_kernel,
        grid=(2,),
        out_shape=(
            shape(1024, ROW_WIDTH),
            shape(1280, D),
            shape(1280, 512),
            shape(1280, 512),
            shape(1280, 512),
            shape(1280, 128),
        ),
        in_specs=[
            SMEM,
            step_block(HALF_MAIN, ROW_WIDTH),
            step_block(HALF, 512),
            whole_block(D, 512),
            whole_block(D, 512),
            whole_block(D, 128),
        ],
        out_specs=(
            step_block(HALF_MAIN, ROW_WIDTH),
            step_block(HALF, D),
            step_block(HALF, 512),
            step_block(HALF, 512),
            step_block(HALF, 512),
            step_block(HALF, 128),
        ),
        compiler_params=step_params,
        cost_estimate=cheap,
    )(place, rows, pull, gate, up, router)


def expert_result(hidden, down):
    return pl.pallas_call(
        result_kernel,
        grid=(2,),
        out_shape=shape(1024, ROW_WIDTH),
        in_specs=[step_block(HALF, 512), whole_block(512, D)],
        out_specs=step_block(HALF_MAIN, ROW_WIDTH),
        compiler_params=step_params,
        cost_estimate=cheap,
    )(hidden, down)


def linger_kernel(value_ref, out_ref):
    out_ref[...] = value_ref[...]


def linger(value):
    return pl.pallas_call(
        linger_kernel,
        out_shape=jax.ShapeDtypeStruct(value.shape, value.dtype),
        in_specs=[VMEM],
        out_specs=VMEM,
        cost_estimate=dear,
    )(value)


def attend(z, queries, factor, kv, inverses, end):
    return pl.pallas_call(
        attend_kernel,
        out_shape=(shape(1024, HD, f32), shape(1, 1024, f32), shape(8192, 2 * HD)),
        in_specs=[SMEM] + [VMEM] * 5,
        out_specs=(VMEM,) * 3,
        compiler_params=params,
        cost_estimate=cheap,
    )(z, queries, factor, kv, inverses, end)


def attend_back(z, raw, factor, queries, grads, kv, end, lse, delta):
    return pl.pallas_call(
        attend_back_kernel,
        out_shape=(
            shape(1024, HD, f32),
            shape(8192, 2 * HD),
        ),
        in_specs=[SMEM] + [VMEM] * 8,
        out_specs=(VMEM,) * 2,
        scratch_shapes=[pltpu.VMEM((8192, 2 * HD), f32)],
        compiler_params=params,
        cost_estimate=cheap,
    )(z, raw, factor, queries, grads, kv, end, lse, delta)


def dispatch(main_table, rest_table, value):
    band = value.shape[1] // QUARTERS
    stacked = value.reshape(128, QUARTERS, band).transpose(1, 0, 2).reshape(QUARTERS * 128, band)
    main = dot(main_table, value).astype(bf16)
    rest = dot(rest_table, stacked).astype(bf16)
    return jnp.concatenate([main, rest], axis=1)


def collect(main_table, rest_table, rows):
    width = rows.shape[1] * QUARTERS // (QUARTERS + 1)
    main = dot(main_table, rows[:, :width], ((0,), (0,)))
    rest = dot(rest_table, rows[:, width:], ((0,), (0,)))
    rest = rest.reshape(QUARTERS, 128, width // QUARTERS).transpose(1, 0, 2)
    return main + rest.reshape(128, width)


def local(
    inputs,
    blocks,
    expert_ids,
    attention_gain,
    query_weight,
    key_weight,
    value_weight,
    query_gain,
    key_gain,
    output_weight,
    mixture_gain,
    router_weight,
    gate_weight,
    up_weight,
    down_weight,
    cotangent,
):
    x = lax.axis_index("x")
    z = lax.axis_index("z")
    yh = lax.axis_index("yh")
    c = lax.axis_index("c")
    place = x * 16 + z * 4 + yh * 2 + c
    head = x * 2 + yh
    z_place = z.reshape(1).astype(jnp.int32)
    side = lax.axis_index("ep")
    side_place = side.reshape(1).astype(jnp.int32)
    heads_below = below(x, yh)

    pad = lambda gain: jnp.pad(gain, (0, 16))[:, None]
    small = jnp.concatenate(
        [
            router_weight,
            attention_gain[:, None],
            mixture_gain[:, None],
            pad(query_gain),
            pad(key_gain),
            blocks.astype(bf16).reshape(32, 4),
            jnp.zeros((32, 56), bf16),
        ],
        axis=1,
    )
    weights_sent = jnp.concatenate(
        [w.reshape(32, 8, HD) for w in (query_weight, key_weight, value_weight)]
        + [jnp.broadcast_to(small[:, None], (32, 8, 128))],
        axis=2,
    )
    weights_sent = weights_sent.transpose(1, 0, 2).reshape(256, 4 * HD)
    inputs_pair = swap(inputs, "yh")
    inputs_all = [ring(inputs, "x"), ring(inputs_pair, "x")]
    inputs_all = [part for i, j in OFFSETS for part in inputs_all[j][i]]
    weights_come = exchange(weights_sent, HEADS)
    weights_all = ring(jnp.stack([weights_come, swap(weights_come, "c")]), "z")
    weights_all = [part for parts in weights_all for part in parts]
    output_all = lax.all_gather(output_weight.T, CTX, axis=0, tiled=True)

    experts = jnp.arange(64, dtype=jnp.int32)
    chosen = jnp.any(expert_ids[:, :, None] == experts[None, None, :], axis=1)
    tokens = jnp.arange(128, dtype=jnp.int32)
    earlier = (tokens[None, :] < tokens[:, None]).astype(bf16)
    ranks = dot(earlier, chosen.astype(bf16)).astype(jnp.int32)
    ranks = jnp.where(chosen, ranks, -1).T
    quarter = jnp.eye(QUARTERS, dtype=bf16)

    table = (ranks[:, None, :] == jnp.arange(CAP, dtype=jnp.int32)[None, :, None]).astype(bf16)
    main_table = table[:, :MAIN].reshape(64 * MAIN, 128)
    rest_table = table[:, None, MAIN:, None, :] * quarter[None, :, None, :, None]
    rest_table = rest_table.reshape(64 * MAIN, QUARTERS * 128)

    cotangent_side = lax.dynamic_slice(cotangent, (0, side * SIDE), (128, SIDE))
    grad_sent = dispatch(main_table, rest_table, cotangent_side)
    inputs_all, weights_all, grad_sent = lax.optimization_barrier(
        (inputs_all, weights_all, grad_sent)
    )
    grad_rows = exchange(grad_sent, CTX)
    chunk = jnp.arange(8, dtype=jnp.int32)
    chunk_start = ((chunk // 2) * 16 + z * 4 + (chunk % 2) * 2 + c) * 128
    positions = (chunk_start[:, None] + tokens[None, :]).reshape(1024)
    cosine, sine = rotary_tables(positions)
    places = jnp.concatenate(
        [heads_below, below(z, c) // 2 * 4 + below(z, c) % 2, head.reshape(1)]
    )
    normed_low, raw, query_some, kv_some, squares, weights_all, small_all, gain_rows = project(
        places.astype(jnp.int32),
        inputs_all,
        weights_all,
        jnp.concatenate([cosine, cosine], axis=1),
        jnp.concatenate([-sine, sine], axis=1),
    )
    blocks_all = small_all[:, 68:72].astype(jnp.int32).reshape(8192)
    attention_gain_all = gain_rows[0]
    mixture_gain_all = gain_rows[1]
    head_gains = small_all.reshape(64, 32, 128)[:, :16, 66:68].reshape(1024, 2).astype(f32)
    head_gains = lax.dynamic_slice(head_gains, (head * HD, 0), (HD, 2))
    query_gain_all = head_gains[:, 0]
    key_gain_all = head_gains[:, 1]
    query_raw, key_raw = raw[:, :HD], raw[:, HD:]

    kv_some, output_all = lax.optimization_barrier((kv_some, output_all))
    kv_some = lax.all_gather(kv_some, TOKENS, axis=0, tiled=True)
    grad_rows, squares = lax.optimization_barrier((grad_rows, squares))
    squares = sum_over_rows(squares)
    grad_rows, squares = lax.optimization_barrier((grad_rows, squares))
    grad_other = swap(grad_rows, "ep")
    group_inverse = lax.rsqrt(squares / float(D) + epsilon)
    inverses = group_inverse[8:]
    inverses = ring(jnp.stack([inverses, swap(inverses, "c")]), "z")
    inverses = jnp.concatenate([part for parts in inverses for part in parts])
    inverses = jnp.take(inverses, below(z, c), axis=0).reshape(8, 1024)
    group_inverse = group_inverse.reshape(2, 1024)
    query_inverse = group_inverse[0][:, None]
    key_inverse = group_inverse[1][:, None]
    query_factor = group_inverse[0:1] * (scale * log2e)
    query_low = (query_some.astype(f32) * query_inverse).astype(bf16)
    own_blocks = blocks_all.reshape(4, 4, 2, 2, 128)[:, z, :, c].reshape(1024)
    end = jnp.sum((blocks_all[:, None] <= own_blocks[None, :]).astype(jnp.int32), axis=0)[None]
    kv_some, end, query_low = lax.optimization_barrier((kv_some, end, query_low))
    attended, lse, kv = attend(
        z_place, query_some, query_factor, kv_some, inverses, end
    )
    attended_low = attended.astype(bf16)

    heads_all = [part for parts in ring(attended_low, "x") for part in parts]
    attended_rows, heads_all, grad_other = lax.optimization_barrier(
        (exchange(attended_low, HEADS).reshape(8, 128, HD), heads_all, grad_other)
    )
    heads_all = jnp.concatenate(heads_all, axis=0).reshape(4, 1024, HD)
    heads_all = jnp.take(heads_all, (x - jnp.arange(4)) % 4, axis=0)
    heads_all = heads_all.transpose(1, 0, 2).reshape(1024, 4 * HD)
    attended_rows = attended_rows.transpose(1, 0, 2).reshape(128, 8 * HD)
    source = inputs.astype(f32)
    residual = source + pair_sum(dot(attended_rows, output_all, ((1,), (1,))))
    mixture_inverse = lax.rsqrt(jnp.mean(residual * residual, axis=-1, keepdims=True) + epsilon)
    mixed_low = (residual * mixture_inverse * mixture_gain_all).astype(bf16)
    mixed_rows = exchange(dispatch(main_table, rest_table, mixed_low), CTX)

    grad_flat, hidden_pull = expert_pull(
        side_place, grad_rows, grad_other, down_weight[0]
    )
    mixed_rows, heads_all = lax.optimization_barrier((mixed_rows, heads_all))
    entry_sent, entry, hidden_low, gate_raw_grad, up_raw_grad, logit_grad = expert_step(
        place.reshape(1).astype(jnp.int32),
        mixed_rows,
        hidden_pull,
        gate_weight[0],
        up_weight[0],
        small_all,
    )
    entry_back = exchange(entry_sent, CTX)
    result_sent = expert_result(hidden_low, down_weight[0])
    down_weight_grad = dot(hidden_low, grad_flat, ((0,), (0,)))
    gate_weight_grad = dot(entry, gate_raw_grad, ((0,), (0,)))
    up_weight_grad = dot(entry, up_raw_grad, ((0,), (0,)))
    router_part = dot(entry, logit_grad, ((0,), (0,)))
    entry_back, down_weight_grad, gate_weight_grad, up_weight_grad, router_part = (
        lax.optimization_barrier(
            (entry_back, down_weight_grad, gate_weight_grad, up_weight_grad, router_part)
        )
    )

    mixed_grad = pair_sum(collect(main_table, rest_table, entry_back))

    grad_out = cotangent.astype(f32)
    scaled = mixed_grad * mixture_gain_all
    residual_grad = (
        grad_out
        + mixture_inverse * scaled
        - residual
        * mixture_inverse
        * mixture_inverse
        * mixture_inverse
        * jnp.mean(scaled * residual, axis=-1, keepdims=True)
    )
    mixture_gain_part = jnp.sum(mixed_grad * residual * mixture_inverse, axis=0)
    residual_low = residual_grad.astype(bf16)
    attended_grad = dot(residual_low, output_all).astype(bf16)
    attended_grad = attended_grad.reshape(128, 8, HD).transpose(1, 0, 2)
    attended_grad = exchange(attended_grad.reshape(1024, HD), HEADS)
    result_sent, attended_grad = lax.optimization_barrier((result_sent, attended_grad))
    result_back = exchange(result_sent, CTX)
    delta = jnp.sum(attended_grad.astype(f32) * attended, axis=-1)[None]
    query_grad, kv_part = attend_back(
        z_place, query_some, query_factor, query_low, attended_grad, kv, end, lse, delta
    )
    kv_grad = lax.psum_scatter(kv_part, TOKENS, scatter_dimension=0, tiled=True)
    query_grad, result_back = lax.optimization_barrier((query_grad, result_back))
    query_grad = linger(query_grad)
    residual_sent, result_back = lax.optimization_barrier((residual_low, result_back))
    bands = residual_sent.reshape(128, 4, 1, BAND).transpose(1, 2, 0, 3)
    bands = jnp.broadcast_to(bands, (4, 2, 128, BAND)).reshape(1024, BAND)
    residual_band = exchange(bands, HEADS)
    kv_grad = kv_grad.astype(f32)
    final = residual + pair_sum(collect(main_table, rest_table, result_back))
    value_grad_low = kv_grad[:, HD:].astype(bf16)
    query_normed_grad = rotate(query_grad, cosine, -sine)
    key_normed_grad = rotate(kv_grad[:, :HD], cosine, -sine)
    query_scaled = query_normed_grad * query_gain_all
    key_scaled = key_normed_grad * key_gain_all
    dots = jnp.stack(
        [jnp.sum(query_scaled * query_raw, axis=-1), jnp.sum(key_scaled * key_raw, axis=-1)]
    )
    residual_band, dots = lax.optimization_barrier((residual_band, dots))
    output_part = dot(residual_band, heads_all, ((0,), (0,)))
    dots = sum_over_rows(dots.reshape(16, 128)).reshape(2, 1024)[:, :, None] / float(D)

    def raw_back(value, inverse, scaled_grad, mean):
        return (inverse * scaled_grad - value * inverse * inverse * inverse * mean).astype(bf16)

    query_raw_low = raw_back(query_raw, query_inverse, query_scaled, dots[0])
    key_raw_low = raw_back(key_raw, key_inverse, key_scaled, dots[1])
    query_gain_part = jnp.sum(query_normed_grad * query_raw * query_inverse, axis=0)
    key_gain_part = jnp.sum(key_normed_grad * key_raw * key_inverse, axis=0)
    raw_grads = jnp.concatenate([query_raw_low, key_raw_low, value_grad_low], axis=1)

    def head_part(value):
        wide = lax.dynamic_update_slice(jnp.zeros((8 * HD,), f32), value, (head * HD,))
        return jnp.pad(wide.reshape(64, 16), ((0, 0), (0, 16))).reshape(1, D)

    extra = jnp.concatenate(
        [
            jnp.zeros((1, D), f32),
            mixture_gain_part[None],
            head_part(query_gain_part),
            head_part(key_gain_part),
            jnp.zeros((4, D), f32),
        ],
        axis=0,
    )
    normed_part, gain_total = back_grads(raw_grads, normed_low, weights_all, gain_rows)
    normed_back = exchange(normed_part, HEADS)
    shares = share_grads(raw_grads, normed_low, router_part, extra, gain_total, output_part)

    summed = lax.psum_scatter(shares, TOKENS, scatter_dimension=0, tiled=True)
    output_sum = jnp.broadcast_to(summed[256:].reshape(1, 2, 32, 512), (4, 2, 32, 512))
    shares = jnp.concatenate(
        [summed[:256].reshape(8, 32, 512), output_sum.reshape(8, 32, 512)], axis=1
    )
    shares, normed_back = lax.optimization_barrier((shares.reshape(512, 512), normed_back))
    shares = exchange(shares, HEADS)
    normed_grad = pair_sum(jnp.sum(normed_back.reshape(8, 128, D).astype(f32), axis=0))
    query_part, key_part, value_part, output_grad, extra = finish(
        x.reshape(1).astype(jnp.int32), shares
    )
    pair = extra + swap(extra, "ep")
    router_grad = pair[:, :64]
    attention_gain_grad = pair[:, 64]

    inverse = lax.rsqrt(jnp.mean(source * source, axis=-1, keepdims=True) + epsilon)
    scaled = normed_grad * attention_gain_all
    input_grad = (
        residual_grad
        + inverse * scaled
        - source
        * inverse
        * inverse
        * inverse
        * jnp.mean(scaled * source, axis=-1, keepdims=True)
    )
    return (
        final,
        input_grad,
        attention_gain_grad,
        query_part,
        key_part,
        value_part,
        extra[:16, 66],
        extra[:16, 67],
        output_grad,
        extra[:, 65],
        router_grad,
        gate_weight_grad[None],
        up_weight_grad[None],
        down_weight_grad[None],
    )


def solution(mesh):
    inner = Mesh(mesh.devices.reshape(4, 4, 2, 2, 2), ("x", "z", "yh", "c", "ep"))
    in_specs = (
        P(CTX, None),
        P(CTX),
        P(CTX, None),
        P(CTX),
        P(CTX, "ep"),
        P(CTX, "ep"),
        P(CTX, "ep"),
        P(("ep",) + CTX),
        P(("ep",) + CTX),
        P("ep", CTX),
        P(CTX),
        P(CTX, None),
        P(CTX, None, "ep"),
        P(CTX, None, "ep"),
        P(CTX, "ep", None),
        P(CTX, None),
    )
    out_specs = (
        P(CTX, None),
        P(CTX, None),
        P(CTX),
        P(CTX, "ep"),
        P(CTX, "ep"),
        P(CTX, "ep"),
        P(("ep",) + CTX),
        P(("ep",) + CTX),
        P("ep", CTX),
        P(CTX),
        P(CTX, None),
        P(CTX, None, "ep"),
        P(CTX, None, "ep"),
        P(CTX, "ep", None),
    )
    return jax.shard_map(local, mesh=inner, in_specs=in_specs, out_specs=out_specs, check_vma=False)
```

```python
import functools

import jax
import jax.numpy as jnp
from jax import lax
from jax.experimental import pallas as pl
from jax.experimental.pallas import tpu as pltpu
from jax.sharding import Mesh
from jax.sharding import PartitionSpec as P

D = 2048
H = 16
HD = 128
TOPK = 8
CAP = 20
MAIN = 16
REST = CAP - MAIN
QUARTERS = 4
BAND = D // QUARTERS
WINDOW = 512
HALF_MAIN = 32 * MAIN
HALF_REST = 32 * REST
HALF = HALF_MAIN + HALF_REST
ROW_WIDTH = D + BAND
SIDE = D // 2
SIDE_BAND = SIDE // QUARTERS
SIDE_WIDTH = SIDE + SIDE_BAND

epsilon = 1e-05
rotary_base = 10000.0
masked_score = -1e30
scale = HD ** (-0.5)
log2e = 1.4426950408889634
bf16 = jnp.bfloat16
f32 = jnp.float32

CTX = ("x", "z", "yh", "c")
HEADS = ("x", "yh")
TOKENS = ("z", "c")
ROWS = ("x", "yh", "ep")


def dot(first, second, dims=((1,), (0,))):
    return lax.dot_general(first, second, (dims, ((), ())), preferred_element_type=f32)


def exchange(value, axes):
    return lax.all_to_all(value, axes, split_axis=0, concat_axis=0, tiled=True)


OFFSETS = [(i, j) for i in range(4) for j in range(2)]


def ahead(value, axis, steps):
    return lax.ppermute(value, axis, [(a, (a + steps) % 4) for a in range(4)])


def ring(value, axis):
    half = value.shape[0] // 2
    behind = ahead(value, axis, 1)
    front = ahead(value, axis, 3)
    far = [ahead(behind[:half], axis, 1), ahead(front[half:], axis, 3)]
    return [[value], [behind], far, [front]]


def swap(value, axis):
    return lax.ppermute(value, axis, [(0, 1), (1, 0)])


def gather_sum(value, x, yh):
    def rows(i):
        return lax.dynamic_slice(value, ((x + i) % 4 * 256, 0), (256, D))

    far, plus, minus, own = rows(2), rows(1), rows(3), rows(0)
    from_behind = ahead(far[:, :SIDE], "x", 1)
    from_front = ahead(far[:, SIDE:], "x", 3)
    plus = jnp.concatenate([plus[:, :SIDE] + from_behind, plus[:, SIDE:]], axis=1)
    minus = jnp.concatenate([minus[:, :SIDE], minus[:, SIDE:] + from_front], axis=1)
    total = own.astype(f32) + ahead(plus, "x", 1).astype(f32)
    total = (total + ahead(minus, "x", 3).astype(f32)).astype(bf16)
    mine = lax.dynamic_slice(total, (yh * 128, 0), (128, D))
    other = lax.dynamic_slice(total, ((1 - yh) * 128, 0), (128, D))
    mine, other = lax.optimization_barrier((mine, other))
    across = lax.ppermute(other, ("yh", "ep"), [(n, 3 - n) for n in range(4)])
    return mine, swap(mine, "ep"), swap(other, "yh"), across


def below(a, b):
    return jnp.stack([(a - i) % 4 * 2 + (b - j) % 2 for i, j in OFFSETS])


def pair_sum(value):
    own = lax.optimization_barrier(value.astype(bf16))
    other = lax.ppermute(own, "ep", [(0, 1), (1, 0)])
    return own.astype(f32) + other.astype(f32)


def sum_over_rows(value):
    rows = value.shape[0]
    sent = jnp.broadcast_to(value[None], (16, rows, 128)).reshape(16 * rows, 128)
    return jnp.sum(exchange(sent, ROWS).reshape(16, rows, 128), axis=0)


def rotary_tables(positions):
    half = HD // 2
    frequency = rotary_base ** (-jnp.arange(half).astype(f32) / half)
    angles = positions.astype(f32)[:, None] * frequency[None, :]
    return (jnp.cos(angles), jnp.sin(angles))


def rotate(value, cosine, sine):
    half = HD // 2
    first = value[:, :half]
    second = value[:, half:]
    return jnp.concatenate(
        [first * cosine - second * sine, second * cosine + first * sine], axis=-1
    )


def window_rows(index):
    return pl.multiple_of((index % 4) * 2048 + (index // 4) * 256, 256)


def window_mask(index, end):
    row = lax.broadcasted_iota(jnp.int32, (WINDOW, 1), 0)
    place = (row & 127) + ((row >> 7) & 1) * 256 + (row >> 8) * 128 + index * WINDOW
    return place < end


def pack_kernel(line_ref, router_ref, query_ref, key_ref, value_ref, out_ref):
    row = lax.broadcasted_iota(jnp.int32, (32, 128), 0)
    lane = lax.broadcasted_iota(jnp.int32, (32, 128), 1)
    gains = jnp.where(lane & 31 == row, line_ref[:, :128], 0.0).astype(bf16)
    marks = jnp.where(lane >> 2 == row, line_ref[:, 128:], 0.0).astype(bf16)
    row = lax.broadcasted_iota(jnp.int32, (128, 128), 0)
    lane = lax.broadcasted_iota(jnp.int32, (128, 128), 1)
    gain_place = jnp.where(lane == 64 + (row >> 5), 1.0, 0.0).astype(bf16)
    mark_place = jnp.where(lane == 68 + (row & 3), 1.0, 0.0).astype(bf16)
    small = jnp.concatenate([router_ref[...].astype(f32), jnp.zeros((32, 64), f32)], axis=1)
    small = (small + dot(gains, gain_place) + dot(marks, mark_place)).astype(bf16)
    for n in range(8):
        here = slice(n * 32, n * 32 + 32)
        for part, ref in enumerate((query_ref, key_ref, value_ref)):
            out_ref[here, part * HD : part * HD + HD] = ref[:, n * HD : n * HD + HD]
        out_ref[here, 3 * HD :] = small


def project_kernel(place_ref, *refs):
    refs = list(refs)
    inputs = [[refs.pop(0) for _ in range(2 if i == 2 else 1)] for i, _ in OFFSETS]
    weights = [[refs.pop(0) for _ in range(2 if i == 2 else 1)] for i in range(4)]
    cosine_ref, sine_ref, normed_ref, raw_ref, query_ref, kv_ref = refs[:6]
    square_ref, weight_ref, small_ref, gain_ref = refs[6:]
    for n, (i, j) in enumerate(OFFSETS):
        piece = weights[2][j].at[0] if i == 2 else weights[i][0].at[j]
        for m in range(8):
            row = (place_ref[8 + n] + (m // 2) * 16 + (m % 2) * 2) * 32
            here = pl.ds(pl.multiple_of(row, 32), 32)
            weight_ref[here, :] = piece[m * 32 : m * 32 + 32, : 3 * HD]
            small_ref[here, :] = piece[m * 32 : m * 32 + 32, 3 * HD :]
    row = lax.broadcasted_iota(jnp.int32, (8, 128), 0)
    column = lax.broadcasted_iota(jnp.int32, (8, 128), 1)
    pick = jnp.where(column == row + 64, 1.0, 0.0).astype(bf16)
    gain_ref[...] = dot(pick, small_ref[...], ((1,), (1,)))
    gain = gain_ref[0:1, :]
    head_gains = jnp.concatenate(
        [
            small_ref[pl.ds(pl.multiple_of((place_ref[16] * 8 + m) * 32, 32), 16), :]
            for m in range(8)
        ],
        axis=0,
    )
    head_gains = head_gains.astype(f32).T
    for n in range(8):
        value = jnp.concatenate([part[...] for part in inputs[n]], axis=0).astype(f32)
        inverse = lax.rsqrt(jnp.mean(value * value, axis=-1, keepdims=True) + epsilon)
        normed = (value * inverse * gain).astype(bf16)
        chunk = place_ref[n]
        here = pl.ds(pl.multiple_of(chunk * 128, 128), 128)
        normed_ref[here, :] = normed
        raw = dot(normed, weight_ref[...])
        raw_ref[here, :] = raw[:, : 2 * HD]
        for part in range(2):
            own = raw[:, part * HD : part * HD + HD]
            square = jnp.sum(own * own, axis=-1, keepdims=True)
            square = jnp.broadcast_to(square, (128, 128)).T
            square_ref[pl.ds(chunk + 8 * part, 1), :] = square[0:1]
            own = own * head_gains[66 + part : 67 + part]
            own = own * cosine_ref[here, :] + pltpu.roll(own, HD // 2, 1) * sine_ref[here, :]
            if part == 0:
                query_ref[here, :] = own.astype(bf16)
            else:
                kv_ref[here, :HD] = own.astype(bf16)
        kv_ref[here, HD:] = raw[:, 2 * HD :].astype(bf16)


def spread_kernel(
    place_ref,
    raw_ref,
    normed_ref,
    weight_ref,
    router_ref,
    gain_ref,
    mixture_ref,
    head_ref,
    output_ref,
    back_ref,
    share_ref,
):
    total = jnp.zeros((1, D), f32)
    for n in range(4):
        here = slice(n * 256, n * 256 + 256)
        part = dot(raw_ref[here, :], weight_ref[...], ((1,), (1,)))
        total = total + jnp.sum(part * normed_ref[here, :].astype(f32), axis=0, keepdims=True)
        back_ref[here, :] = part.astype(bf16)
    total = total / gain_ref[0:1, :]
    row = lax.broadcasted_iota(jnp.int32, (8, 1), 0)
    feature = lax.broadcasted_iota(jnp.int32, (HD, D), 0)
    place = lax.broadcasted_iota(jnp.int32, (HD, D), 1)
    match = (place >> 8 == place_ref[0]) & (place & 31 < 16)
    match = match & (((place >> 5) & 7) * 16 + (place & 31) == feature)
    extra = dot(head_ref[...].astype(bf16), jnp.where(match, 1.0, 0.0).astype(bf16))
    extra = extra + jnp.where(row == 0, total, 0.0) + jnp.where(row == 1, mixture_ref[...], 0.0)
    for n in range(4):
        band = slice(n * 512, n * 512 + 512)
        part = dot(normed_ref[:, band], raw_ref[...], ((0,), (0,))).astype(bf16)
        side = jnp.concatenate(
            [jnp.zeros((64, 512), f32), extra[:, band], jnp.zeros((56, 512), f32)], axis=0
        )
        side = (side.T + router_ref[band, :]).astype(bf16)
        for m in range(16):
            z, yh, c = m // 4, m // 2 % 2, m % 2
            start = (z * 2 + c) * 320
            there = slice(start + (n * 2 + yh) * 32, start + (n * 2 + yh) * 32 + 32)
            share_ref[there, : 3 * HD] = part[m * 32 : m * 32 + 32]
            share_ref[there, 3 * HD :] = side[m * 32 : m * 32 + 32]
            if n == 0:
                there = slice(start + 256 + yh * 32, start + 288 + yh * 32)
                share_ref[there, :] = output_ref[m * 32 : m * 32 + 32, :].astype(bf16)


def finish_kernel(
    place_ref, share_ref, own_ref, other_ref, query_ref, key_ref, value_ref, output_ref, extra_ref
):
    total = None
    for n in range(8):
        rows = share_ref[n * 32 : n * 32 + 32, :].astype(f32)
        for part, ref in enumerate((query_ref, key_ref, value_ref)):
            ref[:, n * HD : n * HD + HD] = rows[:, part * HD : part * HD + HD]
        total = rows[:, 3 * HD :] if n == 0 else total + rows[:, 3 * HD :]
    extra_ref[...] = total
    for ref, group in ((own_ref, place_ref[0]), (other_ref, 1 - place_ref[0])):
        rows = jnp.concatenate([ref[...].astype(f32), jnp.zeros((96, 512), f32)], axis=0).T
        for m in range(4):
            there = pl.ds(pl.multiple_of((m * 2 + group) * HD, HD), HD)
            output_ref[there, :] = rows[m * HD : m * HD + HD, :32]


def attend_kernel(
    z_ref, q_ref, factor_ref, raw_ref, inverse_ref, end_ref, out_ref, lse_ref, kv_ref
):
    z = z_ref[0]
    for n in range(64):
        here = slice(n * 128, n * 128 + 128)
        inverse = inverse_ref[n // 8 : n // 8 + 1, n % 8 * 128 : n % 8 * 128 + 128]
        inverse = jnp.broadcast_to(inverse, (128, 128)).T
        kv_ref[here, :HD] = (raw_ref[here, :HD].astype(f32) * inverse).astype(bf16)
        kv_ref[here, HD:] = raw_ref[here, HD:]
    for x in range(4):
        span = slice(x * 256, (x + 1) * 256)
        queries = q_ref[span, :]
        end = end_ref[:, span]
        factor = factor_ref[:, span]

        def tile(index, state, masked):
            peak, mass, total = state
            base = window_rows(index)
            part = jnp.concatenate(
                [kv_ref[pl.ds(base, 256), :], kv_ref[pl.ds(base + 1024, 256), :]], axis=0
            )
            keys, values = part[:, :HD], part[:, HD:]
            scores = dot(keys, queries, ((1,), (1,)))
            if masked:
                scores = jnp.where(window_mask(index, end), scores, masked_score)
            new_peak = jnp.maximum(peak, jnp.max(scores, axis=0, keepdims=True))
            weights = jnp.exp2((scores - new_peak) * factor)
            shrink = jnp.exp2((peak - new_peak) * factor)
            mass = mass * shrink + jnp.sum(weights, axis=0, keepdims=True)
            total = total * shrink + dot(values, weights.astype(bf16), ((0,), (0,)))
            return (new_peak, mass, total)

        state = (
            jnp.full((1, 256), masked_score, f32),
            jnp.zeros((1, 256), f32),
            jnp.zeros((HD, 256), f32),
        )
        last = 4 * x + z
        state = lax.fori_loop(0, last, lambda i, s: tile(i, s, False), state)
        state = lax.fori_loop(
            last, jnp.minimum(last + 2, 16), lambda i, s: tile(i, s, True), state
        )
        peak, mass, total = state
        out_ref[span, :] = (total / mass).T
        lse_ref[:, span] = peak * factor + jnp.log(mass) * log2e


def attend_back_kernel(
    z_ref,
    raw_ref,
    factor_ref,
    q_ref,
    grad_ref,
    kv_ref,
    end_ref,
    lse_ref,
    delta_ref,
    dq_ref,
    dkv_ref,
    sums,
):
    z = z_ref[0]
    sums[...] = jnp.zeros_like(sums)
    for x in range(4):
        span = slice(x * 256, (x + 1) * 256)
        raw = raw_ref[span, :]
        factor = factor_ref[:, span]
        queries = q_ref[span, :]
        grads = grad_ref[span, :]
        end = end_ref[:, span]
        lse = lse_ref[:, span]
        delta = delta_ref[:, span]

        def tile(index, total, masked):
            base = window_rows(index)
            part = jnp.concatenate(
                [kv_ref[pl.ds(base, 256), :], kv_ref[pl.ds(base + 1024, 256), :]], axis=0
            )
            keys, values = part[:, :HD], part[:, HD:]
            scores = dot(keys, raw, ((1,), (1,))) * factor - lse
            if masked:
                scores = jnp.where(window_mask(index, end), scores, masked_score)
            chances = jnp.exp2(scores)
            value_dot = dot(values, grads, ((1,), (1,)))
            score_grad = (chances * (value_dot - delta)).astype(bf16)
            key_term = dot(score_grad, queries)
            value_term = dot(chances.astype(bf16), grads)
            sums[pl.ds(base, 256), :HD] += key_term[:256]
            sums[pl.ds(base + 1024, 256), :HD] += key_term[256:]
            sums[pl.ds(base, 256), HD:] += value_term[:256]
            sums[pl.ds(base + 1024, 256), HD:] += value_term[256:]
            return total + dot(keys, score_grad, ((0,), (0,)))

        total = jnp.zeros((HD, 256), f32)
        last = 4 * x + z
        total = lax.fori_loop(0, last, lambda i, s: tile(i, s, False), total)
        total = lax.fori_loop(
            last, jnp.minimum(last + 2, 16), lambda i, s: tile(i, s, True), total
        )
        dq_ref[span, :] = total.T * scale
    dkv_ref[:, :HD] = (sums[:, :HD] * scale).astype(bf16)
    dkv_ref[:, HD:] = sums[:, HD:].astype(bf16)


def rest_pick(quarter):
    row = lax.broadcasted_iota(jnp.int32, (HALF_REST, HALF_MAIN), 0)
    column = lax.broadcasted_iota(jnp.int32, (HALF_REST, HALF_MAIN), 1)
    same = (column >> 4 == row >> 2) & (column & 3 == row & 3)
    return jnp.where(same & ((column >> 2) & 3 == quarter), 1.0, 0.0).astype(bf16)


def open_rest(rows):
    rest = rows[:, D:]
    return jnp.concatenate(
        [dot(rest_pick(q), rest).astype(bf16) for q in range(QUARTERS)], axis=1
    )


def open_side(rows_ref):
    rest = rows_ref[:, SIDE:]
    rest = jnp.concatenate(
        [dot(rest_pick(q), rest).astype(bf16) for q in range(QUARTERS)], axis=1
    )
    return rows_ref[:, :SIDE], rest


def pull_kernel(side_ref, own_ref, other_ref, down_ref, flat_ref, pull_ref):
    own = pl.multiple_of(side_ref[0] * SIDE, SIDE)
    other = pl.multiple_of(SIDE - side_ref[0] * SIDE, SIDE)
    for ref, start in ((own_ref, own), (other_ref, other)):
        main, rest = open_side(ref)
        flat_ref[:HALF_MAIN, pl.ds(start, SIDE)] = main
        flat_ref[HALF_MAIN:, pl.ds(start, SIDE)] = rest
    pull_ref[...] = dot(flat_ref[...], down_ref[...], ((1,), (1,)))


def expert_kernel(
    place_ref,
    rows_ref,
    pull_ref,
    gate_ref,
    up_ref,
    router_ref,
    back_ref,
    flat_ref,
    hidden_ref,
    gate_grad_ref,
    up_grad_ref,
    logit_grad_ref,
):
    flat_ref[:HALF_MAIN] = rows_ref[:, :D]
    flat_ref[HALF_MAIN:] = open_rest(rows_ref)
    entry = flat_ref[...]
    lane = lax.broadcasted_iota(jnp.int32, (1, 128), 1)
    logits = jnp.where(lane < 64, dot(entry, router_ref[...]), masked_score)
    shifted = jnp.exp(logits - jnp.max(logits, axis=-1, keepdims=True))
    probability = shifted / jnp.sum(shifted, axis=-1, keepdims=True)
    own = jnp.where(lane == place_ref[0], 1.0, 0.0)
    gates = jnp.sum(probability * own, axis=-1, keepdims=True)
    gate = dot(entry, gate_ref[...])
    upward = dot(entry, up_ref[...])
    pull = pull_ref[...]
    sigma = 1.0 / (1.0 + jnp.exp(-gate))
    swish = gate * sigma
    hidden = swish * upward
    row_grad = jnp.sum(hidden * pull, axis=-1, keepdims=True) * gates
    hidden_ref[...] = (hidden * gates).astype(bf16)
    hidden_grad = pull * gates
    gate_grad = (hidden_grad * upward * (sigma + swish * (1.0 - sigma))).astype(bf16)
    up_grad = (hidden_grad * swish).astype(bf16)
    logit_grad = (row_grad * (own - probability)).astype(bf16)
    gate_grad_ref[...] = gate_grad
    up_grad_ref[...] = up_grad
    logit_grad_ref[...] = logit_grad
    rest = []
    for q in range(QUARTERS):
        band = slice(q * BAND, (q + 1) * BAND)
        part = (
            dot(gate_grad, gate_ref[band, :], ((1,), (1,)))
            + dot(up_grad, up_ref[band, :], ((1,), (1,)))
            + dot(logit_grad, router_ref[band, :], ((1,), (1,)))
        ).astype(bf16)
        back_ref[:, band] = part[:HALF_MAIN]
        rest.append(dot(rest_pick(q), part[HALF_MAIN:], ((0,), (0,))))
    back_ref[:, D:] = (rest[0] + rest[1] + rest[2] + rest[3]).astype(bf16)


def result_kernel(hidden_ref, down_ref, back_ref):
    rest = []
    for q in range(QUARTERS):
        band = slice(q * BAND, (q + 1) * BAND)
        part = dot(hidden_ref[...], down_ref[:, band]).astype(bf16)
        back_ref[:, band] = part[:HALF_MAIN]
        rest.append(dot(rest_pick(q), part[HALF_MAIN:], ((0,), (0,))))
    back_ref[:, D:] = (rest[0] + rest[1] + rest[2] + rest[3]).astype(bf16)


SMEM = pl.BlockSpec(memory_space=pltpu.SMEM)
VMEM = pl.BlockSpec(memory_space=pltpu.VMEM)
params = pltpu.CompilerParams(vmem_limit_bytes=56 * 1024 * 1024)
step_params = pltpu.CompilerParams(
    vmem_limit_bytes=56 * 1024 * 1024, dimension_semantics=("arbitrary",)
)


cheap = pl.CostEstimate(flops=1, bytes_accessed=1, transcendentals=0)
dear = pl.CostEstimate(flops=200_000_000_000, bytes_accessed=1, transcendentals=0)


def step_block(rows, columns):
    return pl.BlockSpec((rows, columns), lambda i: (i, 0))


def whole_block(rows, columns):
    return pl.BlockSpec((rows, columns), lambda i: (0, 0))


def shape(rows, columns, kind=bf16):
    return jax.ShapeDtypeStruct((rows, columns), kind)


def pack(*values):
    return pl.pallas_call(
        pack_kernel,
        out_shape=shape(256, 4 * HD),
        in_specs=[VMEM] * 5,
        out_specs=VMEM,
        compiler_params=params,
        cost_estimate=cheap,
    )(*values)


def project(places, inputs, weights, cosine, sine):
    return pl.pallas_call(
        project_kernel,
        out_shape=(
            shape(1024, D),
            shape(1024, 2 * HD, f32),
            shape(1024, HD),
            shape(1024, 2 * HD),
            shape(16, 128, f32),
            shape(D, 3 * HD),
            shape(D, 128),
            shape(8, D, f32),
        ),
        in_specs=[SMEM] + [VMEM] * (len(inputs) + len(weights) + 2),
        out_specs=(VMEM,) * 8,
        compiler_params=params,
        cost_estimate=pl.CostEstimate(
            flops=50_000_000_000, bytes_accessed=1, transcendentals=0
        ),
    )(places, *inputs, *weights, cosine, sine)


def spread_grads(*values):
    return pl.pallas_call(
        spread_kernel,
        out_shape=(shape(1024, D), shape(2560, 512)),
        in_specs=[SMEM] + [VMEM] * 8,
        out_specs=(VMEM, VMEM),
        compiler_params=params,
        cost_estimate=cheap,
    )(*values)


def finish(*values):
    return pl.pallas_call(
        finish_kernel,
        out_shape=(
            shape(32, 8 * HD, f32),
            shape(32, 8 * HD, f32),
            shape(32, 8 * HD, f32),
            shape(8 * HD, 32, f32),
            shape(32, 128, f32),
        ),
        in_specs=[SMEM] + [VMEM] * 3,
        out_specs=(VMEM,) * 5,
        compiler_params=params,
        cost_estimate=dear,
    )(*values)


def expert_pull(side, own, other, down):
    return pl.pallas_call(
        pull_kernel,
        grid=(2,),
        out_shape=(shape(1280, D), shape(1280, 512, f32)),
        in_specs=[
            SMEM,
            step_block(HALF_MAIN, SIDE_WIDTH),
            step_block(HALF_MAIN, SIDE_WIDTH),
            whole_block(512, D),
        ],
        out_specs=(step_block(HALF, D), step_block(HALF, 512)),
        compiler_params=step_params,
        cost_estimate=cheap,
    )(side, own, other, down)


def expert_step(place, rows, pull, gate, up, router):
    return pl.pallas_call(
        expert_kernel,
        grid=(2,),
        out_shape=(
            shape(1024, ROW_WIDTH),
            shape(1280, D),
            shape(1280, 512),
            shape(1280, 512),
            shape(1280, 512),
            shape(1280, 128),
        ),
        in_specs=[
            SMEM,
            step_block(HALF_MAIN, ROW_WIDTH),
            step_block(HALF, 512),
            whole_block(D, 512),
            whole_block(D, 512),
            whole_block(D, 128),
        ],
        out_specs=(
            step_block(HALF_MAIN, ROW_WIDTH),
            step_block(HALF, D),
            step_block(HALF, 512),
            step_block(HALF, 512),
            step_block(HALF, 512),
            step_block(HALF, 128),
        ),
        compiler_params=step_params,
        cost_estimate=cheap,
    )(place, rows, pull, gate, up, router)


def expert_result(hidden, down):
    return pl.pallas_call(
        result_kernel,
        grid=(2,),
        out_shape=shape(1024, ROW_WIDTH),
        in_specs=[step_block(HALF, 512), whole_block(512, D)],
        out_specs=step_block(HALF_MAIN, ROW_WIDTH),
        compiler_params=step_params,
        cost_estimate=cheap,
    )(hidden, down)


def linger_kernel(value_ref, out_ref):
    out_ref[...] = value_ref[...]


def linger(value):
    return pl.pallas_call(
        linger_kernel,
        out_shape=jax.ShapeDtypeStruct(value.shape, value.dtype),
        in_specs=[VMEM],
        out_specs=VMEM,
        cost_estimate=dear,
    )(value)


def attend(z, queries, factor, kv, inverses, end):
    return pl.pallas_call(
        attend_kernel,
        out_shape=(shape(1024, HD, f32), shape(1, 1024, f32), shape(8192, 2 * HD)),
        in_specs=[SMEM] + [VMEM] * 5,
        out_specs=(VMEM,) * 3,
        compiler_params=params,
        cost_estimate=cheap,
    )(z, queries, factor, kv, inverses, end)


def attend_back(z, raw, factor, queries, grads, kv, end, lse, delta):
    return pl.pallas_call(
        attend_back_kernel,
        out_shape=(
            shape(1024, HD, f32),
            shape(8192, 2 * HD),
        ),
        in_specs=[SMEM] + [VMEM] * 8,
        out_specs=(VMEM,) * 2,
        scratch_shapes=[pltpu.VMEM((8192, 2 * HD), f32)],
        compiler_params=params,
        cost_estimate=cheap,
    )(z, raw, factor, queries, grads, kv, end, lse, delta)


def dispatch(main_table, rest_table, value):
    band = value.shape[1] // QUARTERS
    stacked = value.reshape(128, QUARTERS, band).transpose(1, 0, 2).reshape(QUARTERS * 128, band)
    main = dot(main_table, value).astype(bf16)
    rest = dot(rest_table, stacked).astype(bf16)
    return jnp.concatenate([main, rest], axis=1)


def collect(main_table, rest_table, rows):
    width = rows.shape[1] * QUARTERS // (QUARTERS + 1)
    main = dot(main_table, rows[:, :width], ((0,), (0,)))
    rest = dot(rest_table, rows[:, width:], ((0,), (0,)))
    rest = rest.reshape(QUARTERS, 128, width // QUARTERS).transpose(1, 0, 2)
    return main + rest.reshape(128, width)


def local(
    inputs,
    blocks,
    expert_ids,
    attention_gain,
    query_weight,
    key_weight,
    value_weight,
    query_gain,
    key_gain,
    output_weight,
    mixture_gain,
    router_weight,
    gate_weight,
    up_weight,
    down_weight,
    cotangent,
):
    x = lax.axis_index("x")
    z = lax.axis_index("z")
    yh = lax.axis_index("yh")
    c = lax.axis_index("c")
    place = x * 16 + z * 4 + yh * 2 + c
    head = x * 2 + yh
    z_place = z.reshape(1).astype(jnp.int32)
    side = lax.axis_index("ep")
    side_place = side.reshape(1).astype(jnp.int32)
    heads_below = below(x, yh)

    line = [attention_gain, mixture_gain, jnp.pad(query_gain, (0, 16)), jnp.pad(key_gain, (0, 16))]
    line = jnp.concatenate([v.astype(f32) for v in line + [blocks]])[None]
    weights_sent = pack(line, router_weight, query_weight, key_weight, value_weight)
    inputs_pair = swap(inputs, "yh")
    inputs_all = [ring(inputs, "x"), ring(inputs_pair, "x")]
    inputs_all = [part for i, j in OFFSETS for part in inputs_all[j][i]]
    weights_come = exchange(weights_sent, HEADS)
    weights_all = ring(jnp.stack([weights_come, swap(weights_come, "c")]), "z")
    weights_all = [part for parts in weights_all for part in parts]
    output_all = lax.all_gather(output_weight.T, CTX, axis=0, tiled=True)

    experts = jnp.arange(64, dtype=jnp.int32)
    chosen = jnp.any(expert_ids[:, :, None] == experts[None, None, :], axis=1)
    tokens = jnp.arange(128, dtype=jnp.int32)
    earlier = (tokens[None, :] < tokens[:, None]).astype(bf16)
    ranks = dot(earlier, chosen.astype(bf16)).astype(jnp.int32)
    ranks = jnp.where(chosen, ranks, -1).T
    quarter = jnp.eye(QUARTERS, dtype=bf16)

    table = (ranks[:, None, :] == jnp.arange(CAP, dtype=jnp.int32)[None, :, None]).astype(bf16)
    main_table = table[:, :MAIN].reshape(64 * MAIN, 128)
    rest_table = table[:, None, MAIN:, None, :] * quarter[None, :, None, :, None]
    rest_table = rest_table.reshape(64 * MAIN, QUARTERS * 128)

    cotangent_side = lax.dynamic_slice(cotangent, (0, side * SIDE), (128, SIDE))
    grad_sent = dispatch(main_table, rest_table, cotangent_side)
    inputs_all, weights_all, grad_sent = lax.optimization_barrier(
        (inputs_all, weights_all, grad_sent)
    )
    grad_rows = exchange(grad_sent, CTX)
    chunk = jnp.arange(8, dtype=jnp.int32)
    chunk_start = ((chunk // 2) * 16 + z * 4 + (chunk % 2) * 2 + c) * 128
    positions = (chunk_start[:, None] + tokens[None, :]).reshape(1024)
    cosine, sine = rotary_tables(positions)
    places = jnp.concatenate(
        [heads_below, below(z, c) // 2 * 4 + below(z, c) % 2, head.reshape(1)]
    )
    normed_low, raw, query_some, kv_some, squares, weights_all, small_all, gain_rows = project(
        places.astype(jnp.int32),
        inputs_all,
        weights_all,
        jnp.concatenate([cosine, cosine], axis=1),
        jnp.concatenate([-sine, sine], axis=1),
    )
    blocks_all = small_all[:, 68:72].astype(jnp.int32).reshape(8192)
    attention_gain_all = gain_rows[0]
    mixture_gain_all = gain_rows[1]
    head_gains = small_all.reshape(64, 32, 128)[:, :16, 66:68].reshape(1024, 2).astype(f32)
    head_gains = lax.dynamic_slice(head_gains, (head * HD, 0), (HD, 2))
    query_gain_all = head_gains[:, 0]
    key_gain_all = head_gains[:, 1]
    query_raw, key_raw = raw[:, :HD], raw[:, HD:]

    kv_some, output_all = lax.optimization_barrier((kv_some, output_all))
    kv_some = lax.all_gather(kv_some, TOKENS, axis=0, tiled=True)
    own_blocks = blocks_all.reshape(4, 4, 2, 2, 128)[:, z, :, c].reshape(1024)
    end = jnp.sum((blocks_all[:, None] <= own_blocks[None, :]).astype(jnp.int32), axis=0)[None]
    squares = linger(squares)
    grad_rows, squares, end = lax.optimization_barrier((grad_rows, squares, end))
    squares = sum_over_rows(squares)
    grad_rows, squares = lax.optimization_barrier((grad_rows, squares))
    grad_other = swap(grad_rows, "ep")
    group_inverse = lax.rsqrt(squares / float(D) + epsilon)
    inverses = group_inverse[8:]
    inverses = jnp.stack([inverses, swap(inverses, "c")])
    inverses = jnp.concatenate([inverses] + [ahead(inverses, "z", i) for i in (1, 2, 3)])
    inverses = jnp.take(inverses, below(z, c), axis=0).reshape(8, 1024)
    group_inverse = group_inverse.reshape(2, 1024)
    query_inverse = group_inverse[0][:, None]
    key_inverse = group_inverse[1][:, None]
    query_factor = group_inverse[0:1] * (scale * log2e)
    query_low = (query_some.astype(f32) * query_inverse).astype(bf16)
    kv_some, end, query_low = lax.optimization_barrier((kv_some, end, query_low))
    attended, lse, kv = attend(
        z_place, query_some, query_factor, kv_some, inverses, end
    )
    attended_low = attended.astype(bf16)

    heads_all = [part for parts in ring(attended_low, "x") for part in parts]
    attended_rows, heads_all, grad_other = lax.optimization_barrier(
        (exchange(attended_low, HEADS).reshape(8, 128, HD), heads_all, grad_other)
    )
    heads_all = jnp.concatenate(heads_all, axis=0).reshape(4, 1024, HD)
    heads_all = jnp.take(heads_all, (x - jnp.arange(4)) % 4, axis=0)
    heads_all = heads_all.transpose(1, 0, 2).reshape(1024, 4 * HD)
    attended_rows = attended_rows.transpose(1, 0, 2).reshape(128, 8 * HD)
    source = inputs.astype(f32)
    residual = source + pair_sum(dot(attended_rows, output_all, ((1,), (1,))))
    mixture_inverse = lax.rsqrt(jnp.mean(residual * residual, axis=-1, keepdims=True) + epsilon)
    mixed_low = (residual * mixture_inverse * mixture_gain_all).astype(bf16)
    mixed_rows = exchange(dispatch(main_table, rest_table, mixed_low), CTX)

    grad_flat, hidden_pull = expert_pull(
        side_place, grad_rows, grad_other, down_weight[0]
    )
    mixed_rows, heads_all = lax.optimization_barrier((mixed_rows, heads_all))
    entry_sent, entry, hidden_low, gate_raw_grad, up_raw_grad, logit_grad = expert_step(
        place.reshape(1).astype(jnp.int32),
        mixed_rows,
        hidden_pull,
        gate_weight[0],
        up_weight[0],
        small_all,
    )
    entry_back = exchange(entry_sent, CTX)
    result_sent = expert_result(hidden_low, down_weight[0])
    down_weight_grad = dot(hidden_low, grad_flat, ((0,), (0,)))
    gate_weight_grad = dot(entry, gate_raw_grad, ((0,), (0,)))
    up_weight_grad = dot(entry, up_raw_grad, ((0,), (0,)))
    router_part = dot(entry, logit_grad, ((0,), (0,)))
    entry_back, down_weight_grad, gate_weight_grad, up_weight_grad, router_part = (
        lax.optimization_barrier(
            (entry_back, down_weight_grad, gate_weight_grad, up_weight_grad, router_part)
        )
    )

    mixed_grad = pair_sum(collect(main_table, rest_table, entry_back))

    grad_out = cotangent.astype(f32)
    scaled = mixed_grad * mixture_gain_all
    residual_grad = (
        grad_out
        + mixture_inverse * scaled
        - residual
        * mixture_inverse
        * mixture_inverse
        * mixture_inverse
        * jnp.mean(scaled * residual, axis=-1, keepdims=True)
    )
    mixture_gain_part = jnp.sum(mixed_grad * residual * mixture_inverse, axis=0)
    residual_low = residual_grad.astype(bf16)
    attended_grad = dot(residual_low, output_all).astype(bf16)
    attended_grad = attended_grad.reshape(128, 8, HD).transpose(1, 0, 2)
    attended_grad = exchange(attended_grad.reshape(1024, HD), HEADS)
    result_sent, attended_grad = lax.optimization_barrier((result_sent, attended_grad))
    result_back = exchange(result_sent, CTX)
    delta = jnp.sum(attended_grad.astype(f32) * attended, axis=-1)[None]
    query_grad, kv_part = attend_back(
        z_place, query_some, query_factor, query_low, attended_grad, kv, end, lse, delta
    )
    kv_grad = lax.psum_scatter(kv_part, TOKENS, scatter_dimension=0, tiled=True)
    query_grad, result_back = lax.optimization_barrier((query_grad, result_back))
    query_grad = linger(query_grad)
    residual_sent, result_back = lax.optimization_barrier((residual_low, result_back))
    bands = residual_sent.reshape(128, 4, 1, BAND).transpose(1, 2, 0, 3)
    bands = jnp.broadcast_to(bands, (4, 2, 128, BAND)).reshape(1024, BAND)
    residual_band = exchange(bands, HEADS)
    kv_grad = kv_grad.astype(f32)
    final = residual + pair_sum(collect(main_table, rest_table, result_back))
    value_grad_low = kv_grad[:, HD:].astype(bf16)
    query_normed_grad = rotate(query_grad, cosine, -sine)
    key_normed_grad = rotate(kv_grad[:, :HD], cosine, -sine)
    query_scaled = query_normed_grad * query_gain_all
    key_scaled = key_normed_grad * key_gain_all
    dots = jnp.stack(
        [jnp.sum(query_scaled * query_raw, axis=-1), jnp.sum(key_scaled * key_raw, axis=-1)]
    )
    residual_band, dots = lax.optimization_barrier((residual_band, dots))
    output_part = dot(residual_band, heads_all, ((0,), (0,)))
    dots = sum_over_rows(dots.reshape(16, 128)).reshape(2, 1024)[:, :, None] / float(D)

    def raw_back(value, inverse, scaled_grad, mean):
        return (inverse * scaled_grad - value * inverse * inverse * inverse * mean).astype(bf16)

    query_raw_low = raw_back(query_raw, query_inverse, query_scaled, dots[0])
    key_raw_low = raw_back(key_raw, key_inverse, key_scaled, dots[1])
    query_gain_part = jnp.sum(query_normed_grad * query_raw * query_inverse, axis=0)
    key_gain_part = jnp.sum(key_normed_grad * key_raw * key_inverse, axis=0)
    raw_grads = jnp.concatenate([query_raw_low, key_raw_low, value_grad_low], axis=1)

    head_gains = jnp.concatenate(
        [
            jnp.zeros((2, HD), f32),
            query_gain_part[None],
            key_gain_part[None],
            jnp.zeros((4, HD), f32),
        ],
        axis=0,
    )
    normed_part, shares = spread_grads(
        head.reshape(1).astype(jnp.int32),
        raw_grads,
        normed_low,
        weights_all,
        router_part,
        gain_rows,
        mixture_gain_part[None],
        head_gains,
        output_part,
    )

    summed = lax.psum_scatter(shares, TOKENS, scatter_dimension=0, tiled=True)
    output_own = lax.dynamic_slice(summed, (256 + yh * 32, 0), (32, 512))
    output_other = swap(lax.dynamic_slice(summed, (288 - yh * 32, 0), (32, 512)), "yh")
    shares, output_other, normed_sums = lax.optimization_barrier(
        (exchange(summed[:256], HEADS), output_other, gather_sum(normed_part, x, yh))
    )
    normed_sums = [part.astype(f32) for part in normed_sums]
    normed_grad = (normed_sums[0] + normed_sums[1]) + (normed_sums[2] + normed_sums[3])
    query_part, key_part, value_part, output_grad, extra = finish(
        yh.reshape(1).astype(jnp.int32), shares, output_own, output_other
    )
    pair = extra + swap(extra, "ep")
    router_grad = pair[:, :64]
    attention_gain_grad = pair[:, 64]

    inverse = lax.rsqrt(jnp.mean(source * source, axis=-1, keepdims=True) + epsilon)
    scaled = normed_grad * attention_gain_all
    input_grad = (
        residual_grad
        + inverse * scaled
        - source
        * inverse
        * inverse
        * inverse
        * jnp.mean(scaled * source, axis=-1, keepdims=True)
    )
    return (
        final,
        input_grad,
        attention_gain_grad,
        query_part,
        key_part,
        value_part,
        extra[:16, 66],
        extra[:16, 67],
        output_grad,
        extra[:, 65],
        router_grad,
        gate_weight_grad[None],
        up_weight_grad[None],
        down_weight_grad[None],
    )


def solution(mesh):
    inner = Mesh(mesh.devices.reshape(4, 4, 2, 2, 2), ("x", "z", "yh", "c", "ep"))
    in_specs = (
        P(CTX, None),
        P(CTX),
        P(CTX, None),
        P(CTX),
        P(CTX, "ep"),
        P(CTX, "ep"),
        P(CTX, "ep"),
        P(("ep",) + CTX),
        P(("ep",) + CTX),
        P("ep", CTX),
        P(CTX),
        P(CTX, None),
        P(CTX, None, "ep"),
        P(CTX, None, "ep"),
        P(CTX, "ep", None),
        P(CTX, None),
    )
    out_specs = (
        P(CTX, None),
        P(CTX, None),
        P(CTX),
        P(CTX, "ep"),
        P(CTX, "ep"),
        P(CTX, "ep"),
        P(("ep",) + CTX),
        P(("ep",) + CTX),
        P("ep", CTX),
        P(CTX),
        P(CTX, None),
        P(CTX, None, "ep"),
        P(CTX, None, "ep"),
        P(CTX, "ep", None),
    )
    return jax.shard_map(local, mesh=inner, in_specs=in_specs, out_specs=out_specs, check_vma=False)
```

```python
import functools

import jax
import jax.numpy as jnp
from jax import lax
from jax.experimental import pallas as pl
from jax.experimental.pallas import tpu as pltpu
from jax.sharding import Mesh
from jax.sharding import PartitionSpec as P

D = 2048
H = 16
HD = 128
TOPK = 8
CAP = 20
MAIN = 16
REST = CAP - MAIN
QUARTERS = 4
BAND = D // QUARTERS
WINDOW = 512
HALF_MAIN = 32 * MAIN
HALF_REST = 32 * REST
HALF = HALF_MAIN + HALF_REST
ROW_WIDTH = D + BAND
SIDE = D // 2
SIDE_BAND = SIDE // QUARTERS
SIDE_WIDTH = SIDE + SIDE_BAND

epsilon = 1e-05
rotary_base = 10000.0
masked_score = -1e30
scale = HD ** (-0.5)
log2e = 1.4426950408889634
bf16 = jnp.bfloat16
f32 = jnp.float32

CTX = ("x", "z", "yh", "c")
HEADS = ("x", "yh")
TOKENS = ("z", "c")
ROWS = ("x", "yh", "ep")


def dot(first, second, dims=((1,), (0,))):
    return lax.dot_general(first, second, (dims, ((), ())), preferred_element_type=f32)


def exchange(value, axes):
    return lax.all_to_all(value, axes, split_axis=0, concat_axis=0, tiled=True)


OFFSETS = [(i, j) for i in range(4) for j in range(2)]


def ahead(value, axis, steps):
    return lax.ppermute(value, axis, [(a, (a + steps) % 4) for a in range(4)])


def ring(value, axis):
    half = value.shape[0] // 2
    behind = ahead(value, axis, 1)
    front = ahead(value, axis, 3)
    far = [ahead(behind[:half], axis, 1), ahead(front[half:], axis, 3)]
    return [[value], [behind], far, [front]]


def swap(value, axis):
    return lax.ppermute(value, axis, [(0, 1), (1, 0)])


def gather_sum(value, x, yh):
    def rows(i):
        return lax.dynamic_slice(value, ((x + i) % 4 * 256, 0), (256, D))

    far, plus, minus, own = rows(2), rows(1), rows(3), rows(0)
    from_behind = ahead(far[:, :SIDE], "x", 1)
    from_front = ahead(far[:, SIDE:], "x", 3)
    plus = jnp.concatenate([plus[:, :SIDE] + from_behind, plus[:, SIDE:]], axis=1)
    minus = jnp.concatenate([minus[:, :SIDE], minus[:, SIDE:] + from_front], axis=1)
    total = own.astype(f32) + ahead(plus, "x", 1).astype(f32)
    total = (total + ahead(minus, "x", 3).astype(f32)).astype(bf16)
    mine = lax.dynamic_slice(total, (yh * 128, 0), (128, D))
    other = lax.dynamic_slice(total, ((1 - yh) * 128, 0), (128, D))
    mine, other = lax.optimization_barrier((mine, other))
    across = lax.ppermute(other, ("yh", "ep"), [(n, 3 - n) for n in range(4)])
    return mine, swap(mine, "ep"), swap(other, "yh"), across


def below(a, b):
    return jnp.stack([(a - i) % 4 * 2 + (b - j) % 2 for i, j in OFFSETS])


def pair_sum(value):
    own = lax.optimization_barrier(value.astype(bf16))
    other = lax.ppermute(own, "ep", [(0, 1), (1, 0)])
    return own.astype(f32) + other.astype(f32)


def sum_over_rows(value):
    rows = value.shape[0]
    sent = jnp.broadcast_to(value[None], (16, rows, 128)).reshape(16 * rows, 128)
    return jnp.sum(exchange(sent, ROWS).reshape(16, rows, 128), axis=0)


def rotary_tables(positions):
    half = HD // 2
    frequency = rotary_base ** (-jnp.arange(half).astype(f32) / half)
    angles = positions.astype(f32)[:, None] * frequency[None, :]
    return (jnp.cos(angles), jnp.sin(angles))


def rotate(value, cosine, sine):
    half = HD // 2
    first = value[:, :half]
    second = value[:, half:]
    return jnp.concatenate(
        [first * cosine - second * sine, second * cosine + first * sine], axis=-1
    )


def window_rows(index):
    return pl.multiple_of((index % 4) * 2048 + (index // 4) * 256, 256)


def window(ref, index, count):
    parts = []
    for n in range(count):
        base = window_rows(index + n)
        parts += [ref[pl.ds(base, 256), :], ref[pl.ds(base + 1024, 256), :]]
    return jnp.concatenate(parts, axis=0)


def window_mask(index, end, count):
    row = lax.broadcasted_iota(jnp.int32, (WINDOW * count, 1), 0)
    place = (row & 127) + ((row >> 7) & 1) * 256 + ((row >> 8) & 1) * 128
    place = place + ((row >> 9) + index) * WINDOW
    return place < end


def pack_kernel(line_ref, router_ref, query_ref, key_ref, value_ref, out_ref):
    row = lax.broadcasted_iota(jnp.int32, (32, 128), 0)
    lane = lax.broadcasted_iota(jnp.int32, (32, 128), 1)
    gains = jnp.where(lane & 31 == row, line_ref[:, :128], 0.0).astype(bf16)
    marks = jnp.where(lane >> 2 == row, line_ref[:, 128:], 0.0).astype(bf16)
    row = lax.broadcasted_iota(jnp.int32, (128, 128), 0)
    lane = lax.broadcasted_iota(jnp.int32, (128, 128), 1)
    gain_place = jnp.where(lane == 64 + (row >> 5), 1.0, 0.0).astype(bf16)
    mark_place = jnp.where(lane == 68 + (row & 3), 1.0, 0.0).astype(bf16)
    small = jnp.concatenate([router_ref[...].astype(f32), jnp.zeros((32, 64), f32)], axis=1)
    small = (small + dot(gains, gain_place) + dot(marks, mark_place)).astype(bf16)
    for n in range(8):
        here = slice(n * 32, n * 32 + 32)
        for part, ref in enumerate((query_ref, key_ref, value_ref)):
            out_ref[here, part * HD : part * HD + HD] = ref[:, n * HD : n * HD + HD]
        out_ref[here, 3 * HD :] = small


def project_kernel(place_ref, *refs):
    refs = list(refs)
    inputs = [[refs.pop(0) for _ in range(2 if i == 2 else 1)] for i, _ in OFFSETS]
    weights = [[refs.pop(0) for _ in range(2 if i == 2 else 1)] for i in range(4)]
    cosine_ref, sine_ref, normed_ref, raw_ref, query_ref, kv_ref = refs[:6]
    square_ref, weight_ref, small_ref, gain_ref = refs[6:]
    for n, (i, j) in enumerate(OFFSETS):
        piece = weights[2][j].at[0] if i == 2 else weights[i][0].at[j]
        for m in range(8):
            row = (place_ref[8 + n] + (m // 2) * 16 + (m % 2) * 2) * 32
            here = pl.ds(pl.multiple_of(row, 32), 32)
            weight_ref[here, :] = piece[m * 32 : m * 32 + 32, : 3 * HD]
            small_ref[here, :] = piece[m * 32 : m * 32 + 32, 3 * HD :]
    row = lax.broadcasted_iota(jnp.int32, (8, 128), 0)
    column = lax.broadcasted_iota(jnp.int32, (8, 128), 1)
    pick = jnp.where(column == row + 64, 1.0, 0.0).astype(bf16)
    gain_ref[...] = dot(pick, small_ref[...], ((1,), (1,)))
    gain = gain_ref[0:1, :]
    head_gains = jnp.concatenate(
        [
            small_ref[pl.ds(pl.multiple_of((place_ref[16] * 8 + m) * 32, 32), 16), :]
            for m in range(8)
        ],
        axis=0,
    )
    head_gains = head_gains.astype(f32).T
    for n in range(8):
        value = jnp.concatenate([part[...] for part in inputs[n]], axis=0).astype(f32)
        inverse = lax.rsqrt(jnp.mean(value * value, axis=-1, keepdims=True) + epsilon)
        normed = (value * inverse * gain).astype(bf16)
        chunk = place_ref[n]
        here = pl.ds(pl.multiple_of(chunk * 128, 128), 128)
        normed_ref[here, :] = normed
        raw = dot(normed, weight_ref[...])
        raw_ref[here, :] = raw[:, : 2 * HD]
        for part in range(2):
            own = raw[:, part * HD : part * HD + HD]
            square = jnp.sum(own * own, axis=-1, keepdims=True)
            square = jnp.broadcast_to(square, (128, 128)).T
            square_ref[pl.ds(chunk + 8 * part, 1), :] = square[0:1]
            own = own * head_gains[66 + part : 67 + part]
            own = own * cosine_ref[here, :] + pltpu.roll(own, HD // 2, 1) * sine_ref[here, :]
            if part == 0:
                query_ref[here, :] = own.astype(bf16)
            else:
                kv_ref[here, :HD] = own.astype(bf16)
        kv_ref[here, HD:] = raw[:, 2 * HD :].astype(bf16)


def spread_kernel(
    place_ref,
    raw_ref,
    normed_ref,
    weight_ref,
    router_ref,
    gain_ref,
    mixture_ref,
    head_ref,
    output_ref,
    back_ref,
    share_ref,
):
    total = jnp.zeros((1, D), f32)
    for n in range(4):
        here = slice(n * 256, n * 256 + 256)
        part = dot(raw_ref[here, :], weight_ref[...], ((1,), (1,)))
        total = total + jnp.sum(part * normed_ref[here, :].astype(f32), axis=0, keepdims=True)
        back_ref[here, :] = part.astype(bf16)
    total = total / gain_ref[0:1, :]
    row = lax.broadcasted_iota(jnp.int32, (8, 1), 0)
    feature = lax.broadcasted_iota(jnp.int32, (HD, D), 0)
    place = lax.broadcasted_iota(jnp.int32, (HD, D), 1)
    match = (place >> 8 == place_ref[0]) & (place & 31 < 16)
    match = match & (((place >> 5) & 7) * 16 + (place & 31) == feature)
    extra = dot(head_ref[...].astype(bf16), jnp.where(match, 1.0, 0.0).astype(bf16))
    extra = extra + jnp.where(row == 0, total, 0.0) + jnp.where(row == 1, mixture_ref[...], 0.0)
    for n in range(4):
        band = slice(n * 512, n * 512 + 512)
        part = dot(normed_ref[:, band], raw_ref[...], ((0,), (0,))).astype(bf16)
        side = jnp.concatenate(
            [jnp.zeros((64, 512), f32), extra[:, band], jnp.zeros((56, 512), f32)], axis=0
        )
        side = (side.T + router_ref[band, :]).astype(bf16)
        for m in range(16):
            z, yh, c = m // 4, m // 2 % 2, m % 2
            start = (z * 2 + c) * 320
            there = slice(start + (n * 2 + yh) * 32, start + (n * 2 + yh) * 32 + 32)
            share_ref[there, : 3 * HD] = part[m * 32 : m * 32 + 32]
            share_ref[there, 3 * HD :] = side[m * 32 : m * 32 + 32]
            if n == 0:
                there = slice(start + 256 + yh * 32, start + 288 + yh * 32)
                share_ref[there, :] = output_ref[m * 32 : m * 32 + 32, :].astype(bf16)


def finish_kernel(
    place_ref, share_ref, own_ref, other_ref, query_ref, key_ref, value_ref, output_ref, extra_ref
):
    total = None
    for n in range(8):
        rows = share_ref[n * 32 : n * 32 + 32, :].astype(f32)
        for part, ref in enumerate((query_ref, key_ref, value_ref)):
            ref[:, n * HD : n * HD + HD] = rows[:, part * HD : part * HD + HD]
        total = rows[:, 3 * HD :] if n == 0 else total + rows[:, 3 * HD :]
    extra_ref[...] = total
    for ref, group in ((own_ref, place_ref[0]), (other_ref, 1 - place_ref[0])):
        rows = jnp.concatenate([ref[...].astype(f32), jnp.zeros((96, 512), f32)], axis=0).T
        for m in range(4):
            there = pl.ds(pl.multiple_of((m * 2 + group) * HD, HD), HD)
            output_ref[there, :] = rows[m * HD : m * HD + HD, :32]


def attend_kernel(
    z_ref, q_ref, factor_ref, raw_ref, inverse_ref, end_ref, out_ref, lse_ref, kv_ref
):
    z = z_ref[0]
    for n in range(64):
        here = slice(n * 128, n * 128 + 128)
        inverse = inverse_ref[n // 8 : n // 8 + 1, n % 8 * 128 : n % 8 * 128 + 128]
        inverse = jnp.broadcast_to(inverse, (128, 128)).T
        kv_ref[here, :HD] = (raw_ref[here, :HD].astype(f32) * inverse).astype(bf16)
        kv_ref[here, HD:] = raw_ref[here, HD:]
    for x in range(4):
        span = slice(x * 256, (x + 1) * 256)
        queries = q_ref[span, :]
        end = end_ref[:, span]
        factor = factor_ref[:, span]

        def tile(index, state, count, masked=False):
            peak, mass, total = state
            part = window(kv_ref, index, count)
            keys, values = part[:, :HD], part[:, HD:]
            scores = dot(keys, queries, ((1,), (1,)))
            if masked:
                scores = jnp.where(window_mask(index, end, count), scores, masked_score)
            new_peak = jnp.maximum(peak, jnp.max(scores, axis=0, keepdims=True))
            weights = jnp.exp2((scores - new_peak) * factor)
            shrink = jnp.exp2((peak - new_peak) * factor)
            mass = mass * shrink + jnp.sum(weights, axis=0, keepdims=True)
            total = total * shrink + dot(values, weights.astype(bf16), ((0,), (0,)))
            return (new_peak, mass, total)

        state = (
            jnp.full((1, 256), masked_score, f32),
            jnp.zeros((1, 256), f32),
            jnp.zeros((HD, 256), f32),
        )
        last = 4 * x + z
        state = lax.fori_loop(0, last // 4, lambda i, s: tile(4 * i, s, 4), state)
        state = lax.fori_loop(last // 4 * 2, last // 2, lambda i, s: tile(2 * i, s, 2), state)
        state = lax.fori_loop(last // 2 * 2, last, lambda i, s: tile(i, s, 1), state)
        state = tile(last, state, 2, True)
        peak, mass, total = state
        out_ref[span, :] = (total / mass).T
        lse_ref[:, span] = peak * factor + jnp.log(mass) * log2e


def attend_back_kernel(
    z_ref,
    raw_ref,
    factor_ref,
    q_ref,
    grad_ref,
    kv_ref,
    end_ref,
    lse_ref,
    delta_ref,
    dq_ref,
    dkv_ref,
    sums,
):
    z = z_ref[0]
    sums[...] = jnp.zeros_like(sums)
    for x in range(4):
        span = slice(x * 256, (x + 1) * 256)
        raw = raw_ref[span, :]
        factor = factor_ref[:, span]
        queries = q_ref[span, :]
        grads = grad_ref[span, :]
        end = end_ref[:, span]
        lse = lse_ref[:, span]
        delta = delta_ref[:, span]

        def tile(index, total, count, masked=False):
            part = window(kv_ref, index, count)
            keys, values = part[:, :HD], part[:, HD:]
            scores = dot(keys, raw, ((1,), (1,))) * factor - lse
            if masked:
                scores = jnp.where(window_mask(index, end, count), scores, masked_score)
            chances = jnp.exp2(scores)
            value_dot = dot(values, grads, ((1,), (1,)))
            score_grad = (chances * (value_dot - delta)).astype(bf16)
            key_term = dot(score_grad, queries)
            value_term = dot(chances.astype(bf16), grads)
            for n in range(2 * count):
                here = pl.ds(window_rows(index + n // 2) + n % 2 * 1024, 256)
                sums[here, :HD] += key_term[n * 256 : n * 256 + 256]
                sums[here, HD:] += value_term[n * 256 : n * 256 + 256]
            return total + dot(keys, score_grad, ((0,), (0,)))

        total = jnp.zeros((HD, 256), f32)
        last = 4 * x + z
        total = lax.fori_loop(0, last // 4, lambda i, s: tile(4 * i, s, 4), total)
        total = lax.fori_loop(last // 4 * 2, last // 2, lambda i, s: tile(2 * i, s, 2), total)
        total = lax.fori_loop(last // 2 * 2, last, lambda i, s: tile(i, s, 1), total)
        total = tile(last, total, 2, True)
        dq_ref[span, :] = total.T * scale
    dkv_ref[:, :HD] = (sums[:, :HD] * scale).astype(bf16)
    dkv_ref[:, HD:] = sums[:, HD:].astype(bf16)


def rest_pick(quarter):
    row = lax.broadcasted_iota(jnp.int32, (HALF_REST, HALF_MAIN), 0)
    column = lax.broadcasted_iota(jnp.int32, (HALF_REST, HALF_MAIN), 1)
    same = (column >> 4 == row >> 2) & (column & 3 == row & 3)
    return jnp.where(same & ((column >> 2) & 3 == quarter), 1.0, 0.0).astype(bf16)


def open_rest(rows):
    rest = rows[:, D:]
    return jnp.concatenate(
        [dot(rest_pick(q), rest).astype(bf16) for q in range(QUARTERS)], axis=1
    )


def open_side(rows_ref):
    rest = rows_ref[:, SIDE:]
    rest = jnp.concatenate(
        [dot(rest_pick(q), rest).astype(bf16) for q in range(QUARTERS)], axis=1
    )
    return rows_ref[:, :SIDE], rest


def pull_kernel(side_ref, own_ref, other_ref, down_ref, flat_ref, pull_ref):
    own = pl.multiple_of(side_ref[0] * SIDE, SIDE)
    other = pl.multiple_of(SIDE - side_ref[0] * SIDE, SIDE)
    for ref, start in ((own_ref, own), (other_ref, other)):
        main, rest = open_side(ref)
        flat_ref[:HALF_MAIN, pl.ds(start, SIDE)] = main
        flat_ref[HALF_MAIN:, pl.ds(start, SIDE)] = rest
    pull_ref[...] = dot(flat_ref[...], down_ref[...], ((1,), (1,)))


def expert_kernel(
    place_ref,
    rows_ref,
    pull_ref,
    gate_ref,
    up_ref,
    router_ref,
    back_ref,
    flat_ref,
    hidden_ref,
    gate_grad_ref,
    up_grad_ref,
    logit_grad_ref,
):
    flat_ref[:HALF_MAIN] = rows_ref[:, :D]
    flat_ref[HALF_MAIN:] = open_rest(rows_ref)
    entry = flat_ref[...]
    lane = lax.broadcasted_iota(jnp.int32, (1, 128), 1)
    logits = jnp.where(lane < 64, dot(entry, router_ref[...]), masked_score)
    shifted = jnp.exp(logits - jnp.max(logits, axis=-1, keepdims=True))
    probability = shifted / jnp.sum(shifted, axis=-1, keepdims=True)
    own = jnp.where(lane == place_ref[0], 1.0, 0.0)
    gates = jnp.sum(probability * own, axis=-1, keepdims=True)
    gate = dot(entry, gate_ref[...])
    upward = dot(entry, up_ref[...])
    pull = pull_ref[...]
    sigma = 1.0 / (1.0 + jnp.exp(-gate))
    swish = gate * sigma
    hidden = swish * upward
    row_grad = jnp.sum(hidden * pull, axis=-1, keepdims=True) * gates
    hidden_ref[...] = (hidden * gates).astype(bf16)
    hidden_grad = pull * gates
    gate_grad = (hidden_grad * upward * (sigma + swish * (1.0 - sigma))).astype(bf16)
    up_grad = (hidden_grad * swish).astype(bf16)
    logit_grad = (row_grad * (own - probability)).astype(bf16)
    gate_grad_ref[...] = gate_grad
    up_grad_ref[...] = up_grad
    logit_grad_ref[...] = logit_grad
    rest = []
    for q in range(QUARTERS):
        band = slice(q * BAND, (q + 1) * BAND)
        part = (
            dot(gate_grad, gate_ref[band, :], ((1,), (1,)))
            + dot(up_grad, up_ref[band, :], ((1,), (1,)))
            + dot(logit_grad, router_ref[band, :], ((1,), (1,)))
        ).astype(bf16)
        back_ref[:, band] = part[:HALF_MAIN]
        rest.append(dot(rest_pick(q), part[HALF_MAIN:], ((0,), (0,))))
    back_ref[:, D:] = (rest[0] + rest[1] + rest[2] + rest[3]).astype(bf16)


def result_kernel(hidden_ref, down_ref, back_ref):
    rest = []
    for q in range(QUARTERS):
        band = slice(q * BAND, (q + 1) * BAND)
        part = dot(hidden_ref[...], down_ref[:, band]).astype(bf16)
        back_ref[:, band] = part[:HALF_MAIN]
        rest.append(dot(rest_pick(q), part[HALF_MAIN:], ((0,), (0,))))
    back_ref[:, D:] = (rest[0] + rest[1] + rest[2] + rest[3]).astype(bf16)


SMEM = pl.BlockSpec(memory_space=pltpu.SMEM)
VMEM = pl.BlockSpec(memory_space=pltpu.VMEM)
params = pltpu.CompilerParams(vmem_limit_bytes=56 * 1024 * 1024)
step_params = pltpu.CompilerParams(
    vmem_limit_bytes=56 * 1024 * 1024, dimension_semantics=("arbitrary",)
)


cheap = pl.CostEstimate(flops=1, bytes_accessed=1, transcendentals=0)
dear = pl.CostEstimate(flops=200_000_000_000, bytes_accessed=1, transcendentals=0)


def step_block(rows, columns):
    return pl.BlockSpec((rows, columns), lambda i: (i, 0))


def whole_block(rows, columns):
    return pl.BlockSpec((rows, columns), lambda i: (0, 0))


def shape(rows, columns, kind=bf16):
    return jax.ShapeDtypeStruct((rows, columns), kind)


def pack(*values):
    return pl.pallas_call(
        pack_kernel,
        out_shape=shape(256, 4 * HD),
        in_specs=[VMEM] * 5,
        out_specs=VMEM,
        compiler_params=params,
        cost_estimate=cheap,
    )(*values)


def project(places, inputs, weights, cosine, sine):
    return pl.pallas_call(
        project_kernel,
        out_shape=(
            shape(1024, D),
            shape(1024, 2 * HD, f32),
            shape(1024, HD),
            shape(1024, 2 * HD),
            shape(16, 128, f32),
            shape(D, 3 * HD),
            shape(D, 128),
            shape(8, D, f32),
        ),
        in_specs=[SMEM] + [VMEM] * (len(inputs) + len(weights) + 2),
        out_specs=(VMEM,) * 8,
        compiler_params=params,
        cost_estimate=pl.CostEstimate(
            flops=50_000_000_000, bytes_accessed=1, transcendentals=0
        ),
    )(places, *inputs, *weights, cosine, sine)


def spread_grads(*values):
    return pl.pallas_call(
        spread_kernel,
        out_shape=(shape(1024, D), shape(2560, 512)),
        in_specs=[SMEM] + [VMEM] * 8,
        out_specs=(VMEM, VMEM),
        compiler_params=params,
        cost_estimate=cheap,
    )(*values)


def finish(*values):
    return pl.pallas_call(
        finish_kernel,
        out_shape=(
            shape(32, 8 * HD, f32),
            shape(32, 8 * HD, f32),
            shape(32, 8 * HD, f32),
            shape(8 * HD, 32, f32),
            shape(32, 128, f32),
        ),
        in_specs=[SMEM] + [VMEM] * 3,
        out_specs=(VMEM,) * 5,
        compiler_params=params,
        cost_estimate=dear,
    )(*values)


def expert_pull(side, own, other, down):
    return pl.pallas_call(
        pull_kernel,
        grid=(2,),
        out_shape=(shape(1280, D), shape(1280, 512, f32)),
        in_specs=[
            SMEM,
            step_block(HALF_MAIN, SIDE_WIDTH),
            step_block(HALF_MAIN, SIDE_WIDTH),
            whole_block(512, D),
        ],
        out_specs=(step_block(HALF, D), step_block(HALF, 512)),
        compiler_params=step_params,
        cost_estimate=cheap,
    )(side, own, other, down)


def expert_step(place, rows, pull, gate, up, router):
    return pl.pallas_call(
        expert_kernel,
        grid=(2,),
        out_shape=(
            shape(1024, ROW_WIDTH),
            shape(1280, D),
            shape(1280, 512),
            shape(1280, 512),
            shape(1280, 512),
            shape(1280, 128),
        ),
        in_specs=[
            SMEM,
            step_block(HALF_MAIN, ROW_WIDTH),
            step_block(HALF, 512),
            whole_block(D, 512),
            whole_block(D, 512),
            whole_block(D, 128),
        ],
        out_specs=(
            step_block(HALF_MAIN, ROW_WIDTH),
            step_block(HALF, D),
            step_block(HALF, 512),
            step_block(HALF, 512),
            step_block(HALF, 512),
            step_block(HALF, 128),
        ),
        compiler_params=step_params,
        cost_estimate=cheap,
    )(place, rows, pull, gate, up, router)


def expert_result(hidden, down):
    return pl.pallas_call(
        result_kernel,
        grid=(2,),
        out_shape=shape(1024, ROW_WIDTH),
        in_specs=[step_block(HALF, 512), whole_block(512, D)],
        out_specs=step_block(HALF_MAIN, ROW_WIDTH),
        compiler_params=step_params,
        cost_estimate=cheap,
    )(hidden, down)


def linger_kernel(value_ref, out_ref):
    out_ref[...] = value_ref[...]


def linger(value):
    return pl.pallas_call(
        linger_kernel,
        out_shape=jax.ShapeDtypeStruct(value.shape, value.dtype),
        in_specs=[VMEM],
        out_specs=VMEM,
        cost_estimate=dear,
    )(value)


def attend(z, queries, factor, kv, inverses, end):
    return pl.pallas_call(
        attend_kernel,
        out_shape=(shape(1024, HD, f32), shape(1, 1024, f32), shape(8192, 2 * HD)),
        in_specs=[SMEM] + [VMEM] * 5,
        out_specs=(VMEM,) * 3,
        compiler_params=params,
        cost_estimate=cheap,
    )(z, queries, factor, kv, inverses, end)


def attend_back(z, raw, factor, queries, grads, kv, end, lse, delta):
    return pl.pallas_call(
        attend_back_kernel,
        out_shape=(
            shape(1024, HD, f32),
            shape(8192, 2 * HD),
        ),
        in_specs=[SMEM] + [VMEM] * 8,
        out_specs=(VMEM,) * 2,
        scratch_shapes=[pltpu.VMEM((8192, 2 * HD), f32)],
        compiler_params=params,
        cost_estimate=cheap,
    )(z, raw, factor, queries, grads, kv, end, lse, delta)


def dispatch(main_table, rest_table, value):
    band = value.shape[1] // QUARTERS
    stacked = value.reshape(128, QUARTERS, band).transpose(1, 0, 2).reshape(QUARTERS * 128, band)
    main = dot(main_table, value).astype(bf16)
    rest = dot(rest_table, stacked).astype(bf16)
    return jnp.concatenate([main, rest], axis=1)


def collect(main_table, rest_table, rows):
    width = rows.shape[1] * QUARTERS // (QUARTERS + 1)
    main = dot(main_table, rows[:, :width], ((0,), (0,)))
    rest = dot(rest_table, rows[:, width:], ((0,), (0,)))
    rest = rest.reshape(QUARTERS, 128, width // QUARTERS).transpose(1, 0, 2)
    return main + rest.reshape(128, width)


def local(
    inputs,
    blocks,
    expert_ids,
    attention_gain,
    query_weight,
    key_weight,
    value_weight,
    query_gain,
    key_gain,
    output_weight,
    mixture_gain,
    router_weight,
    gate_weight,
    up_weight,
    down_weight,
    cotangent,
):
    x = lax.axis_index("x")
    z = lax.axis_index("z")
    yh = lax.axis_index("yh")
    c = lax.axis_index("c")
    place = x * 16 + z * 4 + yh * 2 + c
    head = x * 2 + yh
    z_place = z.reshape(1).astype(jnp.int32)
    side = lax.axis_index("ep")
    side_place = side.reshape(1).astype(jnp.int32)
    heads_below = below(x, yh)

    line = [attention_gain, mixture_gain, jnp.pad(query_gain, (0, 16)), jnp.pad(key_gain, (0, 16))]
    line = jnp.concatenate([v.astype(f32) for v in line + [blocks]])[None]
    weights_sent = pack(line, router_weight, query_weight, key_weight, value_weight)
    inputs_pair = swap(inputs, "yh")
    inputs_all = [ring(inputs, "x"), ring(inputs_pair, "x")]
    inputs_all = [part for i, j in OFFSETS for part in inputs_all[j][i]]
    weights_come = exchange(weights_sent, HEADS)
    weights_all = ring(jnp.stack([weights_come, swap(weights_come, "c")]), "z")
    weights_all = [part for parts in weights_all for part in parts]
    output_all = lax.all_gather(output_weight.T, CTX, axis=0, tiled=True)

    experts = jnp.arange(64, dtype=jnp.int32)
    chosen = jnp.any(expert_ids[:, :, None] == experts[None, None, :], axis=1)
    tokens = jnp.arange(128, dtype=jnp.int32)
    earlier = (tokens[None, :] < tokens[:, None]).astype(bf16)
    ranks = dot(earlier, chosen.astype(bf16)).astype(jnp.int32)
    ranks = jnp.where(chosen, ranks, -1).T
    quarter = jnp.eye(QUARTERS, dtype=bf16)

    table = (ranks[:, None, :] == jnp.arange(CAP, dtype=jnp.int32)[None, :, None]).astype(bf16)
    main_table = table[:, :MAIN].reshape(64 * MAIN, 128)
    rest_table = table[:, None, MAIN:, None, :] * quarter[None, :, None, :, None]
    rest_table = rest_table.reshape(64 * MAIN, QUARTERS * 128)

    cotangent_side = lax.dynamic_slice(cotangent, (0, side * SIDE), (128, SIDE))
    grad_sent = dispatch(main_table, rest_table, cotangent_side)
    inputs_all, weights_all, grad_sent = lax.optimization_barrier(
        (inputs_all, weights_all, grad_sent)
    )
    grad_rows = exchange(grad_sent, CTX)
    chunk = jnp.arange(8, dtype=jnp.int32)
    chunk_start = ((chunk // 2) * 16 + z * 4 + (chunk % 2) * 2 + c) * 128
    positions = (chunk_start[:, None] + tokens[None, :]).reshape(1024)
    cosine, sine = rotary_tables(positions)
    places = jnp.concatenate(
        [heads_below, below(z, c) // 2 * 4 + below(z, c) % 2, head.reshape(1)]
    )
    normed_low, raw, query_some, kv_some, squares, weights_all, small_all, gain_rows = project(
        places.astype(jnp.int32),
        inputs_all,
        weights_all,
        jnp.concatenate([cosine, cosine], axis=1),
        jnp.concatenate([-sine, sine], axis=1),
    )
    blocks_all = small_all[:, 68:72].astype(jnp.int32).reshape(8192)
    attention_gain_all = gain_rows[0]
    mixture_gain_all = gain_rows[1]
    head_gains = small_all.reshape(64, 32, 128)[:, :16, 66:68].reshape(1024, 2).astype(f32)
    head_gains = lax.dynamic_slice(head_gains, (head * HD, 0), (HD, 2))
    query_gain_all = head_gains[:, 0]
    key_gain_all = head_gains[:, 1]
    query_raw, key_raw = raw[:, :HD], raw[:, HD:]

    kv_some, output_all = lax.optimization_barrier((kv_some, output_all))
    kv_some = lax.all_gather(kv_some, TOKENS, axis=0, tiled=True)
    own_blocks = blocks_all.reshape(4, 4, 2, 2, 128)[:, z, :, c].reshape(1024)
    end = jnp.sum((blocks_all[:, None] <= own_blocks[None, :]).astype(jnp.int32), axis=0)[None]
    squares = linger(squares)
    grad_rows, squares, end = lax.optimization_barrier((grad_rows, squares, end))
    squares = sum_over_rows(squares)
    grad_rows, squares = lax.optimization_barrier((grad_rows, squares))
    grad_other = swap(grad_rows, "ep")
    group_inverse = lax.rsqrt(squares / float(D) + epsilon)
    inverses = group_inverse[8:]
    inverses = jnp.stack([inverses, swap(inverses, "c")])
    inverses = jnp.concatenate([inverses] + [ahead(inverses, "z", i) for i in (1, 2, 3)])
    inverses = jnp.take(inverses, below(z, c), axis=0).reshape(8, 1024)
    group_inverse = group_inverse.reshape(2, 1024)
    query_inverse = group_inverse[0][:, None]
    key_inverse = group_inverse[1][:, None]
    query_factor = group_inverse[0:1] * (scale * log2e)
    query_low = (query_some.astype(f32) * query_inverse).astype(bf16)
    kv_some, end, query_low = lax.optimization_barrier((kv_some, end, query_low))
    attended, lse, kv = attend(
        z_place, query_some, query_factor, kv_some, inverses, end
    )
    attended_low = attended.astype(bf16)

    heads_all = [part for parts in ring(attended_low, "x") for part in parts]
    attended_rows, heads_all, grad_other = lax.optimization_barrier(
        (exchange(attended_low, HEADS).reshape(8, 128, HD), heads_all, grad_other)
    )
    heads_all = jnp.concatenate(heads_all, axis=0).reshape(4, 1024, HD)
    heads_all = jnp.take(heads_all, (x - jnp.arange(4)) % 4, axis=0)
    heads_all = heads_all.transpose(1, 0, 2).reshape(1024, 4 * HD)
    attended_rows = attended_rows.transpose(1, 0, 2).reshape(128, 8 * HD)
    source = inputs.astype(f32)
    residual = source + pair_sum(dot(attended_rows, output_all, ((1,), (1,))))
    mixture_inverse = lax.rsqrt(jnp.mean(residual * residual, axis=-1, keepdims=True) + epsilon)
    mixed_low = (residual * mixture_inverse * mixture_gain_all).astype(bf16)
    mixed_rows = exchange(dispatch(main_table, rest_table, mixed_low), CTX)

    grad_flat, hidden_pull = expert_pull(
        side_place, grad_rows, grad_other, down_weight[0]
    )
    mixed_rows, heads_all = lax.optimization_barrier((mixed_rows, heads_all))
    entry_sent, entry, hidden_low, gate_raw_grad, up_raw_grad, logit_grad = expert_step(
        place.reshape(1).astype(jnp.int32),
        mixed_rows,
        hidden_pull,
        gate_weight[0],
        up_weight[0],
        small_all,
    )
    entry_back = exchange(entry_sent, CTX)
    result_sent = expert_result(hidden_low, down_weight[0])
    down_weight_grad = dot(hidden_low, grad_flat, ((0,), (0,)))
    gate_weight_grad = dot(entry, gate_raw_grad, ((0,), (0,)))
    up_weight_grad = dot(entry, up_raw_grad, ((0,), (0,)))
    router_part = dot(entry, logit_grad, ((0,), (0,)))
    entry_back, down_weight_grad, gate_weight_grad, up_weight_grad, router_part = (
        lax.optimization_barrier(
            (entry_back, down_weight_grad, gate_weight_grad, up_weight_grad, router_part)
        )
    )

    mixed_grad = pair_sum(collect(main_table, rest_table, entry_back))

    grad_out = cotangent.astype(f32)
    scaled = mixed_grad * mixture_gain_all
    residual_grad = (
        grad_out
        + mixture_inverse * scaled
        - residual
        * mixture_inverse
        * mixture_inverse
        * mixture_inverse
        * jnp.mean(scaled * residual, axis=-1, keepdims=True)
    )
    mixture_gain_part = jnp.sum(mixed_grad * residual * mixture_inverse, axis=0)
    residual_low = residual_grad.astype(bf16)
    attended_grad = dot(residual_low, output_all).astype(bf16)
    attended_grad = attended_grad.reshape(128, 8, HD).transpose(1, 0, 2)
    attended_grad = exchange(attended_grad.reshape(1024, HD), HEADS)
    result_sent, attended_grad = lax.optimization_barrier((result_sent, attended_grad))
    result_back = exchange(result_sent, CTX)
    delta = jnp.sum(attended_grad.astype(f32) * attended, axis=-1)[None]
    query_grad, kv_part = attend_back(
        z_place, query_some, query_factor, query_low, attended_grad, kv, end, lse, delta
    )
    kv_grad = lax.psum_scatter(kv_part, TOKENS, scatter_dimension=0, tiled=True)
    query_grad, result_back = lax.optimization_barrier((query_grad, result_back))
    query_grad = linger(query_grad)
    residual_sent, result_back = lax.optimization_barrier((residual_low, result_back))
    bands = residual_sent.reshape(128, 4, 1, BAND).transpose(1, 2, 0, 3)
    bands = jnp.broadcast_to(bands, (4, 2, 128, BAND)).reshape(1024, BAND)
    residual_band = exchange(bands, HEADS)
    kv_grad = kv_grad.astype(f32)
    final = residual + pair_sum(collect(main_table, rest_table, result_back))
    value_grad_low = kv_grad[:, HD:].astype(bf16)
    query_normed_grad = rotate(query_grad, cosine, -sine)
    key_normed_grad = rotate(kv_grad[:, :HD], cosine, -sine)
    query_scaled = query_normed_grad * query_gain_all
    key_scaled = key_normed_grad * key_gain_all
    dots = jnp.stack(
        [jnp.sum(query_scaled * query_raw, axis=-1), jnp.sum(key_scaled * key_raw, axis=-1)]
    )
    residual_band, dots = lax.optimization_barrier((residual_band, dots))
    output_part = dot(residual_band, heads_all, ((0,), (0,)))
    dots = sum_over_rows(dots.reshape(16, 128)).reshape(2, 1024)[:, :, None] / float(D)

    def raw_back(value, inverse, scaled_grad, mean):
        return (inverse * scaled_grad - value * inverse * inverse * inverse * mean).astype(bf16)

    query_raw_low = raw_back(query_raw, query_inverse, query_scaled, dots[0])
    key_raw_low = raw_back(key_raw, key_inverse, key_scaled, dots[1])
    query_gain_part = jnp.sum(query_normed_grad * query_raw * query_inverse, axis=0)
    key_gain_part = jnp.sum(key_normed_grad * key_raw * key_inverse, axis=0)
    raw_grads = jnp.concatenate([query_raw_low, key_raw_low, value_grad_low], axis=1)

    head_gains = jnp.concatenate(
        [
            jnp.zeros((2, HD), f32),
            query_gain_part[None],
            key_gain_part[None],
            jnp.zeros((4, HD), f32),
        ],
        axis=0,
    )
    normed_part, shares = spread_grads(
        head.reshape(1).astype(jnp.int32),
        raw_grads,
        normed_low,
        weights_all,
        router_part,
        gain_rows,
        mixture_gain_part[None],
        head_gains,
        output_part,
    )

    summed = lax.psum_scatter(shares, TOKENS, scatter_dimension=0, tiled=True)
    output_own = lax.dynamic_slice(summed, (256 + yh * 32, 0), (32, 512))
    output_other = swap(lax.dynamic_slice(summed, (288 - yh * 32, 0), (32, 512)), "yh")
    shares, output_other, normed_sums = lax.optimization_barrier(
        (exchange(summed[:256], HEADS), output_other, gather_sum(normed_part, x, yh))
    )
    normed_sums = [part.astype(f32) for part in normed_sums]
    normed_grad = (normed_sums[0] + normed_sums[1]) + (normed_sums[2] + normed_sums[3])
    query_part, key_part, value_part, output_grad, extra = finish(
        yh.reshape(1).astype(jnp.int32), shares, output_own, output_other
    )
    pair = extra + swap(extra, "ep")
    router_grad = pair[:, :64]
    attention_gain_grad = pair[:, 64]

    inverse = lax.rsqrt(jnp.mean(source * source, axis=-1, keepdims=True) + epsilon)
    scaled = normed_grad * attention_gain_all
    input_grad = (
        residual_grad
        + inverse * scaled
        - source
        * inverse
        * inverse
        * inverse
        * jnp.mean(scaled * source, axis=-1, keepdims=True)
    )
    return (
        final,
        input_grad,
        attention_gain_grad,
        query_part,
        key_part,
        value_part,
        extra[:16, 66],
        extra[:16, 67],
        output_grad,
        extra[:, 65],
        router_grad,
        gate_weight_grad[None],
        up_weight_grad[None],
        down_weight_grad[None],
    )


def solution(mesh):
    inner = Mesh(mesh.devices.reshape(4, 4, 2, 2, 2), ("x", "z", "yh", "c", "ep"))
    in_specs = (
        P(CTX, None),
        P(CTX),
        P(CTX, None),
        P(CTX),
        P(CTX, "ep"),
        P(CTX, "ep"),
        P(CTX, "ep"),
        P(("ep",) + CTX),
        P(("ep",) + CTX),
        P("ep", CTX),
        P(CTX),
        P(CTX, None),
        P(CTX, None, "ep"),
        P(CTX, None, "ep"),
        P(CTX, "ep", None),
        P(CTX, None),
    )
    out_specs = (
        P(CTX, None),
        P(CTX, None),
        P(CTX),
        P(CTX, "ep"),
        P(CTX, "ep"),
        P(CTX, "ep"),
        P(("ep",) + CTX),
        P(("ep",) + CTX),
        P("ep", CTX),
        P(CTX),
        P(CTX, None),
        P(CTX, None, "ep"),
        P(CTX, None, "ep"),
        P(CTX, "ep", None),
    )
    return jax.shard_map(local, mesh=inner, in_specs=in_specs, out_specs=out_specs, check_vma=False)
```

```python
import functools

import jax
import jax.numpy as jnp
from jax import lax
from jax.experimental import pallas as pl
from jax.experimental.pallas import tpu as pltpu
from jax.sharding import Mesh
from jax.sharding import PartitionSpec as P

D = 2048
H = 16
HD = 128
TOPK = 8
CAP = 20
MAIN = 16
REST = CAP - MAIN
QUARTERS = 4
BAND = D // QUARTERS
WINDOW = 512
HALF_MAIN = 32 * MAIN
HALF_REST = 32 * REST
HALF = HALF_MAIN + HALF_REST
ROW_WIDTH = D + BAND
SIDE = D // 2
SIDE_BAND = SIDE // QUARTERS
SIDE_WIDTH = SIDE + SIDE_BAND

epsilon = 1e-05
rotary_base = 10000.0
masked_score = -1e30
scale = HD ** (-0.5)
log2e = 1.4426950408889634
bf16 = jnp.bfloat16
f32 = jnp.float32

CTX = ("x", "z", "yh", "c")
HEADS = ("x", "yh")
TOKENS = ("z", "c")
ROWS = ("x", "yh", "ep")


def dot(first, second, dims=((1,), (0,))):
    return lax.dot_general(first, second, (dims, ((), ())), preferred_element_type=f32)


def exchange(value, axes):
    return lax.all_to_all(value, axes, split_axis=0, concat_axis=0, tiled=True)


OFFSETS = [(i, j) for i in range(4) for j in range(2)]


def ahead(value, axis, steps):
    return lax.ppermute(value, axis, [(a, (a + steps) % 4) for a in range(4)])


def ring(value, axis):
    half = value.shape[0] // 2
    behind = ahead(value, axis, 1)
    front = ahead(value, axis, 3)
    far = [ahead(behind[:half], axis, 1), ahead(front[half:], axis, 3)]
    return [[value], [behind], far, [front]]


def swap(value, axis):
    return lax.ppermute(value, axis, [(0, 1), (1, 0)])


def gather_sum(value, x, yh):
    def rows(i):
        return lax.dynamic_slice(value, ((x + i) % 4 * 256, 0), (256, D))

    far, plus, minus, own = rows(2), rows(1), rows(3), rows(0)
    from_behind = ahead(far[:, :SIDE], "x", 1)
    from_front = ahead(far[:, SIDE:], "x", 3)
    plus = jnp.concatenate([plus[:, :SIDE] + from_behind, plus[:, SIDE:]], axis=1)
    minus = jnp.concatenate([minus[:, :SIDE], minus[:, SIDE:] + from_front], axis=1)
    total = own.astype(f32) + ahead(plus, "x", 1).astype(f32)
    total = (total + ahead(minus, "x", 3).astype(f32)).astype(bf16)
    mine = lax.dynamic_slice(total, (yh * 128, 0), (128, D))
    other = lax.dynamic_slice(total, ((1 - yh) * 128, 0), (128, D))
    mine, other = lax.optimization_barrier((mine, other))
    across = lax.ppermute(other, ("yh", "ep"), [(n, 3 - n) for n in range(4)])
    return mine, swap(mine, "ep"), swap(other, "yh"), across


def below(a, b):
    return jnp.stack([(a - i) % 4 * 2 + (b - j) % 2 for i, j in OFFSETS])


def pair_sum(value):
    own = lax.optimization_barrier(value.astype(bf16))
    other = lax.ppermute(own, "ep", [(0, 1), (1, 0)])
    return own.astype(f32) + other.astype(f32)


def sum_over_rows(value):
    rows = value.shape[0]
    sent = jnp.broadcast_to(value[None], (16, rows, 128)).reshape(16 * rows, 128)
    return jnp.sum(exchange(sent, ROWS).reshape(16, rows, 128), axis=0)


def rotary_tables(positions):
    half = HD // 2
    frequency = rotary_base ** (-jnp.arange(half).astype(f32) / half)
    angles = positions.astype(f32)[:, None] * frequency[None, :]
    return (jnp.cos(angles), jnp.sin(angles))


def rotate(value, cosine, sine):
    half = HD // 2
    first = value[:, :half]
    second = value[:, half:]
    return jnp.concatenate(
        [first * cosine - second * sine, second * cosine + first * sine], axis=-1
    )


def window_rows(index):
    return pl.multiple_of((index % 4) * 2048 + (index // 4) * 256, 256)


def window(ref, index, count):
    parts = []
    for n in range(count):
        base = window_rows(index + n)
        parts += [ref[pl.ds(base, 256), :], ref[pl.ds(base + 1024, 256), :]]
    return jnp.concatenate(parts, axis=0)


def window_mask(index, end, count):
    row = lax.broadcasted_iota(jnp.int32, (WINDOW * count, 1), 0)
    place = (row & 127) + ((row >> 7) & 1) * 256 + ((row >> 8) & 1) * 128
    place = place + ((row >> 9) + index) * WINDOW
    return place < end


def pack_kernel(line_ref, router_ref, query_ref, key_ref, value_ref, out_ref):
    row = lax.broadcasted_iota(jnp.int32, (32, 128), 0)
    lane = lax.broadcasted_iota(jnp.int32, (32, 128), 1)
    gains = jnp.where(lane & 31 == row, line_ref[:, :128], 0.0).astype(bf16)
    marks = jnp.where(lane >> 2 == row, line_ref[:, 128:], 0.0).astype(bf16)
    row = lax.broadcasted_iota(jnp.int32, (128, 128), 0)
    lane = lax.broadcasted_iota(jnp.int32, (128, 128), 1)
    gain_place = jnp.where(lane == 64 + (row >> 5), 1.0, 0.0).astype(bf16)
    mark_place = jnp.where(lane == 68 + (row & 3), 1.0, 0.0).astype(bf16)
    small = jnp.concatenate([router_ref[...].astype(f32), jnp.zeros((32, 64), f32)], axis=1)
    small = (small + dot(gains, gain_place) + dot(marks, mark_place)).astype(bf16)
    for n in range(8):
        here = slice(n * 32, n * 32 + 32)
        for part, ref in enumerate((query_ref, key_ref, value_ref)):
            out_ref[here, part * HD : part * HD + HD] = ref[:, n * HD : n * HD + HD]
        out_ref[here, 3 * HD :] = small


def project_kernel(place_ref, *refs):
    refs = list(refs)
    inputs = [[refs.pop(0) for _ in range(2 if i == 2 else 1)] for i, _ in OFFSETS]
    weights = [[refs.pop(0) for _ in range(2 if i == 2 else 1)] for i in range(4)]
    cosine_ref, sine_ref, normed_ref, raw_ref, query_ref, kv_ref = refs[:6]
    square_ref, weight_ref, small_ref, gain_ref = refs[6:]
    for n, (i, j) in enumerate(OFFSETS):
        piece = weights[2][j].at[0] if i == 2 else weights[i][0].at[j]
        for m in range(8):
            row = (place_ref[8 + n] + (m // 2) * 16 + (m % 2) * 2) * 32
            here = pl.ds(pl.multiple_of(row, 32), 32)
            weight_ref[here, :] = piece[m * 32 : m * 32 + 32, : 3 * HD]
            small_ref[here, :] = piece[m * 32 : m * 32 + 32, 3 * HD :]
    row = lax.broadcasted_iota(jnp.int32, (8, 128), 0)
    column = lax.broadcasted_iota(jnp.int32, (8, 128), 1)
    pick = jnp.where(column == row + 64, 1.0, 0.0).astype(bf16)
    gain_ref[...] = dot(pick, small_ref[...], ((1,), (1,)))
    gain = gain_ref[0:1, :]
    head_gains = jnp.concatenate(
        [
            small_ref[pl.ds(pl.multiple_of((place_ref[16] * 8 + m) * 32, 32), 16), :]
            for m in range(8)
        ],
        axis=0,
    )
    head_gains = head_gains.astype(f32).T
    for n in range(8):
        value = jnp.concatenate([part[...] for part in inputs[n]], axis=0).astype(f32)
        inverse = lax.rsqrt(jnp.mean(value * value, axis=-1, keepdims=True) + epsilon)
        normed = (value * inverse * gain).astype(bf16)
        chunk = place_ref[n]
        here = pl.ds(pl.multiple_of(chunk * 128, 128), 128)
        normed_ref[here, :] = normed
        raw = dot(normed, weight_ref[...])
        raw_ref[here, :] = raw[:, : 2 * HD]
        for part in range(2):
            own = raw[:, part * HD : part * HD + HD]
            square = jnp.sum(own * own, axis=-1, keepdims=True)
            square = jnp.broadcast_to(square, (128, 128)).T
            square_ref[pl.ds(chunk + 8 * part, 1), :] = square[0:1]
            own = own * head_gains[66 + part : 67 + part]
            own = own * cosine_ref[here, :] + pltpu.roll(own, HD // 2, 1) * sine_ref[here, :]
            if part == 0:
                query_ref[here, :] = own.astype(bf16)
            else:
                kv_ref[here, :HD] = own.astype(bf16)
        kv_ref[here, HD:] = raw[:, 2 * HD :].astype(bf16)


def spread_kernel(
    place_ref,
    raw_ref,
    normed_ref,
    weight_ref,
    router_ref,
    gain_ref,
    mixture_ref,
    head_ref,
    output_ref,
    back_ref,
    share_ref,
):
    total = jnp.zeros((1, D), f32)
    for n in range(4):
        here = slice(n * 256, n * 256 + 256)
        part = dot(raw_ref[here, :], weight_ref[...], ((1,), (1,)))
        total = total + jnp.sum(part * normed_ref[here, :].astype(f32), axis=0, keepdims=True)
        back_ref[here, :] = part.astype(bf16)
    total = total / gain_ref[0:1, :]
    row = lax.broadcasted_iota(jnp.int32, (8, 1), 0)
    feature = lax.broadcasted_iota(jnp.int32, (HD, D), 0)
    place = lax.broadcasted_iota(jnp.int32, (HD, D), 1)
    match = (place >> 8 == place_ref[0]) & (place & 31 < 16)
    match = match & (((place >> 5) & 7) * 16 + (place & 31) == feature)
    extra = dot(head_ref[...].astype(bf16), jnp.where(match, 1.0, 0.0).astype(bf16))
    extra = extra + jnp.where(row == 0, total, 0.0) + jnp.where(row == 1, mixture_ref[...], 0.0)
    for n in range(4):
        band = slice(n * 512, n * 512 + 512)
        part = dot(normed_ref[:, band], raw_ref[...], ((0,), (0,))).astype(bf16)
        side = jnp.concatenate(
            [jnp.zeros((64, 512), f32), extra[:, band], jnp.zeros((56, 512), f32)], axis=0
        )
        side = (side.T + router_ref[band, :]).astype(bf16)
        for m in range(16):
            z, yh, c = m // 4, m // 2 % 2, m % 2
            start = (z * 2 + c) * 320
            there = slice(start + (n * 2 + yh) * 32, start + (n * 2 + yh) * 32 + 32)
            share_ref[there, : 3 * HD] = part[m * 32 : m * 32 + 32]
            share_ref[there, 3 * HD :] = side[m * 32 : m * 32 + 32]
            if n == 0:
                there = slice(start + 256 + yh * 32, start + 288 + yh * 32)
                share_ref[there, :] = output_ref[m * 32 : m * 32 + 32, :].astype(bf16)


def finish_kernel(
    place_ref, share_ref, own_ref, other_ref, query_ref, key_ref, value_ref, output_ref, extra_ref
):
    total = None
    for n in range(8):
        rows = share_ref[n * 32 : n * 32 + 32, :].astype(f32)
        for part, ref in enumerate((query_ref, key_ref, value_ref)):
            ref[:, n * HD : n * HD + HD] = rows[:, part * HD : part * HD + HD]
        total = rows[:, 3 * HD :] if n == 0 else total + rows[:, 3 * HD :]
    extra_ref[...] = total
    for ref, group in ((own_ref, place_ref[0]), (other_ref, 1 - place_ref[0])):
        rows = jnp.concatenate([ref[...].astype(f32), jnp.zeros((96, 512), f32)], axis=0).T
        for m in range(4):
            there = pl.ds(pl.multiple_of((m * 2 + group) * HD, HD), HD)
            output_ref[there, :] = rows[m * HD : m * HD + HD, :32]


def attend_kernel(
    z_ref, q_ref, factor_ref, raw_ref, inverse_ref, end_ref, out_ref, lse_ref, kv_ref
):
    z = z_ref[0]
    for n in range(64):
        here = slice(n * 128, n * 128 + 128)
        inverse = inverse_ref[n // 8 : n // 8 + 1, n % 8 * 128 : n % 8 * 128 + 128]
        inverse = jnp.broadcast_to(inverse, (128, 128)).T
        kv_ref[here, :HD] = (raw_ref[here, :HD].astype(f32) * inverse).astype(bf16)
        kv_ref[here, HD:] = raw_ref[here, HD:]
    for x in range(4):
        span = slice(x * 256, (x + 1) * 256)
        queries = q_ref[span, :]
        end = end_ref[:, span]
        factor = factor_ref[:, span]

        def tile(index, state, count, masked=False):
            peak, mass, total = state
            part = window(kv_ref, index, count)
            keys, values = part[:, :HD], part[:, HD:]
            scores = dot(keys, queries, ((1,), (1,)))
            if masked:
                scores = jnp.where(window_mask(index, end, count), scores, masked_score)
            new_peak = jnp.maximum(peak, jnp.max(scores, axis=0, keepdims=True))
            weights = jnp.exp2((scores - new_peak) * factor)
            shrink = jnp.exp2((peak - new_peak) * factor)
            mass = mass * shrink + jnp.sum(weights, axis=0, keepdims=True)
            total = total * shrink + dot(values, weights.astype(bf16), ((0,), (0,)))
            return (new_peak, mass, total)

        state = (
            jnp.full((1, 256), masked_score, f32),
            jnp.zeros((1, 256), f32),
            jnp.zeros((HD, 256), f32),
        )
        last = 4 * x + z
        state = lax.fori_loop(0, last // 4, lambda i, s: tile(4 * i, s, 4), state)
        state = lax.fori_loop(last // 4 * 2, last // 2, lambda i, s: tile(2 * i, s, 2), state)
        state = lax.fori_loop(last // 2 * 2, last, lambda i, s: tile(i, s, 1), state)
        state = tile(last, state, 2, True)
        peak, mass, total = state
        out_ref[span, :] = (total / mass).T
        lse_ref[:, span] = peak * factor + jnp.log(mass) * log2e


def attend_back_kernel(
    z_ref,
    raw_ref,
    factor_ref,
    q_ref,
    grad_ref,
    kv_ref,
    end_ref,
    lse_ref,
    delta_ref,
    dq_ref,
    dkv_ref,
    sums,
):
    z = z_ref[0]
    sums[...] = jnp.zeros_like(sums)
    for x in range(4):
        span = slice(x * 256, (x + 1) * 256)
        raw = raw_ref[span, :]
        factor = factor_ref[:, span]
        queries = q_ref[span, :]
        grads = grad_ref[span, :]
        end = end_ref[:, span]
        lse = lse_ref[:, span]
        delta = delta_ref[:, span]

        def tile(index, total, count, masked=False):
            part = window(kv_ref, index, count)
            keys, values = part[:, :HD], part[:, HD:]
            scores = dot(keys, raw, ((1,), (1,))) * factor - lse
            if masked:
                scores = jnp.where(window_mask(index, end, count), scores, masked_score)
            chances = jnp.exp2(scores)
            value_dot = dot(values, grads, ((1,), (1,)))
            score_grad = (chances * (value_dot - delta)).astype(bf16)
            key_term = dot(score_grad, queries)
            value_term = dot(chances.astype(bf16), grads)
            for n in range(2 * count):
                here = pl.ds(window_rows(index + n // 2) + n % 2 * 1024, 256)
                sums[here, :HD] += key_term[n * 256 : n * 256 + 256]
                sums[here, HD:] += value_term[n * 256 : n * 256 + 256]
            return total + dot(keys, score_grad, ((0,), (0,)))

        total = jnp.zeros((HD, 256), f32)
        last = 4 * x + z
        total = lax.fori_loop(0, last // 4, lambda i, s: tile(4 * i, s, 4), total)
        total = lax.fori_loop(last // 4 * 2, last // 2, lambda i, s: tile(2 * i, s, 2), total)
        total = lax.fori_loop(last // 2 * 2, last, lambda i, s: tile(i, s, 1), total)
        total = tile(last, total, 2, True)
        dq_ref[span, :] = total.T * scale
    dkv_ref[:, :HD] = (sums[:, :HD] * scale).astype(bf16)
    dkv_ref[:, HD:] = sums[:, HD:].astype(bf16)


def rest_pick(quarter):
    row = lax.broadcasted_iota(jnp.int32, (HALF_REST, HALF_MAIN), 0)
    column = lax.broadcasted_iota(jnp.int32, (HALF_REST, HALF_MAIN), 1)
    same = (column >> 4 == row >> 2) & (column & 3 == row & 3)
    return jnp.where(same & ((column >> 2) & 3 == quarter), 1.0, 0.0).astype(bf16)


def open_rest(rows):
    rest = rows[:, D:]
    return jnp.concatenate(
        [dot(rest_pick(q), rest).astype(bf16) for q in range(QUARTERS)], axis=1
    )


def open_side(rows_ref):
    rest = rows_ref[:, SIDE:]
    rest = jnp.concatenate(
        [dot(rest_pick(q), rest).astype(bf16) for q in range(QUARTERS)], axis=1
    )
    return rows_ref[:, :SIDE], rest


def pull_kernel(side_ref, own_ref, other_ref, down_ref, flat_ref, pull_ref):
    own = pl.multiple_of(side_ref[0] * SIDE, SIDE)
    other = pl.multiple_of(SIDE - side_ref[0] * SIDE, SIDE)
    for ref, start in ((own_ref, own), (other_ref, other)):
        main, rest = open_side(ref)
        flat_ref[:HALF_MAIN, pl.ds(start, SIDE)] = main
        flat_ref[HALF_MAIN:, pl.ds(start, SIDE)] = rest
    pull_ref[...] = dot(flat_ref[...], down_ref[...], ((1,), (1,)))


def expert_kernel(
    place_ref,
    rows_ref,
    pull_ref,
    gate_ref,
    up_ref,
    router_ref,
    back_ref,
    flat_ref,
    hidden_ref,
    gate_grad_ref,
    up_grad_ref,
    logit_grad_ref,
):
    flat_ref[:HALF_MAIN] = rows_ref[:, :D]
    flat_ref[HALF_MAIN:] = open_rest(rows_ref)
    entry = flat_ref[...]
    lane = lax.broadcasted_iota(jnp.int32, (1, 128), 1)
    logits = jnp.where(lane < 64, dot(entry, router_ref[...]), masked_score)
    shifted = jnp.exp(logits - jnp.max(logits, axis=-1, keepdims=True))
    probability = shifted / jnp.sum(shifted, axis=-1, keepdims=True)
    own = jnp.where(lane == place_ref[0], 1.0, 0.0)
    gates = jnp.sum(probability * own, axis=-1, keepdims=True)
    gate = dot(entry, gate_ref[...])
    upward = dot(entry, up_ref[...])
    pull = pull_ref[...]
    sigma = 1.0 / (1.0 + jnp.exp(-gate))
    swish = gate * sigma
    hidden = swish * upward
    row_grad = jnp.sum(hidden * pull, axis=-1, keepdims=True) * gates
    hidden_ref[...] = (hidden * gates).astype(bf16)
    hidden_grad = pull * gates
    gate_grad = (hidden_grad * upward * (sigma + swish * (1.0 - sigma))).astype(bf16)
    up_grad = (hidden_grad * swish).astype(bf16)
    logit_grad = (row_grad * (own - probability)).astype(bf16)
    gate_grad_ref[...] = gate_grad
    up_grad_ref[...] = up_grad
    logit_grad_ref[...] = logit_grad
    rest = []
    for q in range(QUARTERS):
        band = slice(q * BAND, (q + 1) * BAND)
        part = (
            dot(gate_grad, gate_ref[band, :], ((1,), (1,)))
            + dot(up_grad, up_ref[band, :], ((1,), (1,)))
            + dot(logit_grad, router_ref[band, :], ((1,), (1,)))
        ).astype(bf16)
        back_ref[:, band] = part[:HALF_MAIN]
        rest.append(dot(rest_pick(q), part[HALF_MAIN:], ((0,), (0,))))
    back_ref[:, D:] = (rest[0] + rest[1] + rest[2] + rest[3]).astype(bf16)


def result_kernel(hidden_ref, down_ref, back_ref):
    rest = []
    for q in range(QUARTERS):
        band = slice(q * BAND, (q + 1) * BAND)
        part = dot(hidden_ref[...], down_ref[:, band]).astype(bf16)
        back_ref[:, band] = part[:HALF_MAIN]
        rest.append(dot(rest_pick(q), part[HALF_MAIN:], ((0,), (0,))))
    back_ref[:, D:] = (rest[0] + rest[1] + rest[2] + rest[3]).astype(bf16)


SMEM = pl.BlockSpec(memory_space=pltpu.SMEM)
VMEM = pl.BlockSpec(memory_space=pltpu.VMEM)
params = pltpu.CompilerParams(vmem_limit_bytes=56 * 1024 * 1024)
step_params = pltpu.CompilerParams(
    vmem_limit_bytes=56 * 1024 * 1024, dimension_semantics=("arbitrary",)
)


cheap = pl.CostEstimate(flops=1, bytes_accessed=1, transcendentals=0)
dear = pl.CostEstimate(flops=200_000_000_000, bytes_accessed=1, transcendentals=0)


def step_block(rows, columns):
    return pl.BlockSpec((rows, columns), lambda i: (i, 0))


def whole_block(rows, columns):
    return pl.BlockSpec((rows, columns), lambda i: (0, 0))


def shape(rows, columns, kind=bf16):
    return jax.ShapeDtypeStruct((rows, columns), kind)


def pack(*values):
    return pl.pallas_call(
        pack_kernel,
        out_shape=shape(256, 4 * HD),
        in_specs=[VMEM] * 5,
        out_specs=VMEM,
        compiler_params=params,
        cost_estimate=cheap,
    )(*values)


def project(places, inputs, weights, cosine, sine):
    return pl.pallas_call(
        project_kernel,
        out_shape=(
            shape(1024, D),
            shape(1024, 2 * HD, f32),
            shape(1024, HD),
            shape(1024, 2 * HD),
            shape(16, 128, f32),
            shape(D, 3 * HD),
            shape(D, 128),
            shape(8, D, f32),
        ),
        in_specs=[SMEM] + [VMEM] * (len(inputs) + len(weights) + 2),
        out_specs=(VMEM,) * 8,
        compiler_params=params,
        cost_estimate=pl.CostEstimate(
            flops=50_000_000_000, bytes_accessed=1, transcendentals=0
        ),
    )(places, *inputs, *weights, cosine, sine)


def spread_grads(*values):
    return pl.pallas_call(
        spread_kernel,
        out_shape=(shape(1024, D), shape(2560, 512)),
        in_specs=[SMEM] + [VMEM] * 8,
        out_specs=(VMEM, VMEM),
        compiler_params=params,
        cost_estimate=cheap,
    )(*values)


def finish(*values):
    return pl.pallas_call(
        finish_kernel,
        out_shape=(
            shape(32, 8 * HD, f32),
            shape(32, 8 * HD, f32),
            shape(32, 8 * HD, f32),
            shape(8 * HD, 32, f32),
            shape(32, 128, f32),
        ),
        in_specs=[SMEM] + [VMEM] * 3,
        out_specs=(VMEM,) * 5,
        compiler_params=params,
        cost_estimate=dear,
    )(*values)


def expert_pull(side, own, other, down):
    return pl.pallas_call(
        pull_kernel,
        grid=(2,),
        out_shape=(shape(1280, D), shape(1280, 512, f32)),
        in_specs=[
            SMEM,
            step_block(HALF_MAIN, SIDE_WIDTH),
            step_block(HALF_MAIN, SIDE_WIDTH),
            whole_block(512, D),
        ],
        out_specs=(step_block(HALF, D), step_block(HALF, 512)),
        compiler_params=step_params,
        cost_estimate=cheap,
    )(side, own, other, down)


def expert_step(place, rows, pull, gate, up, router):
    return pl.pallas_call(
        expert_kernel,
        grid=(2,),
        out_shape=(
            shape(1024, ROW_WIDTH),
            shape(1280, D),
            shape(1280, 512),
            shape(1280, 512),
            shape(1280, 512),
            shape(1280, 128),
        ),
        in_specs=[
            SMEM,
            step_block(HALF_MAIN, ROW_WIDTH),
            step_block(HALF, 512),
            whole_block(D, 512),
            whole_block(D, 512),
            whole_block(D, 128),
        ],
        out_specs=(
            step_block(HALF_MAIN, ROW_WIDTH),
            step_block(HALF, D),
            step_block(HALF, 512),
            step_block(HALF, 512),
            step_block(HALF, 512),
            step_block(HALF, 128),
        ),
        compiler_params=step_params,
        cost_estimate=cheap,
    )(place, rows, pull, gate, up, router)


def expert_result(hidden, down):
    return pl.pallas_call(
        result_kernel,
        grid=(2,),
        out_shape=shape(1024, ROW_WIDTH),
        in_specs=[step_block(HALF, 512), whole_block(512, D)],
        out_specs=step_block(HALF_MAIN, ROW_WIDTH),
        compiler_params=step_params,
        cost_estimate=cheap,
    )(hidden, down)


def linger_kernel(value_ref, out_ref):
    out_ref[...] = value_ref[...]


def linger(value):
    return pl.pallas_call(
        linger_kernel,
        out_shape=jax.ShapeDtypeStruct(value.shape, value.dtype),
        in_specs=[VMEM],
        out_specs=VMEM,
        cost_estimate=dear,
    )(value)


def attend(z, queries, factor, kv, inverses, end):
    return pl.pallas_call(
        attend_kernel,
        out_shape=(shape(1024, HD, f32), shape(1, 1024, f32), shape(8192, 2 * HD)),
        in_specs=[SMEM] + [VMEM] * 5,
        out_specs=(VMEM,) * 3,
        compiler_params=params,
        cost_estimate=cheap,
    )(z, queries, factor, kv, inverses, end)


def attend_back(z, raw, factor, queries, grads, kv, end, lse, delta):
    return pl.pallas_call(
        attend_back_kernel,
        out_shape=(
            shape(1024, HD, f32),
            shape(8192, 2 * HD),
        ),
        in_specs=[SMEM] + [VMEM] * 8,
        out_specs=(VMEM,) * 2,
        scratch_shapes=[pltpu.VMEM((8192, 2 * HD), f32)],
        compiler_params=params,
        cost_estimate=cheap,
    )(z, raw, factor, queries, grads, kv, end, lse, delta)


def dispatch(main_table, rest_table, value):
    band = value.shape[1] // QUARTERS
    stacked = value.reshape(128, QUARTERS, band).transpose(1, 0, 2).reshape(QUARTERS * 128, band)
    main = dot(main_table, value).astype(bf16)
    rest = dot(rest_table, stacked).astype(bf16)
    return jnp.concatenate([main, rest], axis=1)


def collect(main_table, rest_table, rows):
    width = rows.shape[1] * QUARTERS // (QUARTERS + 1)
    main = dot(main_table, rows[:, :width], ((0,), (0,)))
    rest = dot(rest_table, rows[:, width:], ((0,), (0,)))
    rest = rest.reshape(QUARTERS, 128, width // QUARTERS).transpose(1, 0, 2)
    return main + rest.reshape(128, width)


def local(
    inputs,
    blocks,
    expert_ids,
    attention_gain,
    query_weight,
    key_weight,
    value_weight,
    query_gain,
    key_gain,
    output_weight,
    mixture_gain,
    router_weight,
    gate_weight,
    up_weight,
    down_weight,
    cotangent,
):
    x = lax.axis_index("x")
    z = lax.axis_index("z")
    yh = lax.axis_index("yh")
    c = lax.axis_index("c")
    place = x * 16 + z * 4 + yh * 2 + c
    head = x * 2 + yh
    z_place = z.reshape(1).astype(jnp.int32)
    side = lax.axis_index("ep")
    side_place = side.reshape(1).astype(jnp.int32)
    heads_below = below(x, yh)

    line = [attention_gain, mixture_gain, jnp.pad(query_gain, (0, 16)), jnp.pad(key_gain, (0, 16))]
    line = jnp.concatenate([v.astype(f32) for v in line + [blocks]])[None]
    weights_sent = pack(line, router_weight, query_weight, key_weight, value_weight)
    inputs_pair = swap(inputs, "yh")
    inputs_all = [ring(inputs, "x"), ring(inputs_pair, "x")]
    near = [inputs_all[0][1], inputs_all[0][3], inputs_all[0][2]]
    near += [inputs_all[1][1], inputs_all[1][3]]
    inputs_all = [part for i, j in OFFSETS for part in inputs_all[j][i]]
    weights_come = exchange(weights_sent, HEADS)
    weights_all = ring(jnp.stack([weights_come, swap(weights_come, "c")]), "z")
    near += [weights_all[1], weights_all[3]]
    weights_all = [part for parts in weights_all for part in parts]
    output_all = lax.all_gather(output_weight.T, CTX, axis=0, tiled=True)

    experts = jnp.arange(64, dtype=jnp.int32)
    chosen = jnp.any(expert_ids[:, :, None] == experts[None, None, :], axis=1)
    tokens = jnp.arange(128, dtype=jnp.int32)
    earlier = (tokens[None, :] < tokens[:, None]).astype(bf16)
    ranks = dot(earlier, chosen.astype(bf16)).astype(jnp.int32)
    ranks = jnp.where(chosen, ranks, -1).T
    quarter = jnp.eye(QUARTERS, dtype=bf16)

    table = (ranks[:, None, :] == jnp.arange(CAP, dtype=jnp.int32)[None, :, None]).astype(bf16)
    main_table = table[:, :MAIN].reshape(64 * MAIN, 128)
    rest_table = table[:, None, MAIN:, None, :] * quarter[None, :, None, :, None]
    rest_table = rest_table.reshape(64 * MAIN, QUARTERS * 128)

    cotangent_side = lax.dynamic_slice(cotangent, (0, side * SIDE), (128, SIDE))
    grad_sent = dispatch(main_table, rest_table, cotangent_side)
    near, grad_sent = lax.optimization_barrier((near, grad_sent))
    grad_rows = exchange(grad_sent, CTX)
    chunk = jnp.arange(8, dtype=jnp.int32)
    chunk_start = ((chunk // 2) * 16 + z * 4 + (chunk % 2) * 2 + c) * 128
    positions = (chunk_start[:, None] + tokens[None, :]).reshape(1024)
    cosine, sine = rotary_tables(positions)
    places = jnp.concatenate(
        [heads_below, below(z, c) // 2 * 4 + below(z, c) % 2, head.reshape(1)]
    )
    normed_low, raw, query_some, kv_some, squares, weights_all, small_all, gain_rows = project(
        places.astype(jnp.int32),
        inputs_all,
        weights_all,
        jnp.concatenate([cosine, cosine], axis=1),
        jnp.concatenate([-sine, sine], axis=1),
    )
    blocks_all = small_all[:, 68:72].astype(jnp.int32).reshape(8192)
    attention_gain_all = gain_rows[0]
    mixture_gain_all = gain_rows[1]
    head_gains = small_all.reshape(64, 32, 128)[:, :16, 66:68].reshape(1024, 2).astype(f32)
    head_gains = lax.dynamic_slice(head_gains, (head * HD, 0), (HD, 2))
    query_gain_all = head_gains[:, 0]
    key_gain_all = head_gains[:, 1]
    query_raw, key_raw = raw[:, :HD], raw[:, HD:]

    kv_some, output_all = lax.optimization_barrier((kv_some, output_all))
    kv_some = lax.all_gather(kv_some, TOKENS, axis=0, tiled=True)
    own_blocks = blocks_all.reshape(4, 4, 2, 2, 128)[:, z, :, c].reshape(1024)
    end = jnp.sum((blocks_all[:, None] <= own_blocks[None, :]).astype(jnp.int32), axis=0)[None]
    squares = linger(squares)
    grad_rows, squares, end = lax.optimization_barrier((grad_rows, squares, end))
    squares = sum_over_rows(squares)
    grad_rows, squares = lax.optimization_barrier((grad_rows, squares))
    grad_other = swap(grad_rows, "ep")
    group_inverse = lax.rsqrt(squares / float(D) + epsilon)
    inverses = group_inverse[8:]
    inverses = jnp.stack([inverses, swap(inverses, "c")])
    inverses = jnp.concatenate([inverses] + [ahead(inverses, "z", i) for i in (1, 2, 3)])
    inverses = jnp.take(inverses, below(z, c), axis=0).reshape(8, 1024)
    group_inverse = group_inverse.reshape(2, 1024)
    query_inverse = group_inverse[0][:, None]
    key_inverse = group_inverse[1][:, None]
    query_factor = group_inverse[0:1] * (scale * log2e)
    query_low = (query_some.astype(f32) * query_inverse).astype(bf16)
    kv_some, end, query_low = lax.optimization_barrier((kv_some, end, query_low))
    attended, lse, kv = attend(
        z_place, query_some, query_factor, kv_some, inverses, end
    )
    attended_low = attended.astype(bf16)

    heads_all = [part for parts in ring(attended_low, "x") for part in parts]
    attended_rows, heads_all, grad_other = lax.optimization_barrier(
        (exchange(attended_low, HEADS).reshape(8, 128, HD), heads_all, grad_other)
    )
    heads_all = jnp.concatenate(heads_all, axis=0).reshape(4, 1024, HD)
    heads_all = jnp.take(heads_all, (x - jnp.arange(4)) % 4, axis=0)
    heads_all = heads_all.transpose(1, 0, 2).reshape(1024, 4 * HD)
    attended_rows = attended_rows.transpose(1, 0, 2).reshape(128, 8 * HD)
    source = inputs.astype(f32)
    residual = source + pair_sum(dot(attended_rows, output_all, ((1,), (1,))))
    mixture_inverse = lax.rsqrt(jnp.mean(residual * residual, axis=-1, keepdims=True) + epsilon)
    mixed_low = (residual * mixture_inverse * mixture_gain_all).astype(bf16)
    mixed_rows = exchange(dispatch(main_table, rest_table, mixed_low), CTX)

    grad_flat, hidden_pull = expert_pull(
        side_place, grad_rows, grad_other, down_weight[0]
    )
    mixed_rows, heads_all = lax.optimization_barrier((mixed_rows, heads_all))
    entry_sent, entry, hidden_low, gate_raw_grad, up_raw_grad, logit_grad = expert_step(
        place.reshape(1).astype(jnp.int32),
        mixed_rows,
        hidden_pull,
        gate_weight[0],
        up_weight[0],
        small_all,
    )
    entry_back = exchange(entry_sent, CTX)
    result_sent = expert_result(hidden_low, down_weight[0])
    down_weight_grad = dot(hidden_low, grad_flat, ((0,), (0,)))
    gate_weight_grad = dot(entry, gate_raw_grad, ((0,), (0,)))
    up_weight_grad = dot(entry, up_raw_grad, ((0,), (0,)))
    router_part = dot(entry, logit_grad, ((0,), (0,)))
    entry_back, down_weight_grad, gate_weight_grad, up_weight_grad, router_part = (
        lax.optimization_barrier(
            (entry_back, down_weight_grad, gate_weight_grad, up_weight_grad, router_part)
        )
    )

    mixed_grad = pair_sum(collect(main_table, rest_table, entry_back))

    grad_out = cotangent.astype(f32)
    scaled = mixed_grad * mixture_gain_all
    residual_grad = (
        grad_out
        + mixture_inverse * scaled
        - residual
        * mixture_inverse
        * mixture_inverse
        * mixture_inverse
        * jnp.mean(scaled * residual, axis=-1, keepdims=True)
    )
    mixture_gain_part = jnp.sum(mixed_grad * residual * mixture_inverse, axis=0)
    residual_low = residual_grad.astype(bf16)
    attended_grad = dot(residual_low, output_all).astype(bf16)
    attended_grad = attended_grad.reshape(128, 8, HD).transpose(1, 0, 2)
    attended_grad = exchange(attended_grad.reshape(1024, HD), HEADS)
    result_sent, attended_grad = lax.optimization_barrier((result_sent, attended_grad))
    result_back = exchange(result_sent, CTX)
    delta = jnp.sum(attended_grad.astype(f32) * attended, axis=-1)[None]
    query_grad, kv_part = attend_back(
        z_place, query_some, query_factor, query_low, attended_grad, kv, end, lse, delta
    )
    kv_grad = lax.psum_scatter(kv_part, TOKENS, scatter_dimension=0, tiled=True)
    query_grad, result_back = lax.optimization_barrier((query_grad, result_back))
    query_grad = linger(query_grad)
    residual_sent, result_back = lax.optimization_barrier((residual_low, result_back))
    bands = residual_sent.reshape(128, 4, 1, BAND).transpose(1, 2, 0, 3)
    bands = jnp.broadcast_to(bands, (4, 2, 128, BAND)).reshape(1024, BAND)
    residual_band = exchange(bands, HEADS)
    kv_grad = kv_grad.astype(f32)
    final = residual + pair_sum(collect(main_table, rest_table, result_back))
    value_grad_low = kv_grad[:, HD:].astype(bf16)
    query_normed_grad = rotate(query_grad, cosine, -sine)
    key_normed_grad = rotate(kv_grad[:, :HD], cosine, -sine)
    query_scaled = query_normed_grad * query_gain_all
    key_scaled = key_normed_grad * key_gain_all
    dots = jnp.stack(
        [jnp.sum(query_scaled * query_raw, axis=-1), jnp.sum(key_scaled * key_raw, axis=-1)]
    )
    residual_band, dots = lax.optimization_barrier((residual_band, dots))
    output_part = dot(residual_band, heads_all, ((0,), (0,)))
    dots = sum_over_rows(dots.reshape(16, 128)).reshape(2, 1024)[:, :, None] / float(D)

    def raw_back(value, inverse, scaled_grad, mean):
        return (inverse * scaled_grad - value * inverse * inverse * inverse * mean).astype(bf16)

    query_raw_low = raw_back(query_raw, query_inverse, query_scaled, dots[0])
    key_raw_low = raw_back(key_raw, key_inverse, key_scaled, dots[1])
    query_gain_part = jnp.sum(query_normed_grad * query_raw * query_inverse, axis=0)
    key_gain_part = jnp.sum(key_normed_grad * key_raw * key_inverse, axis=0)
    raw_grads = jnp.concatenate([query_raw_low, key_raw_low, value_grad_low], axis=1)

    head_gains = jnp.concatenate(
        [
            jnp.zeros((2, HD), f32),
            query_gain_part[None],
            key_gain_part[None],
            jnp.zeros((4, HD), f32),
        ],
        axis=0,
    )
    normed_part, shares = spread_grads(
        head.reshape(1).astype(jnp.int32),
        raw_grads,
        normed_low,
        weights_all,
        router_part,
        gain_rows,
        mixture_gain_part[None],
        head_gains,
        output_part,
    )

    summed = lax.psum_scatter(shares, TOKENS, scatter_dimension=0, tiled=True)
    output_own = lax.dynamic_slice(summed, (256 + yh * 32, 0), (32, 512))
    output_other = swap(lax.dynamic_slice(summed, (288 - yh * 32, 0), (32, 512)), "yh")
    shares, output_other, normed_sums = lax.optimization_barrier(
        (exchange(summed[:256], HEADS), output_other, gather_sum(normed_part, x, yh))
    )
    normed_sums = [part.astype(f32) for part in normed_sums]
    normed_grad = (normed_sums[0] + normed_sums[1]) + (normed_sums[2] + normed_sums[3])
    query_part, key_part, value_part, output_grad, extra = finish(
        yh.reshape(1).astype(jnp.int32), shares, output_own, output_other
    )
    pair = extra + swap(extra, "ep")
    router_grad = pair[:, :64]
    attention_gain_grad = pair[:, 64]

    inverse = lax.rsqrt(jnp.mean(source * source, axis=-1, keepdims=True) + epsilon)
    scaled = normed_grad * attention_gain_all
    input_grad = (
        residual_grad
        + inverse * scaled
        - source
        * inverse
        * inverse
        * inverse
        * jnp.mean(scaled * source, axis=-1, keepdims=True)
    )
    return (
        final,
        input_grad,
        attention_gain_grad,
        query_part,
        key_part,
        value_part,
        extra[:16, 66],
        extra[:16, 67],
        output_grad,
        extra[:, 65],
        router_grad,
        gate_weight_grad[None],
        up_weight_grad[None],
        down_weight_grad[None],
    )


def solution(mesh):
    inner = Mesh(mesh.devices.reshape(4, 4, 2, 2, 2), ("x", "z", "yh", "c", "ep"))
    in_specs = (
        P(CTX, None),
        P(CTX),
        P(CTX, None),
        P(CTX),
        P(CTX, "ep"),
        P(CTX, "ep"),
        P(CTX, "ep"),
        P(("ep",) + CTX),
        P(("ep",) + CTX),
        P("ep", CTX),
        P(CTX),
        P(CTX, None),
        P(CTX, None, "ep"),
        P(CTX, None, "ep"),
        P(CTX, "ep", None),
        P(CTX, None),
    )
    out_specs = (
        P(CTX, None),
        P(CTX, None),
        P(CTX),
        P(CTX, "ep"),
        P(CTX, "ep"),
        P(CTX, "ep"),
        P(("ep",) + CTX),
        P(("ep",) + CTX),
        P("ep", CTX),
        P(CTX),
        P(CTX, None),
        P(CTX, None, "ep"),
        P(CTX, None, "ep"),
        P(CTX, "ep", None),
    )
    return jax.shard_map(local, mesh=inner, in_specs=in_specs, out_specs=out_specs, check_vma=False)
```
